32 devices in a mesh: seq: 32 (over z, y, x, core).
Axes of the slice: x: 2, y: 2, z: 4, core: 2. Of those that a mesh axis runs over, the one named last changes fastest.
Arguments:
- tokens: bfloat16 [4, 2048, 1024], P(None, 'seq'), may hold values from -6 to 6
- gain_attn: float32 [1024], replicated, may hold values from 0.25 to 1.75
- gain_mlp: float32 [1024], replicated, may hold values from 0.25 to 1.75
- w_query: bfloat16 [1024, 1024], replicated, may hold values from -0.1875 to 0.1875
- w_key: bfloat16 [1024, 1024], replicated, may hold values from -0.1875 to 0.1875
- w_value: bfloat16 [1024, 1024], replicated, may hold values from -0.1875 to 0.1875
- w_out: bfloat16 [1024, 1024], replicated, may hold values from -1 to 1
- w_gate: bfloat16 [1024, 2752], replicated, may hold values from -0.1875 to 0.1875
- w_up: bfloat16 [1024, 2752], replicated, may hold values from -0.1875 to 0.1875
- w_down: bfloat16 [2752, 1024], replicated, may hold values from -0.109375 to 0.109375
- cotangent: bfloat16 [4, 2048, 1024], P(None, 'seq'), may hold values from -6 to 6
- lengths: int32 [4, 8], replicated, may hold values from 192 to 320, as said below
Outputs:
- output: bfloat16 [4, 2048, 1024], P(None, 'seq')
- input_grad: float32 [4, 2048, 1024], P(None, 'seq')
- grad_gain_attn: float32 [1024], replicated
- grad_gain_mlp: float32 [1024], replicated
- grad_w_query: float32 [1048576], P('seq')
- grad_w_key: float32 [1048576], P('seq')
- grad_w_value: float32 [1048576], P('seq')
- grad_w_out: float32 [1048576], P('seq')
- grad_w_gate: float32 [2818048], P('seq')
- grad_w_up: float32 [2818048], P('seq')
- grad_w_down: float32 [2818048], P('seq')
The draws below stay inside these ranges and needn't reach their ends.
Inputs may be any that keep to these rules, and one draw needn't show every extreme that they name: `lengths`: each row sums to 2048; every row holds a length of 192 and one of 320.
All inputs are finite; a program needn't handle non-finite values.
Results may differ from the reference program's by a relative error of at most 0.013.
Values may be sent and summed in bfloat16 or wider, within the bound.
A program may use at most 320 MiB of HBM per device.

```python
import math
import jax
import jax.numpy as jnp
from jax import lax

D = 1024
HEADS = 16
HEAD = 64
FF = 2752
WIN = 64
MB = 4
TOKENS = 2048
SEQ_COUNT = 8


def draw_lengths(key, part):
    key = jax.random.fold_in(key, 7)
    half_count = SEQ_COUNT // 2
    spread_key, order_key = jax.random.split(key)
    deviation = jax.random.randint(spread_key, (MB, half_count), 0, WIN + 1)
    column = jnp.arange(half_count, dtype=jnp.int32)[None, :]
    deviation = jnp.where(column == 0, WIN, deviation)
    paired = jnp.concatenate([4 * WIN + deviation, 4 * WIN - deviation], axis=1)
    order_keys = jax.random.split(order_key, MB)
    orders = jax.vmap(lambda one_key: jax.random.permutation(one_key, SEQ_COUNT))(order_keys)
    return jnp.take_along_axis(paired, orders, axis=1).astype(jnp.int32)


def block_scale(key, dims, cuts, least, top_value):
    level, own = 1.0, jax.random.fold_in(key, 6)
    for axis_at, shards_of in cuts:
        steps = jnp.exp(jax.random.uniform(jax.random.fold_in(own, axis_at), (shards_of,), jnp.float32, least / len(cuts), top_value / len(cuts)))
        level = level * jnp.repeat(steps, dims[axis_at] // shards_of).reshape([-1 if axis == axis_at else 1 for axis in range(len(dims))])
    return level


def bell_draw(own_key, shape, width, reach, cuts=(), held_as=jnp.bfloat16):
    level = block_scale(own_key, shape, cuts, -0.22, 0.18) if cuts else 1.0
    drawn = jax.random.normal(own_key, shape, jnp.float32) * width * level
    return jnp.minimum(jnp.maximum(drawn, -reach), reach).astype(held_as)


def setup_inputs(seed: int = 0) -> dict:
    keys = jax.random.split(jax.random.key(seed), 13)
    tokens = bell_draw(keys[0], (MB, TOKENS, D), 1.0, 6.0, ((1, 32),))
    gain_attn = jnp.clip(1.0 + 0.15 * jax.random.normal(keys[1], (D,), jnp.float32), 0.25, 1.75)
    gain_mlp = jnp.clip(1.0 + 0.15 * jax.random.normal(keys[2], (D,), jnp.float32), 0.25, 1.75)
    w_query = bell_draw(keys[3], (D, D), D ** -0.5, 0.1875)
    w_key = bell_draw(keys[4], (D, D), D ** -0.5, 0.1875)
    w_value = bell_draw(keys[5], (D, D), D ** -0.5, 0.1875)
    w_out = bell_draw(keys[6], (D, D), (D // 32) ** -0.5, 1.0)
    w_gate = bell_draw(keys[7], (D, FF), D ** -0.5, 0.1875)
    w_up = bell_draw(keys[8], (D, FF), D ** -0.5, 0.1875)
    w_down = bell_draw(keys[9], (FF, D), FF ** -0.5, 0.109375)
    cotangent = bell_draw(keys[10], (MB, TOKENS, D), 1.0, 6.0, ((1, 32),))
    lengths = draw_lengths(jax.random.fold_in(keys[12], 71), 0)
    return {"tokens": tokens, "gain_attn": gain_attn, "gain_mlp": gain_mlp, "w_query": w_query, "w_key": w_key, "w_value": w_value, "w_out": w_out, "w_gate": w_gate, "w_up": w_up, "w_down": w_down, "cotangent": cotangent, "lengths": lengths}


norm_epsilon = 1e-05
highest_precision = lax.Precision.HIGHEST

@jax.custom_vjp
def low(v):
    return lax.optimization_barrier(v.astype(jnp.bfloat16)).astype(jnp.float32)

@jax.custom_vjp
def low_back(v):
    return v

def low_keep(v):
    return (low(v), None)

def low_pass(kept, grad):
    return (grad,)

def back_keep(v):
    return (v, None)

def back_low(kept, grad):
    return (low(grad),)
low.defvjp(low_keep, low_pass)
low_back.defvjp(back_keep, back_low)

def matmul(left, right):
    return jnp.dot(left, right, precision=highest_precision)

def rms_norm(rows_in, gain):
    row_scale = lax.rsqrt(lax.optimization_barrier(jnp.mean(rows_in * rows_in, axis=-1, keepdims=True)) + norm_epsilon)
    return rows_in * row_scale * gain

def band_windows(padded, blocks):
    split_rows = padded.reshape((blocks + 1, WIN) + padded.shape[1:])
    return jnp.concatenate([split_rows[:-1], split_rows[1:]], axis=1)

def band_attention(pieces):
    queries, key_rows, value_rows, query_seg, key_seg, query_pos, key_pos = pieces
    blocks = queries.shape[0] // WIN
    query_blocks = queries.reshape(blocks, WIN, HEADS, HEAD)
    key_blocks = band_windows(key_rows, blocks).reshape(blocks, 2 * WIN, HEADS, HEAD)
    value_blocks = band_windows(value_rows, blocks).reshape(blocks, 2 * WIN, HEADS, HEAD)
    seg_query = query_seg.reshape(blocks, WIN)
    seg_keys = band_windows(key_seg, blocks)
    pos_query = query_pos.reshape(blocks, WIN)
    pos_keys = band_windows(key_pos, blocks)
    offset = pos_query[:, :, None] - pos_keys[:, None, :]
    allowed = (seg_query[:, :, None] == seg_keys[:, None, :]) & (offset >= 0) & (offset < WIN)
    raw_scores = jnp.einsum('bqhd,bkhd->bhqk', query_blocks, key_blocks, precision=highest_precision)
    raw_scores = low_back(raw_scores)
    logits = jnp.where(allowed[:, None], raw_scores * (1.0 / math.sqrt(HEAD)), -1e+30)
    row_peak = lax.optimization_barrier(jnp.max(logits, axis=-1, keepdims=True))
    exp_scores = jnp.exp(logits - row_peak)
    probability = low(exp_scores / lax.optimization_barrier(jnp.sum(exp_scores, axis=-1, keepdims=True)))
    attended = jnp.einsum('bhqk,bkhd->bqhd', probability, value_blocks, precision=highest_precision)
    return attended.reshape(blocks * WIN, HEADS * HEAD)

def grouped(array_in, pad_value, group_rows):
    groups = array_in.shape[0] // group_rows
    split_rows = array_in.reshape((groups, group_rows) + array_in.shape[1:])
    lead_rows = jnp.full((1, WIN) + array_in.shape[1:], pad_value, array_in.dtype)
    lead_rows = jnp.concatenate([lead_rows, split_rows[:-1, group_rows - WIN:]], axis=0)
    return jnp.concatenate([lead_rows, split_rows], axis=1)

def forward(inputs, gain_attn, gain_mlp, w_query, w_key, w_value, w_out, w_gate, w_up, w_down, segments, positions):
    row_count = inputs.shape[0]
    group_rows = math.gcd(row_count, 4096)
    groups = row_count // group_rows
    normed = low(rms_norm(inputs, gain_attn))
    queries = low(low_back(matmul(normed, w_query)))
    key_rows = low(low_back(matmul(normed, w_key)))
    value_rows = low(low_back(matmul(normed, w_value)))
    attend = jax.checkpoint(band_attention)
    mixed_rows = lax.map(attend, (queries.reshape(groups, group_rows, D), grouped(key_rows, 0.0, group_rows), grouped(value_rows, 0.0, group_rows), segments.reshape(groups, group_rows), grouped(segments, -1, group_rows), positions.reshape(groups, group_rows), grouped(positions, 0, group_rows)))
    attended = low(low_back(mixed_rows.reshape(row_count, D)))
    middle = inputs + low_back(matmul(attended, w_out))
    second = low(rms_norm(middle, gain_mlp))
    gate_proj = low_back(matmul(second, w_gate))
    up_proj = low_back(matmul(second, w_up))
    hidden = low(jax.nn.silu(gate_proj) * up_proj)
    return middle + low_back(matmul(hidden, w_down))

def reference(tokens, gain_attn, gain_mlp, w_query, w_key, w_value, w_out, w_gate, w_up, w_down, cotangent, lengths):
    row_count = MB * TOKENS
    flat_rows = tokens.astype(jnp.float32).reshape(row_count, D)
    seq_ends = jnp.cumsum(lengths.reshape(-1)).astype(jnp.int32)
    positions = jnp.arange(row_count, dtype=jnp.int32)
    segments = jnp.searchsorted(seq_ends, positions, side='right').astype(jnp.int32)

    def forward_flat(inputs, gain_one, gain_two, mat_query, mat_key, mat_value, mat_out, mat_gate, mat_up, mat_down):
        return forward(inputs, gain_one, gain_two, mat_query, mat_key, mat_value, mat_out, mat_gate, mat_up, mat_down, segments, positions)
    result, pullback = jax.vjp(forward_flat, flat_rows, gain_attn, gain_mlp, w_query.astype(jnp.float32), w_key.astype(jnp.float32), w_value.astype(jnp.float32), w_out.astype(jnp.float32), w_gate.astype(jnp.float32), w_up.astype(jnp.float32), w_down.astype(jnp.float32))
    gradients = pullback(cotangent.astype(jnp.float32).reshape(row_count, D))
    out_shape = (MB, TOKENS, D)
    return (result.astype(jnp.bfloat16).reshape(out_shape), gradients[0].reshape(out_shape), gradients[1], gradients[2], gradients[3].reshape(-1), gradients[4].reshape(-1), gradients[5].reshape(-1), gradients[6].reshape(-1), gradients[7].reshape(-1), gradients[8].reshape(-1), gradients[9].reshape(-1))
```

```python
import functools
import math

import jax
import jax.numpy as jnp
from jax import lax
from jax.experimental import pallas as pl
from jax.experimental.pallas import tpu as pltpu
from jax.sharding import PartitionSpec as P

HEAD = 64
WIN = 64
EPSILON = 1e-05
LOGICAL = pl.DeviceIdType.MESH
MOST_GROUPS = 32
BF16 = jnp.bfloat16
F32 = jnp.float32


def round_up(value, unit):
    return -(-value // unit) * unit


ROW_FACTORS = ("hidden", "second", "first", "attended")
MATRICES = (
    ("down", "hidden", "cot"),
    ("gate", "second", "dgate"),
    ("up", "second", "dup"),
    ("query", "first", "dquery"),
    ("keyval", "first", "dkeyval"),
    ("out", "attended", "branch"),
)


def bit_orders(bits):
    ascending = list(range(1, bits + 1))
    swapped = [2, 1] + ascending[2:]
    last_first = ascending[2:] + [1, 2]
    return {
        "down": last_first,
        "gate": ascending,
        "query": ascending,
        "out": ascending,
        "up": swapped,
        "keyval": swapped,
    }


def bit_of(number, bit):
    return (number // (1 << bit)) % 2


def flip(number, bit):
    return number + (1 << bit) * (1 - 2 * bit_of(number, bit))


def reduce_kernel(bits, lower, names, *refs):
    count = 1 << bits
    half = count // 2
    orders = bit_orders(bits)
    refs = list(refs)

    def take(how_many):
        taken = refs[:how_many]
        del refs[:how_many]
        return taken

    row_names = [name for name in ROW_FACTORS]
    col_names = [col for _, _, col in MATRICES]
    row_in = dict(zip(row_names, take(len(row_names))))
    col_in = dict(zip(col_names, take(len(col_names))))
    (gains_in,) = take(1)
    outs = dict(zip(names, take(len(names))))
    (gains_out,) = take(1)
    rows = dict(zip(row_names, take(len(row_names))))
    cols = dict(zip(col_names, take(len(col_names))))
    send_buf = dict(zip(names, take(len(names))))
    own_buf = dict(zip(names, take(len(names))))
    landed = {name: take(bits) for name in names}
    (gain_buf, local_sem, pair_send, pair_recv, step_send, step_recv, gain_send, gain_recv) = refs

    position = lax.axis_index("seq")
    me, rest = position // lower, position % lower
    core = me % 2
    my_unit = me // 2

    def partner(bit):
        return (flip(me, bit) * lower + rest,)

    def unit_at(order, slot):
        unit = my_unit
        for place, bit in enumerate(order):
            rel = (slot // (1 << (bits - 1 - place))) % 2
            own = bit_of(me, bit)
            unit = unit + (1 << (bit - 1)) * rel * (1 - 2 * own)
        return unit

    barrier = pltpu.get_barrier_semaphore()
    for bit in range(bits + 1):
        pl.semaphore_signal(barrier, inc=1, device_id=partner(bit), device_id_type=LOGICAL)
    pl.semaphore_wait(barrier, bits + 1)

    factor_copies = {}
    for index, (kind, name) in enumerate(
        [("row", "hidden"), ("col", "cot"), ("row", "second"), ("col", "dgate"), ("col", "dup"),
         ("row", "first"), ("col", "dquery"), ("col", "dkeyval"), ("row", "attended"), ("col", "branch")]
    ):
        if kind == "row":
            mine, theirs, kept = row_in[name].at[core], row_in[name].at[1 - core], rows[name]
        else:
            mine, theirs, kept = col_in[name], col_in[name], cols[name]
        local = pltpu.make_async_copy(mine, kept.at[0], local_sem.at[index])
        remote = pltpu.make_async_remote_copy(
            src_ref=theirs, dst_ref=kept.at[1], send_sem=pair_send.at[index], recv_sem=pair_recv.at[index],
            device_id=partner(0), device_id_type=LOGICAL,
        )
        local.start()
        remote.start()
        factor_copies[name] = (local, remote)
    ready = set()

    def need(name):
        if name not in ready:
            ready.add(name)
            local, remote = factor_copies[name]
            local.wait()
            remote.wait_recv()

    def product(index, into, base):
        name, row_name, col_name = MATRICES[index]
        need(row_name)
        need(col_name)
        order = orders[name]
        row_ref, col_ref = rows[row_name], cols[col_name]
        unit_rows = row_ref.shape[2]
        width = col_ref.shape[2]
        step = 256
        units = [unit_at(order, base + slot) for slot in range(half)]
        lefts = [
            jnp.concatenate([row_ref[source, unit] for unit in units], axis=0) for source in range(2)
        ]

        def body(at, carry):
            lanes = pl.ds(pl.multiple_of(at * step, step), step)
            total = jnp.dot(lefts[0], col_ref[0, :, lanes], preferred_element_type=F32)
            total += jnp.dot(lefts[1], col_ref[1, :, lanes], preferred_element_type=F32)
            into[:, :, lanes] = total.astype(BF16).reshape(half, unit_rows, step)
            return carry

        lax.fori_loop(0, width // step, body, 0)

    def step_copy(index, level, slot):
        name = MATRICES[index][0]
        bit = orders[name][level]
        size = half >> level
        source = send_buf[name].at[slot] if level == 0 else landed[name][level - 1].at[size + slot]
        place = count - 2 * size + slot
        return pltpu.make_async_remote_copy(
            src_ref=source, dst_ref=landed[name][level].at[slot],
            send_sem=step_send.at[index, place], recv_sem=step_recv.at[index, place],
            device_id=partner(bit), device_id_type=LOGICAL,
        )

    def start_level_zero(index):
        def body(at, carry):
            step_copy(index, 0, (at + half // 2) % half).start()
            return carry

        lax.fori_loop(0, half, body, 0)

    def arrive(index, level, first, last, forward):
        name = MATRICES[index][0]
        size = half >> level
        buffer = landed[name][level]
        before = own_buf[name] if level == 0 else landed[name][level - 1]

        def body(slot, carry):
            step_copy(index, level, slot).wait_recv()
            total = buffer[slot].astype(F32) + before[slot].astype(F32)
            if level == bits - 1:
                outs[name][...] = total
            else:
                buffer[slot] = total.astype(BF16)
            if forward:
                step_copy(index, level + 1, slot - size // 2).start()
            return carry

        lax.fori_loop(first, last, body, 0)

    for index in range(len(MATRICES)):
        product(index, send_buf[MATRICES[index][0]], half)
        start_level_zero(index)
    for index in range(len(MATRICES)):
        product(index, own_buf[MATRICES[index][0]], 0)

    gain_buf[0] = gains_in[...]

    def gain_copy(bit):
        return pltpu.make_async_remote_copy(
            src_ref=gain_buf.at[2 * bit], dst_ref=gain_buf.at[2 * bit + 1],
            send_sem=gain_send.at[bit], recv_sem=gain_recv.at[bit],
            device_id=partner(bit), device_id_type=LOGICAL,
        )

    def gain_step(bit):
        gain_copy(bit).wait_recv()
        total = gain_buf[2 * bit] + gain_buf[2 * bit + 1]
        if bit < bits:
            gain_buf[2 * bit + 2] = total
            gain_copy(bit + 1).start()
        else:
            gains_out[...] = total

    gain_copy(0).start()
    index_of = {name: index for index, (name, _, _) in enumerate(MATRICES)}
    turn = [index_of[name] for name in ("gate", "up", "down", "query", "keyval", "out")]
    for level in range(bits):
        size = half >> level
        gain_step(level)
        for index in turn:
            if size > 1:
                arrive(index, level, size // 2, size, True)
        for index in turn:
            arrive(index, level, 0, max(size // 2, 1), False)
    gain_step(bits)

    for local, remote in factor_copies.values():
        remote.wait_send()
    for bit in range(bits + 1):
        gain_copy(bit).wait_send()
    for index in range(len(MATRICES)):
        for level in range(bits):

            def drain(slot, carry, index=index, level=level):
                step_copy(index, level, slot).wait_send()
                return carry

            lax.fori_loop(0, half >> level, drain, 0)


def reduce_scatter(row_factors, col_factors, gains, bits, lower):
    count = 1 << bits
    half = count // 2
    names = tuple(name for name, _, _ in MATRICES)
    any_spec = pl.BlockSpec(memory_space=pl.ANY)
    vmem_spec = pl.BlockSpec(memory_space=pltpu.VMEM)
    row_args = [row_factors[name] for name in ROW_FACTORS]
    col_args = [col_factors[col] for _, _, col in MATRICES]
    shapes = {
        name: (row_factors[row].shape[2], col_factors[col].shape[1]) for name, row, col in MATRICES
    }
    scratch = [pltpu.VMEM((2,) + row.shape[1:], BF16) for row in row_args]
    scratch += [pltpu.VMEM((2,) + col.shape, BF16) for col in col_args]
    scratch += [pltpu.VMEM((half,) + shapes[name], BF16) for name in names]
    scratch += [pltpu.VMEM((half,) + shapes[name], BF16) for name in names]
    for name in names:
        scratch += [pltpu.VMEM((half >> level,) + shapes[name], BF16) for level in range(bits)]
    factors = len(row_args) + len(col_args)
    scratch += [
        pltpu.VMEM((2 * bits + 2,) + gains.shape, F32),
        pltpu.SemaphoreType.DMA((factors,)),
        pltpu.SemaphoreType.DMA((factors,)),
        pltpu.SemaphoreType.DMA((factors,)),
        pltpu.SemaphoreType.DMA((len(names), count)),
        pltpu.SemaphoreType.DMA((len(names), count)),
        pltpu.SemaphoreType.DMA((bits + 1,)),
        pltpu.SemaphoreType.DMA((bits + 1,)),
    ]
    results = pl.pallas_call(
        functools.partial(reduce_kernel, bits, lower, names),
        out_shape=[jax.ShapeDtypeStruct(shapes[name], F32) for name in names]
        + [jax.ShapeDtypeStruct(gains.shape, F32)],
        in_specs=[any_spec] * factors + [vmem_spec],
        out_specs=[vmem_spec] * (len(names) + 1),
        scratch_shapes=scratch,
        compiler_params=pltpu.CompilerParams(
            collective_id=0, has_side_effects=True, vmem_limit_bytes=62 * 2**20
        ),
        name="weight_grads",
    )(*row_args, *col_args, gains)
    return dict(zip(names, results[:-1])), results[-1]


def times_transpose(left, weight):
    return lax.dot_general(left, weight, (((1,), (1,)), ((), ())), preferred_element_type=F32)


def norm_backward(grad_normed, normed, row_scale):
    return row_scale * (
        grad_normed - normed * jnp.mean(grad_normed * normed, axis=-1, keepdims=True)
    )


def shifted(value, steps):
    count = lax.axis_size("seq")
    leading, last = max(0, -steps), min(count, count - steps)
    return lax.ppermute(value, "seq", [(source, source + steps) for source in range(leading, last)])


def band_mask(lengths, start):
    ends = jnp.cumsum(lengths, axis=1)
    positions = start + jnp.arange(-WIN, WIN, dtype=jnp.int32)
    segments = jnp.sum((ends[:, None, :] <= positions[None, :, None]).astype(jnp.int32), axis=2)
    offset = positions[WIN:, None] - positions[None, :]
    near = (offset >= 0) & (offset < WIN) & (positions[None, :] >= 0)
    return near[None] & (segments[:, WIN:, None] == segments[:, None, :])


def per_device(
    tokens, gain_attn, gain_mlp, w_query, w_key, w_value, w_out, w_gate, w_up, w_down, cotangent, lengths
):
    devices = lax.axis_size("seq")
    groups = min(devices, MOST_GROUPS)
    lower = devices // groups
    bits = groups.bit_length() - 2
    micro, block, width = tokens.shape
    heads = width // HEAD
    rows_all = micro * block
    score_scale = 1.0 / math.sqrt(HEAD)
    start = lax.axis_index("seq") * block
    allowed = band_mask(lengths, start)[:, None]

    inputs = tokens.reshape(rows_all, width).astype(F32)
    scale_attn = lax.rsqrt(jnp.mean(inputs * inputs, axis=-1, keepdims=True) + EPSILON)
    normed_attn = inputs * scale_attn
    first = (normed_attn * gain_attn).astype(BF16)
    queries = jnp.dot(first, w_query, preferred_element_type=F32).astype(BF16)
    keys = jnp.dot(first, w_key, preferred_element_type=F32).astype(BF16)
    values = jnp.dot(first, w_value, preferred_element_type=F32).astype(BF16)
    before_keys, before_values = shifted((keys, values), 1)

    def joined(before, own):
        both = jnp.stack([before.reshape(micro, block, width), own.reshape(micro, block, width)], axis=1)
        return both.reshape(micro, 2 * block, heads, HEAD)

    query_blocks = queries.reshape(micro, block, heads, HEAD)
    key_blocks = joined(before_keys, keys)
    value_blocks = joined(before_values, values)
    scores = jnp.einsum("bqhd,bkhd->bhqk", query_blocks, key_blocks, preferred_element_type=F32)
    logits = jnp.where(allowed, scores * score_scale, -1e30)
    exp_scores = jnp.exp(logits - jnp.max(logits, axis=-1, keepdims=True))
    probability = exp_scores / jnp.sum(exp_scores, axis=-1, keepdims=True)
    rounded = probability.astype(BF16)
    attended = jnp.einsum("bhqk,bkhd->bqhd", rounded, value_blocks, preferred_element_type=F32)
    attended = attended.reshape(rows_all, width).astype(BF16)
    middle = inputs + jnp.dot(attended, w_out, preferred_element_type=F32)
    scale_mlp = lax.rsqrt(jnp.mean(middle * middle, axis=-1, keepdims=True) + EPSILON)
    normed_mlp = middle * scale_mlp
    second = (normed_mlp * gain_mlp).astype(BF16)
    gate = jnp.dot(second, w_gate, preferred_element_type=F32)
    up = jnp.dot(second, w_up, preferred_element_type=F32)
    sigmoid = jax.nn.sigmoid(gate)
    silu = gate * sigmoid
    hidden = (silu * up).astype(BF16)
    output = (middle + jnp.dot(hidden, w_down, preferred_element_type=F32)).astype(BF16)

    cot = cotangent.reshape(rows_all, width)
    grad_hidden = times_transpose(cot, w_down)
    dgate = (grad_hidden * up * sigmoid * (1.0 + gate * (1.0 - sigmoid))).astype(BF16)
    dup = (grad_hidden * silu).astype(BF16)
    grad_second = times_transpose(dgate, w_gate) + times_transpose(dup, w_up)
    grad_gain_mlp = jnp.sum(grad_second * normed_mlp, axis=0)
    grad_middle = cot.astype(F32) + norm_backward(grad_second * gain_mlp, normed_mlp, scale_mlp)
    branch = grad_middle.astype(BF16)
    grad_attended = times_transpose(branch, w_out).astype(BF16).reshape(micro, block, heads, HEAD)
    grad_prob = jnp.einsum("bqhd,bkhd->bhqk", grad_attended, value_blocks, preferred_element_type=F32)
    delta = jnp.sum(probability * grad_prob, axis=-1, keepdims=True)
    grad_scores = (score_scale * probability * (grad_prob - delta)).astype(BF16)
    dquery = jnp.einsum("bhqk,bkhd->bqhd", grad_scores, key_blocks, preferred_element_type=F32)
    dquery = dquery.reshape(rows_all, width).astype(BF16)
    dkey_both = jnp.einsum("bhqk,bqhd->bkhd", grad_scores, query_blocks, preferred_element_type=F32)
    dvalue_both = jnp.einsum("bhqk,bqhd->bkhd", rounded, grad_attended, preferred_element_type=F32)

    def halves(both):
        both = both.reshape(micro, 2, block, width)
        return both[:, 0].reshape(rows_all, width).astype(BF16), both[:, 1].reshape(rows_all, width)

    key_back, key_own = halves(dkey_both)
    value_back, value_own = halves(dvalue_both)
    key_back, value_back = shifted((key_back, value_back), -1)
    dkey = (key_own + key_back.astype(F32)).astype(BF16)
    dvalue = (value_own + value_back.astype(F32)).astype(BF16)
    grad_first = (
        times_transpose(dquery, w_query) + times_transpose(dkey, w_key) + times_transpose(dvalue, w_value)
    )
    grad_gain_attn = jnp.sum(grad_first * normed_attn, axis=0)
    input_grad = grad_middle + norm_backward(grad_first * gain_attn, normed_attn, scale_attn)

    hidden_width = w_gate.shape[1]
    padded = round_up(hidden_width, 256)
    unit_rows = {"first": width // groups, "second": width // groups, "attended": width // groups}
    unit_rows["hidden"] = hidden_width // groups

    def by_owner(value, own_rows):
        parts = value.T.reshape(groups // 2, 2, own_rows, rows_all).transpose(1, 0, 2, 3)
        pad = round_up(own_rows, 16) - own_rows
        return jnp.pad(parts, ((0, 0), (0, 0), (0, pad), (0, 0)))

    def widened(value):
        return jnp.pad(value, ((0, 0), (0, padded - hidden_width)))

    row_factors = {
        "first": by_owner(first, unit_rows["first"]),
        "second": by_owner(second, unit_rows["second"]),
        "attended": by_owner(attended, unit_rows["attended"]),
        "hidden": by_owner(hidden, unit_rows["hidden"]),
    }
    col_factors = {
        "cot": cot,
        "dgate": widened(dgate),
        "dup": widened(dup),
        "dquery": dquery,
        "dkeyval": jnp.concatenate([dkey, dvalue], axis=1),
        "branch": branch,
    }
    gains = jnp.concatenate(
        [grad_gain_attn[None], grad_gain_mlp[None], jnp.zeros((6, width), F32)], axis=0
    )
    sums, gain_sums = reduce_scatter(row_factors, col_factors, gains, bits, lower)
    own = unit_rows["first"]

    def slice_of(value):
        flat = value.reshape(-1)
        if lower == 1:
            return flat
        near = [[high * lower + low for low in range(lower)] for high in range(groups)]
        return lax.psum_scatter(flat, "seq", axis_index_groups=near, tiled=True)

    if lower > 1:
        across = [[high * lower + low for low in range(lower)] for high in range(groups)]
        gain_sums = lax.psum(gain_sums, "seq", axis_index_groups=across)
    return (
        output.reshape(tokens.shape),
        input_grad.reshape(tokens.shape),
        gain_sums[0],
        gain_sums[1],
        slice_of(sums["query"][:own]),
        slice_of(sums["keyval"][:own, :width]),
        slice_of(sums["keyval"][:own, width:]),
        slice_of(sums["out"][:own]),
        slice_of(sums["gate"][:own, :hidden_width]),
        slice_of(sums["up"][:own, :hidden_width]),
        slice_of(sums["down"][: unit_rows["hidden"]]),
    )


def solution(mesh):
    tokens_spec = P(None, "seq", None)
    return jax.shard_map(
        per_device,
        mesh=mesh,
        in_specs=(tokens_spec,) + (P(),) * 9 + (tokens_spec, P()),
        out_specs=(tokens_spec, tokens_spec, P(), P()) + (P("seq"),) * 7,
        check_vma=False,
    )
```

```python
import functools
import math

import jax
import jax.numpy as jnp
from jax import lax
from jax.experimental import pallas as pl
from jax.experimental.pallas import tpu as pltpu
from jax.sharding import PartitionSpec as P

HEAD = 64
WIN = 64
EPSILON = 1e-05
MESH = pl.DeviceIdType.MESH
MOST_GROUPS = 32
CHUNK = 256
BF16 = jnp.bfloat16
F32 = jnp.float32

MATRICES = {
    "down": (("hidden", "cot"),),
    "gate": (("second", "dgate"),),
    "up": (("second", "dup"),),
    "query": (("first", "dquery"),),
    "keyval": (("first", "dkeyval"), ("before", "dkvback")),
    "out": (("attended", "branch"),),
}
ROWS = ("first", "before", "attended", "second", "hidden")
COLS = ("cot", "dgate", "dup", "branch", "dquery", "dkeyval", "dkvback")
NAMES = tuple(MATRICES)
INDEX = {name: index for index, name in enumerate(NAMES)}


def round_up(value, unit):
    return -(-value // unit) * unit


def bit_orders(bits):
    ascending = list(range(1, bits + 1))
    swapped = [2, 1] + ascending[2:]
    last_first = ascending[2:] + [1, 2]
    return {
        "down": last_first,
        "gate": ascending,
        "query": ascending,
        "out": ascending,
        "up": swapped,
        "keyval": swapped,
    }


def bit_of(number, bit):
    return (number // (1 << bit)) % 2


def flip(number, bit):
    return number + (1 << bit) * (1 - 2 * bit_of(number, bit))


def dot(left, right):
    return jnp.dot(left, right, preferred_element_type=F32)


def dot_rows(left, right):
    return lax.dot_general(left, right, (((1,), (1,)), ((), ())), preferred_element_type=F32)


def dot_cols(left, right):
    return lax.dot_general(left, right, (((0,), (0,)), ((), ())), preferred_element_type=F32)


def at_chunk(index, size=CHUNK):
    return pl.ds(index * size, size)


def loop(first, last, body, **options):
    def step(at, carry):
        body(at)
        return carry

    lax.fori_loop(first, last, step, 0, **options)


def layer_kernel(sizes, in_names, out_names, scratch_names, *refs):
    micro, block, width, hidden_width, devices, groups = sizes
    r = dict(zip(in_names + out_names + scratch_names, refs))
    lower = devices // groups
    bits = groups.bit_length() - 2
    count = 1 << bits
    half = count // 2
    orders = bit_orders(bits)
    rows_all = micro * block
    chunks = width // CHUNK
    full = hidden_width // CHUNK
    tail = hidden_width % CHUNK
    depth = r["ring_gate"].shape[0]
    kept = full - depth
    scale = 1.0 / math.sqrt(HEAD)

    position = lax.axis_index("seq")
    me, rest = position // lower, position % lower
    core = me % 2
    my_unit = me // 2
    after = ((position + 1) % devices,)
    behind = ((position + devices - 1) % devices,)

    def partner(bit):
        return (flip(me, bit) * lower + rest,)


    def local_copy(source, target, index):
        return pltpu.make_async_copy(source, target, r["local_sem"].at[index])

    def remote_copy(source, target, sems, index, device):
        send, recv = r[sems + "_send"], r[sems + "_recv"]
        return pltpu.make_async_remote_copy(
            src_ref=source, dst_ref=target, send_sem=send.at[index], recv_sem=recv.at[index],
            device_id=device, device_id_type=MESH,
        )

    load_tokens = local_copy(r["tokens"], r["x"], 0)
    load_cot = local_copy(r["cotangent"], r["col_cot"].at[0], 1)
    load_out = local_copy(r["w_out"], r["wo"], 2)
    rings = ("ring_gate", "ring_up", "ring_down")
    past = pl.ds(full * CHUNK, tail)
    load_tails = [
        local_copy(r[name].at[past, :], r["tail_" + name[2:]], 3 + index)
        for index, name in enumerate(("w_gate", "w_up", "w_down"))
    ]
    def attention_weights(base):
        return [
            pltpu.make_async_copy(
                r[name].at[at_chunk(slot), :], r[ring].at[slot], r["ring_sem"].at[index, base + slot]
            )
            for index, (name, ring) in enumerate(zip(("w_query", "w_key", "w_value"), rings))
            for slot in range(depth)
        ]

    attention_first = attention_weights(2 * full)
    attention_again = attention_weights(2 * full + depth)

    def hidden_weights(chunk, place):
        slot = place % depth
        return [
            pltpu.make_async_copy(r[name].at[at_chunk(chunk), :], r[ring].at[slot], r["ring_sem"].at[index, place])
            for index, (name, ring) in enumerate(zip(("w_gate", "w_up", "w_down"), rings))
        ]

    padded = r["col_dgate"].shape[2]

    def pair_copies():
        plan = {}
        for name in ROWS:
            plan[name] = (r["row_" + name].at[:, 1 - core], r["peer_" + name])
        plan["cot"] = (r["cotangent"], r["col_cot"].at[1])
        for name in ("dgate", "dup", "branch", "dquery", "dkeyval", "dkvback"):
            plan[name] = (r["col_" + name].at[0], r["col_" + name].at[1])
        return {
            name: remote_copy(source, target, "pair", index, partner(0))
            for index, (name, (source, target)) in enumerate(plan.items())
        }

    pair = pair_copies()
    ready = set()

    def need(name):
        if name not in ready:
            ready.add(name)
            pair[name].wait_recv()

    halo_out = remote_copy(r["tokens"], r["x_before"], "halo", 0, after)
    halo_back = remote_copy(r["back_out"], r["back_in"], "halo", 1, behind)

    load_tokens.start()
    for copy in attention_first:
        copy.start()
    load_out.start()
    load_cot.start()
    for copy in load_tails:
        copy.start()
    barrier = pltpu.get_barrier_semaphore()
    for device in [after, behind] + [partner(bit) for bit in range(bits + 1)]:
        pl.semaphore_signal(barrier, inc=1, device_id=device, device_id_type=MESH)
    pl.semaphore_wait(barrier, bits + 3)
    halo_out.start()
    pair["cot"].start()
    for name in ("dgate", "dup"):
        r["col_" + name][0, :, pl.ds(full * CHUNK, padded - full * CHUNK)] = jnp.zeros(
            (rows_all, padded - full * CHUNK), BF16
        )


    def unit_at(order, slot):
        unit = my_unit
        for place, bit in enumerate(order):
            rel = (slot // (1 << (bits - 1 - place))) % 2
            unit = unit + (1 << (bit - 1)) * rel * (1 - 2 * bit_of(me, bit))
        return unit

    def product(name, first, last, store):
        units = [unit_at(orders[name], slot) for slot in range(first, last)]
        pairs = []
        for row, col in MATRICES[name]:
            need(row)
            need(col)
            for source in range(2):
                parts = [
                    r["row_" + row][unit, core] if source == 0 else r["peer_" + row][unit] for unit in units
                ]
                pairs.append((jnp.concatenate(parts, axis=0), r["col_" + col], source))
        unit_rows = r["row_" + MATRICES[name][0][0]].shape[2]

        def body(at):
            lanes = at_chunk(at)
            total = None
            for left, ref, source in pairs:
                term = dot(left, ref[source, :, lanes])
                total = term if total is None else total + term
            store(lanes, total.reshape(last - first, unit_rows, CHUNK))

        loop(0, pairs[0][1].shape[2] // CHUNK, body)

    def step_copy(name, level, slot):
        size = half >> level
        source = r["send_" + name].at[slot] if level == 0 else r[f"land_{name}{level - 1}"].at[size + slot]
        return remote_copy(
            source, r[f"land_{name}{level}"].at[slot], "step", (INDEX[name], count - 2 * size + slot),
            partner(orders[name][level]),
        )

    def send_product(name):
        target = r["send_" + name]

        def store(lanes, value):
            target[:, :, lanes] = value.astype(BF16)

        product(name, half, count, store)
        loop(0, half, lambda at: step_copy(name, 0, (at + half // 2) % half).start())

    def finish(name, total):
        flat = r["flat_" + name]
        if name in ("gate", "up"):
            rows, wide = total.shape
            turn = r["turn"]
            for j in range(wide // 128):
                turn[pl.ds(rows * j, rows), :] = total[:, 128 * j : 128 * (j + 1)]
            few = rows // 2
            steps = hidden_width // 64
            whole = hidden_width // 128
            even = [turn[pl.ds(rows * j, few, stride=2), :] for j in range(whole + 1)]
            odd = [pltpu.roll(turn[pl.ds(rows * j + 1, few, stride=2), :], 64, 1) for j in range(whole + 1)]
            low = lax.broadcasted_iota(jnp.int32, (few, 128), 1) < 64
            for j in range(whole):
                flat[pl.ds(j, few, stride=steps), :] = even[j]
                flat[pl.ds(whole + 1 + j, few, stride=steps), :] = jnp.where(low, odd[j], odd[j + 1])
            flat[pl.ds(whole, few, stride=steps), :] = jnp.where(low, even[whole], odd[0])
            return
        parts = ((flat, 0),)
        if name == "keyval":
            parts = ((flat, 0), (r["flat_value"], width))
        per_row = width // 128
        for ref, base in parts:
            rows = ref.shape[0] // per_row
            for j in range(per_row):
                ref[pl.ds(j, rows, stride=per_row), :] = total[:rows, base + 128 * j : base + 128 * (j + 1)]

    def arrive(name, level, first, last, forward):
        size = half >> level
        buffer = r[f"land_{name}{level}"]
        if level == 0:
            loop(first, last, lambda slot: step_copy(name, 0, slot).wait_recv())

            def store(lanes, value):
                buffer[first:last, :, lanes] = (value + buffer[first:last, :, lanes].astype(F32)).astype(BF16)

            product(name, first, last, store)
            if forward:
                loop(first, last, lambda slot: step_copy(name, 1, slot - size // 2).start())
            return
        before = r[f"land_{name}{level - 1}"]

        def body(slot):
            step_copy(name, level, slot).wait_recv()
            total = buffer[slot].astype(F32) + before[slot].astype(F32)
            if level == bits - 1:
                finish(name, total)
            else:
                buffer[slot] = total.astype(BF16)
            if forward:
                step_copy(name, level + 1, slot - size // 2).start()

        loop(first, last, body)

    def gain_copy(bit):
        return remote_copy(r["gain_buf"].at[2 * bit], r["gain_buf"].at[2 * bit + 1], "gain", bit, partner(bit))

    def gain_step(bit):
        gain_copy(bit).wait_recv()
        total = r["gain_buf"][2 * bit] + r["gain_buf"][2 * bit + 1]
        if bit < bits:
            r["gain_buf"][2 * bit + 2] = total
            gain_copy(bit + 1).start()
        else:
            for row, name in enumerate(("gain_attn_sum", "gain_mlp_sum")):
                for j in range(width // 128):
                    r[name][j : j + 1, :] = total[row : row + 1, 128 * j : 128 * (j + 1)]


    def some_rows(at):
        return pl.ds(at * block, block)

    def row_scale(value):
        return lax.rsqrt(jnp.mean(value * value, axis=-1, keepdims=True) + EPSILON)

    def first_norm(source, target):
        def body(at):
            value = source[some_rows(at), :].astype(F32)
            target[some_rows(at), :] = (value * row_scale(value) * r["gain_attn"][...]).astype(BF16)

        loop(0, micro, body)

    def by_owner(name, source):
        ref = r["row_" + name]
        ref[...] = source[...].T.reshape(ref.shape)
        pair[name].start()

    def project(left, ring, target):
        def body(at):
            total = dot(left[:, at_chunk(0)], r[ring][0, :, at_chunk(at)])
            for part in range(1, chunks):
                total += dot(left[:, at_chunk(part)], r[ring][part, :, at_chunk(at)])
            target[:, at_chunk(at)] = total.astype(BF16)

        loop(0, chunks, body)

    act, other = r["act"], r["other"]
    load_tokens.wait()
    first_norm(r["x"], act)
    by_owner("first", act)
    for index, (ring, target) in enumerate(zip(rings, ("queries", "keys", "values"))):
        for copy in attention_first[index * depth : (index + 1) * depth]:
            copy.wait()
        project(act, ring, r[target])
    halo_out.wait_recv()
    first_norm(r["x_before"], other)
    by_owner("before", other)
    project(other, "ring_up", r["keys_before"])
    project(other, "ring_down", r["values_before"])
    for slot in range(depth):
        for copy in hidden_weights(slot, slot):
            copy.start()

    quad = CHUNK // HEAD
    start = position * block
    lane_head = lax.broadcasted_iota(jnp.int32, (block, CHUNK), 1) // HEAD
    key_at = start - WIN + lax.broadcasted_iota(jnp.int32, (2 * block, CHUNK), 0)
    query_at = start + lax.broadcasted_iota(jnp.int32, (1, CHUNK), 1) % block

    def stacked(value):
        return jnp.concatenate([jnp.where(lane_head == h, value, jnp.zeros_like(value)) for h in range(quad)], axis=0)

    def unstacked(value):
        total = jnp.zeros((block, CHUNK), F32)
        for h in range(quad):
            total = jnp.where(lane_head == h, value[h * block : (h + 1) * block], total)
        return total

    def unit(index):
        return index // chunks, some_rows(index // chunks), at_chunk(index % chunks)

    def both(before, own, rows, lanes):
        return jnp.concatenate([r[before][rows, lanes], r[own][rows, lanes]], axis=0)

    def allowed(which):
        def body(at, carry):
            end, low = carry
            end = end + r["lengths"][which, at]
            return end, jnp.where(query_at >= end, end, low)

        _, low = lax.fori_loop(
            0, r["lengths"].shape[1], body, (jnp.int32(0), jnp.zeros((1, CHUNK), jnp.int32))
        )
        low = jnp.maximum(low, query_at - (WIN - 1))
        return (key_at >= low) & (key_at <= query_at)

    def scores(which, keys, queries):
        return jnp.where(allowed(which), dot_rows(keys, queries) * scale, -1e30)

    def attend(index):
        which, rows, lanes = unit(index)
        logits = scores(which, both("keys_before", "keys", rows, lanes), stacked(r["queries"][rows, lanes]))
        peak = jnp.max(logits, axis=0, keepdims=True)
        powers = jnp.exp(logits - peak)
        total = jnp.sum(powers, axis=0, keepdims=True)
        r["log_sums"][index] = jnp.broadcast_to(peak + jnp.log(total), (8, CHUNK))
        probability = (powers / total).astype(BF16)
        mixed = dot_cols(probability, both("values_before", "values", rows, lanes))
        act[rows, lanes] = unstacked(mixed).astype(BF16)

    loop(0, micro * chunks, attend)
    by_owner("attended", act)
    load_out.wait()
    middle = r["input_grad"]

    def out_project(at):
        lanes = at_chunk(at)
        middle[:, lanes] = r["x"][:, lanes].astype(F32) + dot(act[...], r["wo"][:, lanes])

    loop(0, chunks, out_project)

    def second_norm(at):
        value = middle[some_rows(at), :]
        other[some_rows(at), :] = (value * row_scale(value) * r["gain_mlp"][...]).astype(BF16)

    loop(0, micro, second_norm)
    by_owner("second", other)


    def hidden_part(gate, up, grad_hidden):
        sigmoid = jax.nn.sigmoid(gate)
        silu = gate * sigmoid
        hidden = (silu * up).astype(BF16)
        dgate = (grad_hidden * up * sigmoid * (1.0 + gate * (1.0 - sigmoid))).astype(BF16)
        return hidden, dgate, (grad_hidden * silu).astype(BF16)

    columns = r["columns"]

    def hidden_chunk(at, prefetch):
        slot = at % depth
        for copy in hidden_weights(at, at):
            copy.wait()
        hidden, dgate, dup = hidden_part(
            dot_rows(other[...], r["ring_gate"][slot]),
            dot_rows(other[...], r["ring_up"][slot]),
            dot_rows(r["col_cot"][0], r["ring_down"][slot]),
        )
        lanes = at_chunk(at)
        r["hidden"][:, lanes] = hidden
        r["col_dgate"][0, :, lanes] = dgate
        r["col_dup"][0, :, lanes] = dup
        columns[lanes, :] = hidden.astype(F32).T
        if prefetch:
            for copy in hidden_weights(at + depth, at + depth):
                copy.start()

    load_cot.wait()
    for copy in load_tails:
        copy.wait()
    for at in range(full):
        hidden_chunk(at, at < kept)
    hidden, dgate, dup = hidden_part(
        dot_rows(other[...], r["tail_gate"][...]),
        dot_rows(other[...], r["tail_up"][...]),
        dot_rows(r["col_cot"][0], r["tail_down"][...]),
    )
    r["hidden"][:, past] = hidden
    r["col_dgate"][0, :, past] = dgate
    r["col_dup"][0, :, past] = dup
    r["square"][...] = jnp.zeros_like(r["square"])
    r["square"][:, :tail] = hidden.astype(F32)
    columns[pl.ds(full * CHUNK, CHUNK), :] = r["square"][...].T
    own_rows = hidden_width // groups
    held_rows = r["row_hidden"].shape[2]
    for owner in range(groups):
        r["row_hidden"][owner // 2, owner % 2] = columns[pl.ds(owner * own_rows, held_rows), :].astype(BF16)
    pair["hidden"].start()
    pair["dgate"].start()
    pair["dup"].start()
    send_product("down")
    send_product("gate")
    send_product("up")


    sums = [pl.ds(n * CHUNK, CHUNK) for n in range(2 * chunks)]

    def fold(hidden, dgate, dup, gate_ref, up_ref, down_ref):
        back = dot(dgate, gate_ref[...]) + dot(dup, up_ref[...])
        onward = dot(hidden, down_ref[...])
        for n in range(chunks):
            columns[sums[n], :] += back[:, n * CHUNK : (n + 1) * CHUNK]
            columns[sums[chunks + n], :] += onward[:, n * CHUNK : (n + 1) * CHUNK]

    def fold_chunk(at, arrived, prefetch):
        slot = at % depth
        chunk = at - depth if arrived else at - depth - full
        if not arrived:
            for copy in hidden_weights(chunk, at):
                copy.wait()
        lanes = at_chunk(chunk)
        fold(
            r["hidden"][:, lanes], r["col_dgate"][0, :, lanes], r["col_dup"][0, :, lanes],
            *(r[ring].at[slot] for ring in rings),
        )
        if prefetch:
            for copy in hidden_weights(at - full, at + depth):
                copy.start()

    for some in sums:
        columns[some, :] = jnp.zeros((CHUNK, CHUNK), F32)
    fold(
        r["hidden"][:, past], r["col_dgate"][0, :, past], r["col_dup"][0, :, past],
        r["tail_gate"], r["tail_up"], r["tail_down"],
    )
    for at in range(full, 2 * full):
        fold_chunk(at, at < full + depth, at < full + kept)
    for copy in attention_again:
        copy.start()

    def summed(at, base):
        return jnp.concatenate(
            [columns[pl.ds((base + n) * CHUNK + at * block, block), :] for n in range(chunks)],
            axis=1,
        )

    def norm_backward(grad, value, gain):
        inverse = row_scale(value)
        normed = value * inverse
        scaled = grad * gain
        mean = jnp.mean(scaled * normed, axis=-1, keepdims=True)
        return inverse * (scaled - normed * mean), jnp.sum(grad * normed, axis=0, keepdims=True)

    def middle_backward(at, gain_sum):
        rows = some_rows(at)
        value = middle[rows, :]
        r["output"][rows, :] = (value + summed(at, chunks)).astype(BF16)
        grad, part = norm_backward(summed(at, 0), value, r["gain_mlp"][...])
        grad = grad + r["col_cot"][0, rows, :].astype(F32)
        middle[rows, :] = grad
        r["col_branch"][0, rows, :] = grad.astype(BF16)
        return gain_sum + part

    gain_mlp_sum = lax.fori_loop(0, micro, middle_backward, jnp.zeros((1, width), F32))
    pair["branch"].start()

    def attended_backward(at):
        r["grad_attended"][:, at_chunk(at)] = dot_rows(r["col_branch"][0], r["wo"][at_chunk(at), :]).astype(BF16)

    loop(0, chunks, attended_backward)


    def attend_backward(index):
        which, rows, lanes = unit(index)
        keys = both("keys_before", "keys", rows, lanes)
        values = both("values_before", "values", rows, lanes)
        queries = stacked(r["queries"][rows, lanes])
        grads = stacked(r["grad_attended"][rows, lanes])
        probability = jnp.exp(scores(which, keys, queries) - r["log_sums"][index][:1])
        grad_prob = dot_rows(values, grads)
        delta = jnp.sum(probability * grad_prob, axis=0, keepdims=True)
        grad_scores = (scale * probability * (grad_prob - delta)).astype(BF16)
        r["col_dquery"][0, rows, lanes] = unstacked(dot_cols(grad_scores, keys)).astype(BF16)
        dkey = dot(grad_scores, queries).astype(BF16)
        dvalue = dot(probability.astype(BF16), grads).astype(BF16)
        lanes_value = at_chunk(chunks + index % chunks)
        r["col_dkvback"][0, rows, lanes] = dkey[:block]
        r["col_dkvback"][0, rows, lanes_value] = dvalue[:block]
        r["col_dkeyval"][0, rows, lanes] = dkey[block:]
        r["col_dkeyval"][0, rows, lanes_value] = dvalue[block:]

    loop(0, micro * chunks, attend_backward)
    for name in ("dquery", "dkeyval", "dkvback"):
        pair[name].start()
    send_product("out")

    def through_keys(ref, at):
        return dot_rows(ref[0, :, :width], r["ring_up"][at]) + dot_rows(ref[0, :, width:], r["ring_down"][at])

    def back_chunk(at):
        r["back_out"][:, at_chunk(at)] = through_keys(r["col_dkvback"], at).astype(BF16)

    def first_chunk(at):
        columns[at_chunk(at), :] = through_keys(r["col_dkeyval"], at) + dot_rows(
            r["col_dquery"][0], r["ring_gate"][at]
        )

    for copy in attention_again:
        copy.wait()
    loop(0, chunks, back_chunk)
    pl.when(position > 0)(halo_back.start)
    send_product("query")
    send_product("keyval")
    loop(0, chunks, first_chunk)


    def input_backward(at, gain_sum):
        rows = some_rows(at)
        back = jnp.where(position < devices - 1, r["back_in"][rows, :].astype(F32), 0.0)
        grad = summed(at, 0) + back
        grad, part = norm_backward(grad, r["x"][rows, :].astype(F32), r["gain_attn"][...])
        middle[rows, :] = middle[rows, :] + grad
        return gain_sum + part

    turn = ("gate", "up", "down", "query", "keyval", "out")
    for level in range(bits):
        size = half >> level
        if level > 0:
            gain_step(level - 1)
        for name in turn:
            if size > 1:
                arrive(name, level, size // 2, size, True)
        for name in turn:
            arrive(name, level, 0, max(size // 2, 1), False)
        if level == 0:
            pl.when(position < devices - 1)(halo_back.wait_recv)
            gain_attn_sum = lax.fori_loop(0, micro, input_backward, jnp.zeros((1, width), F32))
            r["gain_buf"][0] = jnp.concatenate(
                [gain_attn_sum, gain_mlp_sum, jnp.zeros((6, width), F32)], axis=0
            )
            gain_copy(0).start()
    gain_step(bits - 1)
    gain_step(bits)

    halo_out.wait_send()
    pl.when(position > 0)(halo_back.wait_send)
    for copy in pair.values():
        copy.wait_send()
    for bit in range(bits + 1):
        gain_copy(bit).wait_send()
    for name in NAMES:
        for level in range(bits):
            loop(0, half >> level, lambda slot: step_copy(name, level, slot).wait_send())


def layer(tokens, gain_attn, gain_mlp, weights, cotangent, lengths, micro, devices, groups):
    rows_all, width = tokens.shape
    hidden_width = weights["w_gate"].shape[0]
    block = rows_all // micro
    bits = groups.bit_length() - 2
    count = 1 << bits
    half = count // 2
    chunks = width // CHUNK
    padded = round_up(hidden_width, CHUNK)
    tail = hidden_width % CHUNK
    depth = chunks
    unit_rows = {name: width // groups for name in ROWS}
    unit_rows["hidden"] = round_up(hidden_width // groups, 16)
    widths = {name: width for name in COLS}
    widths.update(dgate=padded, dup=padded, dkeyval=2 * width, dkvback=2 * width)

    inputs = {"tokens": tokens, "cotangent": cotangent, **weights}
    any_spec = pl.BlockSpec(memory_space=pl.ANY)
    vmem_spec = pl.BlockSpec(memory_space=pltpu.VMEM)
    in_specs = [any_spec] * len(inputs) + [vmem_spec] * 2 + [pl.BlockSpec(memory_space=pltpu.SMEM)]
    inputs.update(gain_attn=gain_attn[None], gain_mlp=gain_mlp[None], lengths=lengths)

    outs = {
        "output": ((rows_all, width), BF16),
        "input_grad": ((rows_all, width), F32),
        "gain_attn_sum": ((width // 128, 128), F32),
        "gain_mlp_sum": ((width // 128, 128), F32),
    }
    own = {"query": width * width, "keyval": width * width, "value": width * width, "out": width * width}
    own.update(gate=width * hidden_width, up=width * hidden_width, down=width * hidden_width)
    for name, size in own.items():
        outs["flat_" + name] = ((size // groups // 128, 128), F32)

    scratch = {
        "x": pltpu.VMEM((rows_all, width), BF16),
        "x_before": pltpu.VMEM((rows_all, width), BF16),
        "act": pltpu.VMEM((rows_all, width), BF16),
        "other": pltpu.VMEM((rows_all, width), BF16),
        "queries": pltpu.VMEM((rows_all, width), BF16),
        "keys": pltpu.VMEM((rows_all, width), BF16),
        "values": pltpu.VMEM((rows_all, width), BF16),
        "keys_before": pltpu.VMEM((rows_all, width), BF16),
        "values_before": pltpu.VMEM((rows_all, width), BF16),
        "grad_attended": pltpu.VMEM((rows_all, width), BF16),
        "back_out": pltpu.VMEM((rows_all, width), BF16),
        "back_in": pltpu.VMEM((rows_all, width), BF16),
        "log_sums": pltpu.VMEM((micro * chunks, 8, CHUNK), F32),
        "wo": pltpu.VMEM((width, width), BF16),
        "ring_gate": pltpu.VMEM((depth, CHUNK, width), BF16),
        "ring_up": pltpu.VMEM((depth, CHUNK, width), BF16),
        "ring_down": pltpu.VMEM((depth, CHUNK, width), BF16),
        "tail_gate": pltpu.VMEM((tail, width), BF16),
        "tail_up": pltpu.VMEM((tail, width), BF16),
        "tail_down": pltpu.VMEM((tail, width), BF16),
        "hidden": pltpu.VMEM((rows_all, padded), BF16),
        "columns": pltpu.VMEM((padded, rows_all), F32),
        "square": pltpu.VMEM((rows_all, CHUNK), F32),
        "turn": pltpu.VMEM((padded // 128 * unit_rows["second"], 128), F32),
        "gain_buf": pltpu.VMEM((2 * bits + 2, 8, width), F32),
    }
    for name in ROWS:
        scratch["row_" + name] = pltpu.VMEM((count, 2, unit_rows[name], rows_all), BF16)
        scratch["peer_" + name] = pltpu.VMEM((count, unit_rows[name], rows_all), BF16)
    for name in COLS:
        scratch["col_" + name] = pltpu.VMEM((2, rows_all, widths[name]), BF16)
    for name, ((row, col), *_) in MATRICES.items():
        shape = (unit_rows[row], widths[col])
        scratch["send_" + name] = pltpu.VMEM((half,) + shape, BF16)
        for level in range(bits):
            scratch[f"land_{name}{level}"] = pltpu.VMEM((half >> level,) + shape, BF16)
    copies = {"pair": (len(ROWS) + len(COLS),), "halo": (2,), "step": (len(NAMES), count), "gain": (bits + 1,)}
    scratch["local_sem"] = pltpu.SemaphoreType.DMA((6,))
    scratch["ring_sem"] = pltpu.SemaphoreType.DMA((3, 2 * (hidden_width // CHUNK + depth)))
    for name, shape in copies.items():
        scratch[name + "_send"] = pltpu.SemaphoreType.DMA(shape)
        scratch[name + "_recv"] = pltpu.SemaphoreType.DMA(shape)

    sizes = (micro, block, width, hidden_width, devices, groups)
    results = pl.pallas_call(
        functools.partial(layer_kernel, sizes, tuple(inputs), tuple(outs), tuple(scratch)),
        out_shape=[jax.ShapeDtypeStruct(*spec) for spec in outs.values()],
        in_specs=in_specs,
        out_specs=[vmem_spec] * len(outs),
        scratch_shapes=list(scratch.values()),
        compiler_params=pltpu.CompilerParams(
            collective_id=0, has_side_effects=True, vmem_limit_bytes=63 * 2**20
        ),
        name="layer",
    )(*inputs.values())
    return dict(zip(outs, handed_on(results)))


def hand_on_kernel(count, *refs):
    sources, targets, passing = (refs[part * count : (part + 1) * count] for part in range(3))
    sems = refs[-1]
    arriving = [
        pltpu.make_async_copy(source, middle, sems.at[0, index])
        for index, (source, middle) in enumerate(zip(sources, passing))
    ]
    leaving = [
        pltpu.make_async_copy(middle, target, sems.at[1, index])
        for index, (middle, target) in enumerate(zip(passing, targets))
    ]
    for copy in arriving:
        copy.start()
    for before, copy in zip(arriving, leaving):
        before.wait()
        copy.start()
    for copy in leaving:
        copy.wait()


def handed_on(arrays):
    any_spec = pl.BlockSpec(memory_space=pl.ANY)
    count = len(arrays)
    return pl.pallas_call(
        functools.partial(hand_on_kernel, count),
        out_shape=[jax.ShapeDtypeStruct(array.shape, array.dtype) for array in arrays],
        in_specs=[any_spec] * count,
        out_specs=[any_spec] * count,
        scratch_shapes=[pltpu.VMEM(array.shape, array.dtype) for array in arrays]
        + [pltpu.SemaphoreType.DMA((2, count))],
        name="hand_on",
    )(*arrays)


def per_device(
    tokens, gain_attn, gain_mlp, w_query, w_key, w_value, w_out, w_gate, w_up, w_down, cotangent, lengths
):
    devices = lax.axis_size("seq")
    groups = min(devices, MOST_GROUPS)
    lower = devices // groups
    micro, block, width = tokens.shape
    weights = dict(
        w_query=w_query, w_key=w_key, w_value=w_value, w_out=w_out, w_gate=w_gate.T, w_up=w_up.T, w_down=w_down
    )
    result = layer(
        tokens.reshape(micro * block, width), gain_attn, gain_mlp, weights,
        cotangent.reshape(micro * block, width), lengths, micro, devices, groups,
    )
    near = [[high * lower + low for low in range(lower)] for high in range(groups)]

    def slice_of(name):
        flat = result["flat_" + name].reshape(-1)
        if lower == 1:
            return flat
        return lax.psum_scatter(flat, "seq", axis_index_groups=near, tiled=True)

    gain_sums = [result["gain_attn_sum"].reshape(-1), result["gain_mlp_sum"].reshape(-1)]
    if lower > 1:
        gain_sums = lax.psum(gain_sums, "seq", axis_index_groups=near)
    return (
        result["output"].reshape(tokens.shape),
        result["input_grad"].reshape(tokens.shape),
        gain_sums[0],
        gain_sums[1],
        slice_of("query"),
        slice_of("keyval"),
        slice_of("value"),
        slice_of("out"),
        slice_of("gate"),
        slice_of("up"),
        slice_of("down"),
    )


def solution(mesh):
    tokens_spec = P(None, "seq", None)
    return jax.shard_map(
        per_device,
        mesh=mesh,
        in_specs=(tokens_spec,) + (P(),) * 9 + (tokens_spec, P()),
        out_specs=(tokens_spec, tokens_spec, P(), P()) + (P("seq"),) * 7,
        check_vma=False,
    )
```

```python
import functools
import math

import jax
import jax.numpy as jnp
from jax import lax
from jax.experimental import pallas as pl
from jax.experimental.pallas import tpu as pltpu
from jax.sharding import PartitionSpec as P

HEAD = 64
WIN = 64
EPSILON = 1e-05
MESH = pl.DeviceIdType.MESH
MOST_GROUPS = 32
CHUNK = 256
BF16 = jnp.bfloat16
F32 = jnp.float32

MATRICES = {
    "down": (("hidden", "cot"),),
    "gate": (("second", "dgate"),),
    "up": (("second", "dup"),),
    "query": (("first", "dquery"),),
    "keyval": (("first", "dkeyval"), ("before", "dkvback")),
    "out": (("attended", "branch"),),
}
ROWS = ("first", "before", "attended", "second", "hidden")
CHUNKED = ("dgate", "dup")
COLS = ("cot", "dgate", "dup", "branch", "dquery", "dkeyval", "dkvback")
PARTS = {
    "gate": ("gate", 0, 11, "ascending"),
    "up": ("up", 0, 11, "swapped"),
    "down": ("down", 0, 3, "last_first"),
    "rest": ("down", 3, 4, "ascending"),
    "out": ("out", 0, 4, "ascending"),
    "query": ("query", 0, 4, "ascending"),
    "keyval": ("keyval", 0, 8, "swapped"),
}
INDEX = {name: index for index, name in enumerate(PARTS)}
SPANS = (1, 2, 4, 4)
LAG = 2


SCHEDULE = {
    "middle": (
        ("gate", 0, 0),
        ("gate", 0, 2),
    ),
    "attend0": (
        ("gate", 0, 4),
        ("down", 0, 0),
        ("up", 0, 0),
        ("gate", 0, 6),
    ),
    "attend1": (
        ("down", 0, 1),
        ("up", 0, 2),
        ("gate", 0, 8),
        ("up", 0, 4),
        ("gate", 0, 10),
        ("up", 0, 6),
    ),
    "attend2": (
        ("up", 0, 8),
        ("gate", 1, 0),
        ("down", 0, 2),
    ),
    "attend3": (
        ("rest", 0, 0),
        ("down", 1, 0),
        ("up", 0, 10),
        ("gate", 1, 4),
    ),
    "back": (
        ("up", 1, 0),
    ),
    "query": (
        ("gate", 1, 8),
    ),
    "keyval": (
        ("gate", 2, 0),
    ),
    "first": (
        ("up", 1, 4),
        ("rest", 1, 0),
    ),
    "input": (
        ("gate", 2, 4),
        ("up", 1, 8),
        ("down", 2, 0),
        ("down", 1, 1),
        ("down", 1, 2),
        ("keyval", 0, 0),
    ),
    "gain0": (
        ("up", 2, 0),
        ("gate", 2, 8),
        ("gate", 3, 0),
        ("out", 0, 0),
    ),
    "gain1": (
        ("keyval", 0, 2),
        ("up", 2, 4),
    ),
    "gain2": (
        ("rest", 2, 0),
        ("keyval", 0, 4),
        ("out", 0, 2),
        ("gate", 3, 4),
    ),
    "gain3": (
        ("up", 2, 8),
        ("up", 3, 0),
        ("gate", 3, 8),
        ("keyval", 0, 6),
        ("query", 0, 0),
        ("up", 3, 4),
        ("down", 3, 0),
        ("rest", 3, 0),
        ("up", 3, 8),
        ("query", 0, 2),
        ("out", 1, 0),
        ("down", 2, 1),
        ("down", 2, 2),
        ("query", 1, 0),
        ("out", 2, 0),
        ("down", 3, 1),
        ("down", 3, 2),
        ("keyval", 1, 0),
        ("query", 2, 0),
        ("out", 3, 0),
        ("keyval", 1, 4),
        ("keyval", 2, 0),
        ("query", 3, 0),
        ("keyval", 2, 4),
        ("keyval", 3, 0),
        ("keyval", 3, 4),
    ),
}


def round_up(value, unit):
    return -(-value // unit) * unit


def bit_order(kind, bits):
    ascending = list(range(1, bits + 1))
    if kind == "swapped":
        return [2, 1] + ascending[2:]
    if kind == "last_first":
        return ascending[2:] + [1, 2]
    return ascending


def length(name):
    return PARTS[name][2] - PARTS[name][1]


def step_span(name, level):
    return 1 if PARTS[name][0] == "down" else SPANS[min(level, len(SPANS) - 1)]


def step_layout(bits):
    places, total = {}, 0
    for name in PARTS:
        for level in range(bits):
            places[name, level] = total
            total += -(-length(name) // step_span(name, level))
    return places, total


def bit_of(number, bit):
    return (number // (1 << bit)) % 2


def flip(number, bit):
    return number + (1 << bit) * (1 - 2 * bit_of(number, bit))


def dot(left, right):
    return jnp.dot(left, right, preferred_element_type=F32)


def dot_rows(left, right):
    return lax.dot_general(left, right, (((1,), (1,)), ((), ())), preferred_element_type=F32)


def dot_cols(left, right):
    return lax.dot_general(left, right, (((0,), (0,)), ((), ())), preferred_element_type=F32)


def at_chunk(index, size=CHUNK):
    return pl.ds(index * size, size)


def loop(first, last, body, **options):
    def step(at, carry):
        body(at)
        return carry

    lax.fori_loop(first, last, step, 0, **options)


def layer_kernel(sizes, in_names, out_names, scratch_names, *refs):
    micro, block, width, hidden_width, devices, groups = sizes
    r = dict(zip(in_names + out_names + scratch_names, refs))
    lower = devices // groups
    bits = groups.bit_length() - 2
    count = 1 << bits
    half = count // 2
    step_places, _ = step_layout(bits)
    orders = {name: bit_order(kind, bits) for name, (_, _, _, kind) in PARTS.items()}
    rows_all = micro * block
    chunks = width // CHUNK
    full = hidden_width // CHUNK
    tail = hidden_width % CHUNK
    depth = r["ring_gate"].shape[0]
    kept = full - depth
    scale = 1.0 / math.sqrt(HEAD)

    schedule = SCHEDULE
    if bits != 4:
        schedule = {"last": [
            (name, level, first)
            for level in range(bits) for name in PARTS
            for first in range(0, length(name), step_span(name, min(level + 1, bits - 1)))
        ]}

    position = lax.axis_index("seq")
    me, rest = position // lower, position % lower
    core = me % 2
    my_unit = me // 2
    after = ((position + 1) % devices,)
    behind = ((position + devices - 1) % devices,)

    def partner(bit):
        return (flip(me, bit) * lower + rest,)


    def local_copy(source, target, index):
        return pltpu.make_async_copy(source, target, r["local_sem"].at[index])

    def remote_copy(source, target, sems, index, device):
        send, recv = r[sems + "_send"], r[sems + "_recv"]
        return pltpu.make_async_remote_copy(
            src_ref=source, dst_ref=target, send_sem=send.at[index], recv_sem=recv.at[index],
            device_id=device, device_id_type=MESH,
        )

    load_tokens = local_copy(r["tokens"], r["x"], 0)
    load_cot = local_copy(r["cotangent"], r["col_cot"].at[0], 1)
    load_out = local_copy(r["w_out"], r["wo"], 2)
    rings = ("ring_gate", "ring_up", "ring_down")
    past = pl.ds(full * CHUNK, tail)
    load_tails = [
        local_copy(r[name].at[past, :], r["tail_" + name[2:]], 3 + index)
        for index, name in enumerate(("w_gate", "w_up", "w_down"))
    ]
    attention_weights = [
        pltpu.make_async_copy(r[name].at[at_chunk(slot), :], r[ring].at[slot], r["ring_sem"].at[index, slot])
        for index, (name, ring) in enumerate(zip(("w_query", "w_key", "w_value"), rings))
        for slot in range(depth)
    ]

    def hidden_weights(chunk, place):
        slot = place % depth
        return [
            pltpu.make_async_copy(r[name].at[at_chunk(chunk), :], r[ring].at[slot], r["ring_sem"].at[index, slot])
            for index, (name, ring) in enumerate(zip(("w_gate", "w_up", "w_down"), rings))
        ]

    def pair_copies():
        plan = {}
        for name in ROWS:
            plan[name] = (r["row_" + name].at[:, 1 - core], r["peer_" + name])
        plan["cot"] = (r["cotangent"], r["col_cot"].at[1])
        for name in ("branch", "dquery", "dkeyval", "dkvback"):
            plan[name] = (r["col_" + name].at[0], r["col_" + name].at[1])
        return {
            name: remote_copy(source, target, "pair", index, partner(0))
            for index, (name, (source, target)) in enumerate(plan.items())
        }

    pair = pair_copies()
    ready = set()

    def need(name):
        if name not in ready and name not in CHUNKED:
            ready.add(name)
            pair[name].wait_recv()

    def pair_chunk(first, last=None):
        ref = r["col_hidden"]
        some = pl.ds(first, 1 if last is None else last - first)
        return pltpu.make_async_remote_copy(
            src_ref=ref.at[0, some], dst_ref=ref.at[1, some],
            send_sem=r["chunk_send"].at[0], recv_sem=r["chunk_recv"].at[first],
            device_id=partner(0), device_id_type=MESH,
        )

    halo_out = remote_copy(r["x"], r["x_before"], "halo", 0, after)
    halo_back = remote_copy(r["back_out"], r["back_in"], "halo", 1, behind)

    load_tokens.start()
    r["x_before"][...] = jnp.zeros_like(r["x_before"])
    barrier = pltpu.get_barrier_semaphore()
    for device in [after, behind] + [partner(bit) for bit in range(bits + 1)]:
        pl.semaphore_signal(barrier, inc=1, device_id=device, device_id_type=MESH)
    for copy in attention_weights:
        copy.start()
    for part in range(2):
        r["col_hidden"][0, full, part] = jnp.zeros((rows_all, CHUNK), BF16)


    def unit_at(order, slot):
        unit = my_unit
        for place, bit in enumerate(order):
            rel = (slot // (1 << (bits - 1 - place))) % 2
            unit = unit + (1 << (bit - 1)) * rel * (1 - 2 * bit_of(me, bit))
        return unit

    def factors(name, base):
        matrix = PARTS[name][0]
        units = [unit_at(orders[name], base + slot) for slot in range(half)]
        pairs = []
        for row, col in MATRICES[matrix]:
            need(row)
            need(col)
            for source in range(2):
                parts = [
                    r["row_" + row][unit, core] if source == 0 else r["peer_" + row][unit] for unit in units
                ]
                pairs.append((jnp.concatenate(parts, axis=0), col, source))
        return pairs

    def product(pairs, chunk):
        total = None
        for left, col, source in pairs:
            if col in CHUNKED:
                right = r["col_hidden"][source, chunk, CHUNKED.index(col)]
            else:
                right = r["col_" + col][source, :, at_chunk(chunk)]
            term = dot(left, right)
            total = term if total is None else total + term
        return total.reshape(half, total.shape[0] // half, CHUNK)

    def step_copy(name, level, first, last):
        size = half >> level
        some = pl.ds(first, last - first)
        if level == 0:
            source = r["send_" + name].at[some]
        else:
            source = r[f"land_{name}{level - 1}"].at[some, pl.ds(size, size)]
        place = step_places[name, level] + first // step_span(name, level)
        return pltpu.make_async_remote_copy(
            src_ref=source, dst_ref=r[f"land_{name}{level}"].at[some],
            send_sem=r["step_send"].at[INDEX[name], level], recv_sem=r["step_recv"].at[place],
            device_id=partner(orders[name][level]), device_id_type=MESH,
        )

    def send_products(name):
        pairs = factors(name, half)
        for at in range(length(name)):
            r["send_" + name][at] = product(pairs, PARTS[name][1] + at).astype(BF16)
            step_copy(name, 0, at, at + 1).start()

    def arrive(name, level, first):
        last = min(first + step_span(name, min(level + 1, bits - 1)), length(name))
        here = r[f"land_{name}{level}"]
        pairs = factors(name, 0) if level == 0 else None
        size = half >> level
        span = step_span(name, level)
        for at in range(first, last, span):
            step_copy(name, level, at, min(at + span, last)).wait_recv()
        for at in range(first, last):
            if level == 0:
                own = product(pairs, PARTS[name][1] + at)
            else:
                own = r[f"land_{name}{level - 1}"][at, :size].astype(F32)
            total = own + here[at].astype(F32)
            if level < bits - 1:
                here[at] = total.astype(BF16)
            elif name in ("gate", "up"):
                rows = total.shape[1]
                for part in range(CHUNK // 128):
                    place = (at * (CHUNK // 128) + part) * rows
                    r["turn_" + name][pl.ds(place, rows), :] = total[0, :, 128 * part : 128 * (part + 1)]
            else:
                r["total_" + name][at] = total[0]
        if level < bits - 1:
            step_copy(name, level + 1, first, last).start()
        elif last == length(name):
            finish(name)

    def finish(name):
        if name in ("gate", "up"):
            flat, turn = r["flat_" + name], r["turn_" + name]
            whole = hidden_width // 128
            steps = hidden_width // 64
            rows = turn.shape[0] // (whole + 1)
            few = rows // 2
            even = [turn[pl.ds(rows * j, few, stride=2), :] for j in range(whole + 1)]
            odd = [pltpu.roll(turn[pl.ds(rows * j + 1, few, stride=2), :], 64, 1) for j in range(whole + 1)]
            low = lax.broadcasted_iota(jnp.int32, (few, 128), 1) < 64
            for j in range(whole):
                flat[pl.ds(j, few, stride=steps), :] = even[j]
                flat[pl.ds(whole + 1 + j, few, stride=steps), :] = jnp.where(low, odd[j], odd[j + 1])
            flat[pl.ds(whole, few, stride=steps), :] = jnp.where(low, even[whole], odd[0])
            return
        matrix, first, last, _ = PARTS[name]
        per_row = width // 128
        for at in range(last - first):
            total = r["total_" + name][at]
            for part in range(CHUNK // 128):
                column = (first + at) * (CHUNK // 128) + part
                target = "flat_value" if column >= per_row else "flat_" + matrix
                rows = r[target].shape[0] // per_row
                r[target][pl.ds(column % per_row, rows, stride=per_row), :] = total[:rows, 128 * part : 128 * (part + 1)]

    def gain_copy(bit):
        return remote_copy(r["gain_buf"].at[2 * bit], r["gain_buf"].at[2 * bit + 1], "gain", bit, partner(bit))

    def gain_step(bit):
        gain_copy(bit).wait_recv()
        total = r["gain_buf"][2 * bit] + r["gain_buf"][2 * bit + 1]
        if bit < bits:
            r["gain_buf"][2 * bit + 2] = total
            gain_copy(bit + 1).start()
        else:
            for row, name in enumerate(("gain_attn_sum", "gain_mlp_sum")):
                for j in range(width // 128):
                    r[name][j : j + 1, :] = total[row : row + 1, 128 * j : 128 * (j + 1)]

    def arrivals(point):
        for name, level, first in schedule.get(point, ()):
            arrive(name, level, first)


    def some_rows(at):
        return pl.ds(at * block, block)

    def row_scale(value):
        return lax.rsqrt(jnp.mean(value * value, axis=-1, keepdims=True) + EPSILON)

    def first_norm(source, target):
        def body(at):
            value = source[some_rows(at), :].astype(F32)
            target[some_rows(at), :] = (value * row_scale(value) * r["gain_attn"][...]).astype(BF16)

        loop(0, micro, body)

    def by_owner(name, source):
        ref = r["row_" + name]
        ref[...] = source[...].T.reshape(ref.shape)
        pair[name].start()

    def project(left, ring, target):
        target[...] = dot(left[...], r[ring][...].reshape(width, width)).astype(BF16)

    act, other = r["act"], r["other"]
    load_tokens.wait()
    pl.semaphore_wait(barrier, bits + 3)
    pl.when(position < devices - 1)(halo_out.start)
    first_norm(r["x"], act)
    load_out.start()
    load_cot.start()
    for copy in load_tails:
        copy.start()
    for index, (ring, target) in enumerate(zip(rings, ("queries", "keys", "values"))):
        for copy in attention_weights[index * depth : (index + 1) * depth]:
            copy.wait()
        project(act, ring, r[target])
    pl.when(position > 0)(halo_out.wait_recv)
    first_norm(r["x_before"], other)
    project(other, "ring_up", r["keys_before"])
    project(other, "ring_down", r["values_before"])
    for slot in range(depth):
        for copy in hidden_weights(slot, slot):
            copy.start()

    quad = CHUNK // HEAD
    start = position * block
    lane_head = lax.broadcasted_iota(jnp.int32, (block, CHUNK), 1) // HEAD
    key_at = start - WIN + lax.broadcasted_iota(jnp.int32, (2 * block, CHUNK), 0)
    query_at = start + lax.broadcasted_iota(jnp.int32, (1, CHUNK), 1) % block

    def stacked(value):
        return jnp.concatenate([jnp.where(lane_head == h, value, jnp.zeros_like(value)) for h in range(quad)], axis=0)

    def unstacked(value):
        total = jnp.zeros((block, CHUNK), F32)
        for h in range(quad):
            total = jnp.where(lane_head == h, value[h * block : (h + 1) * block], total)
        return total

    def unit(index):
        return index // chunks, some_rows(index // chunks), at_chunk(index % chunks)

    def both(before, own, rows, lanes):
        return jnp.concatenate([r[before][rows, lanes], r[own][rows, lanes]], axis=0)

    def allowed(which):
        def body(at, carry):
            end, low = carry
            end = end + r["lengths"][which, at]
            return end, jnp.where(query_at >= end, end, low)

        _, low = lax.fori_loop(
            0, r["lengths"].shape[1], body, (jnp.int32(0), jnp.zeros((1, CHUNK), jnp.int32))
        )
        low = jnp.maximum(low, query_at - (WIN - 1))
        return (key_at >= low) & (key_at <= query_at)

    def scores(which, keys, queries):
        return jnp.where(allowed(which), dot_rows(keys, queries) * scale, -1e30)

    def attend(index):
        which, rows, lanes = unit(index)
        logits = scores(which, both("keys_before", "keys", rows, lanes), stacked(r["queries"][rows, lanes]))
        peak = jnp.max(logits, axis=0, keepdims=True)
        powers = jnp.exp(logits - peak)
        total = jnp.sum(powers, axis=0, keepdims=True)
        r["log_sums"][index] = jnp.broadcast_to(peak + jnp.log(total), (8, CHUNK))
        probability = (powers / total).astype(BF16)
        mixed = dot_cols(probability, both("values_before", "values", rows, lanes))
        act[rows, lanes] = unstacked(mixed).astype(BF16)

    pair["cot"].start()
    loop(0, micro * chunks, attend, unroll=2)
    load_out.wait()
    middle = r["input_grad"]

    middle[...] = r["x"][...].astype(F32) + dot(act[...], r["wo"][...])

    def second_norm(at):
        value = middle[some_rows(at), :]
        other[some_rows(at), :] = (value * row_scale(value) * r["gain_mlp"][...]).astype(BF16)

    loop(0, micro, second_norm)
    by_owner("second", other)


    def hidden_part(gate, up, grad_hidden):
        sigmoid = jax.nn.sigmoid(gate)
        silu = gate * sigmoid
        hidden = (silu * up).astype(BF16)
        dgate = (grad_hidden * up * sigmoid * (1.0 + gate * (1.0 - sigmoid))).astype(BF16)
        return hidden, dgate, (grad_hidden * silu).astype(BF16)

    columns = r["columns"]

    def hidden_chunk(at, prefetch):
        slot = at % depth
        for copy in hidden_weights(at, at):
            copy.wait()
        wait_chunk(at - LAG)
        hidden, dgate, dup = hidden_part(
            dot_rows(other[...], r["ring_gate"][slot]),
            dot_rows(other[...], r["ring_up"][slot]),
            dot_rows(r["col_cot"][0], r["ring_down"][slot]),
        )
        lanes = at_chunk(at)
        form_chunk(at - LAG)
        r["hidden"][:, lanes] = hidden
        r["col_hidden"][0, at, 0] = dgate
        r["col_hidden"][0, at, 1] = dup
        columns[lanes, :] = hidden.astype(F32).T
        pair_chunk(at).start()
        send_chunk(at - LAG)
        if prefetch:
            for copy in hidden_weights(at + depth, at + depth):
                copy.start()

    early = (("gate", "dgate"), ("up", "dup"))
    early_factors = {}

    def wait_chunk(at):
        if at >= 0:
            pair_chunk(at).wait_recv()

    def form_chunk(at):
        if at >= 0:
            for name, _ in early:
                if name not in early_factors:
                    early_factors[name] = factors(name, half)
                r["send_" + name][at] = product(early_factors[name], at).astype(BF16)

    def send_chunk(at):
        if at >= 0:
            for name, _ in early:
                step_copy(name, 0, at, at + 1).start()

    load_cot.wait()
    for copy in load_tails:
        copy.wait()
    for at in range(full):
        hidden_chunk(at, at < kept)
    hidden, dgate, dup = hidden_part(
        dot_rows(other[...], r["tail_gate"][...]),
        dot_rows(other[...], r["tail_up"][...]),
        dot_rows(r["col_cot"][0], r["tail_down"][...]),
    )
    r["hidden"][:, past] = hidden
    r["col_hidden"][0, full, 0, :, :tail] = dgate
    r["col_hidden"][0, full, 1, :, :tail] = dup
    pair_chunk(full).start()
    r["square"][...] = jnp.zeros_like(r["square"])
    r["square"][:, :tail] = hidden.astype(F32)
    columns[pl.ds(full * CHUNK, CHUNK), :] = r["square"][...].T
    own_rows = hidden_width // groups
    held_rows = r["row_hidden"].shape[2]
    for owner in range(groups):
        r["row_hidden"][owner // 2, owner % 2] = columns[pl.ds(owner * own_rows, held_rows), :].astype(BF16)
    pair["hidden"].start()
    for at in range(full - LAG, full + 1):
        wait_chunk(at)
        form_chunk(at)
        send_chunk(at)
    send_products("down")
    send_products("rest")


    sums = [pl.ds(n * CHUNK, CHUNK) for n in range(2 * chunks)]

    def fold(*pieces):
        back, onward = None, None
        for hidden, dgate, dup, gate_ref, up_ref, down_ref in pieces:
            one = dot(dgate, gate_ref[...]) + dot(dup, up_ref[...])
            two = dot(hidden, down_ref[...])
            back, onward = (one, two) if back is None else (back + one, onward + two)
        for n in range(chunks):
            columns[sums[n], :] += back[:, n * CHUNK : (n + 1) * CHUNK]
            columns[sums[chunks + n], :] += onward[:, n * CHUNK : (n + 1) * CHUNK]

    def fold_chunks(places):
        pieces = []
        for at in places:
            chunk = at - depth if at < full + depth else at - depth - full
            if at >= full + depth:
                for copy in hidden_weights(chunk, at):
                    copy.wait()
            pieces.append((
                r["hidden"][:, at_chunk(chunk)], r["col_hidden"][0, chunk, 0], r["col_hidden"][0, chunk, 1],
                *(r[ring].at[at % depth] for ring in rings),
            ))
        fold(*pieces)
        for at in places:
            if at < full + kept:
                for copy in hidden_weights(at - full, at + depth):
                    copy.start()

    for some in sums:
        columns[some, :] = jnp.zeros((CHUNK, CHUNK), F32)
    fold((
        r["hidden"][:, past], r["col_hidden"][0, full, 0, :, :tail], r["col_hidden"][0, full, 1, :, :tail],
        r["tail_gate"], r["tail_up"], r["tail_down"],
    ))
    for at in range(full, 2 * full, 2):
        fold_chunks(range(at, min(at + 2, 2 * full)))
    for copy in attention_weights:
        copy.start()

    def summed(at, base):
        return jnp.concatenate(
            [columns[pl.ds((base + n) * CHUNK + at * block, block), :] for n in range(chunks)],
            axis=1,
        )

    def norm_backward(grad, value, gain):
        inverse = row_scale(value)
        normed = value * inverse
        scaled = grad * gain
        mean = jnp.mean(scaled * normed, axis=-1, keepdims=True)
        return inverse * (scaled - normed * mean), jnp.sum(grad * normed, axis=0, keepdims=True)

    def middle_backward(at, gain_sum):
        rows = some_rows(at)
        value = middle[rows, :]
        r["output"][rows, :] = (value + summed(at, chunks)).astype(BF16)
        grad, part = norm_backward(summed(at, 0), value, r["gain_mlp"][...])
        grad = grad + r["col_cot"][0, rows, :].astype(F32)
        middle[rows, :] = grad
        r["col_branch"][0, rows, :] = grad.astype(BF16)
        return gain_sum + part

    gain_mlp_sum = lax.fori_loop(0, micro, middle_backward, jnp.zeros((1, width), F32))
    pair["branch"].start()
    by_owner("attended", act)
    for name, source in (("first", "x"), ("before", "x_before")):
        first_norm(r[source], r["back_out"])
        by_owner(name, r["back_out"])

    r["grad_attended"][...] = dot_rows(r["col_branch"][0], r["wo"][...]).astype(BF16)


    def attend_backward(index):
        which, rows, lanes = unit(index)
        keys = both("keys_before", "keys", rows, lanes)
        values = both("values_before", "values", rows, lanes)
        queries = stacked(r["queries"][rows, lanes])
        grads = stacked(r["grad_attended"][rows, lanes])
        probability = jnp.exp(scores(which, keys, queries) - r["log_sums"][index][:1])
        grad_prob = dot_rows(values, grads)
        delta = jnp.sum(probability * grad_prob, axis=0, keepdims=True)
        grad_scores = (scale * probability * (grad_prob - delta)).astype(BF16)
        r["col_dquery"][0, rows, lanes] = unstacked(dot_cols(grad_scores, keys)).astype(BF16)
        dkey = dot(grad_scores, queries).astype(BF16)
        dvalue = dot(probability.astype(BF16), grads).astype(BF16)
        lanes_value = at_chunk(chunks + index % chunks)
        r["col_dkvback"][0, rows, lanes] = dkey[:block]
        r["col_dkvback"][0, rows, lanes_value] = dvalue[:block]
        r["col_dkeyval"][0, rows, lanes] = dkey[block:]
        r["col_dkeyval"][0, rows, lanes_value] = dvalue[block:]

    arrivals("middle")
    for at in range(micro):
        loop(at * chunks, (at + 1) * chunks, attend_backward, unroll=2)
        arrivals("attend" + str(at))
    for name in ("dquery", "dkeyval", "dkvback"):
        pair[name].start()
    send_products("out")
    arrivals("out")

    def through_keys(ref, at):
        return dot_rows(ref[0, :, :width], r["ring_up"][at]) + dot_rows(ref[0, :, width:], r["ring_down"][at])

    def back_chunk(at):
        r["back_out"][:, at_chunk(at)] = through_keys(r["col_dkvback"], at).astype(BF16)

    def first_chunk(at):
        columns[at_chunk(at), :] = through_keys(r["col_dkeyval"], at) + dot_rows(
            r["col_dquery"][0], r["ring_gate"][at]
        )

    for copy in attention_weights:
        copy.wait()
    loop(0, chunks, back_chunk)
    pl.when(position > 0)(halo_back.start)
    arrivals("back")
    send_products("query")
    arrivals("query")
    send_products("keyval")
    arrivals("keyval")
    loop(0, chunks, first_chunk)
    arrivals("first")


    def input_backward(at, gain_sum):
        rows = some_rows(at)
        back = jnp.where(position < devices - 1, r["back_in"][rows, :].astype(F32), 0.0)
        grad = summed(at, 0) + back
        grad, part = norm_backward(grad, r["x"][rows, :].astype(F32), r["gain_attn"][...])
        middle[rows, :] = middle[rows, :] + grad
        return gain_sum + part

    pl.when(position < devices - 1)(halo_back.wait_recv)
    gain_attn_sum = lax.fori_loop(0, micro, input_backward, jnp.zeros((1, width), F32))
    r["gain_buf"][0] = jnp.concatenate([gain_attn_sum, gain_mlp_sum, jnp.zeros((6, width), F32)], axis=0)
    gain_copy(0).start()
    arrivals("input")
    for bit in range(bits - 1):
        gain_step(bit)
        arrivals("gain" + str(bit))
    gain_step(bits - 1)
    arrivals("gain" + str(bits - 1))
    gain_step(bits)
    arrivals("last")

    pl.when(position < devices - 1)(halo_out.wait_send)
    pl.when(position > 0)(halo_back.wait_send)
    for copy in pair.values():
        copy.wait_send()
    for bit in range(bits + 1):
        gain_copy(bit).wait_send()
    pair_chunk(0, full + 1).wait_send()
    for name in PARTS:
        for level in range(bits):
            step_copy(name, level, 0, length(name)).wait_send()


def layer(tokens, gain_attn, gain_mlp, weights, cotangent, lengths, micro, devices, groups):
    rows_all, width = tokens.shape
    hidden_width = weights["w_gate"].shape[0]
    block = rows_all // micro
    bits = groups.bit_length() - 2
    count = 1 << bits
    half = count // 2
    chunks = width // CHUNK
    padded = round_up(hidden_width, CHUNK)
    tail = hidden_width % CHUNK
    depth = chunks
    unit_rows = {name: width // groups for name in ROWS}
    unit_rows["hidden"] = round_up(hidden_width // groups, 16)
    widths = {name: width for name in COLS}
    widths.update(dkeyval=2 * width, dkvback=2 * width)

    inputs = {"tokens": tokens, "cotangent": cotangent, **weights}
    any_spec = pl.BlockSpec(memory_space=pl.ANY)
    vmem_spec = pl.BlockSpec(memory_space=pltpu.VMEM)
    in_specs = [any_spec] * len(inputs) + [vmem_spec] * 2 + [pl.BlockSpec(memory_space=pltpu.SMEM)]
    inputs.update(gain_attn=gain_attn[None], gain_mlp=gain_mlp[None], lengths=lengths)

    outs = {
        "output": ((rows_all, width), BF16),
        "input_grad": ((rows_all, width), F32),
        "gain_attn_sum": ((width // 128, 128), F32),
        "gain_mlp_sum": ((width // 128, 128), F32),
    }
    own = {"query": width * width, "keyval": width * width, "value": width * width, "out": width * width}
    own.update(gate=width * hidden_width, up=width * hidden_width, down=width * hidden_width)
    for name, size in own.items():
        outs["flat_" + name] = ((size // groups // 128, 128), F32)

    scratch = {
        "x": pltpu.VMEM((rows_all, width), BF16),
        "x_before": pltpu.VMEM((rows_all, width), BF16),
        "act": pltpu.VMEM((rows_all, width), BF16),
        "other": pltpu.VMEM((rows_all, width), BF16),
        "queries": pltpu.VMEM((rows_all, width), BF16),
        "keys": pltpu.VMEM((rows_all, width), BF16),
        "values": pltpu.VMEM((rows_all, width), BF16),
        "keys_before": pltpu.VMEM((rows_all, width), BF16),
        "values_before": pltpu.VMEM((rows_all, width), BF16),
        "grad_attended": pltpu.VMEM((rows_all, width), BF16),
        "back_out": pltpu.VMEM((rows_all, width), BF16),
        "back_in": pltpu.VMEM((rows_all, width), BF16),
        "log_sums": pltpu.VMEM((micro * chunks, 8, CHUNK), F32),
        "wo": pltpu.VMEM((width, width), BF16),
        "ring_gate": pltpu.VMEM((depth, CHUNK, width), BF16),
        "ring_up": pltpu.VMEM((depth, CHUNK, width), BF16),
        "ring_down": pltpu.VMEM((depth, CHUNK, width), BF16),
        "tail_gate": pltpu.VMEM((tail, width), BF16),
        "tail_up": pltpu.VMEM((tail, width), BF16),
        "tail_down": pltpu.VMEM((tail, width), BF16),
        "hidden": pltpu.VMEM((rows_all, padded), BF16),
        "columns": pltpu.VMEM((padded, rows_all), F32),
        "square": pltpu.VMEM((rows_all, CHUNK), F32),
        "gain_buf": pltpu.VMEM((2 * bits + 2, 8, width), F32),
    }
    for name in ROWS:
        scratch["row_" + name] = pltpu.VMEM((count, 2, unit_rows[name], rows_all), BF16)
        scratch["peer_" + name] = pltpu.VMEM((count, unit_rows[name], rows_all), BF16)
    for name in COLS:
        if name not in CHUNKED:
            scratch["col_" + name] = pltpu.VMEM((2, rows_all, widths[name]), BF16)
    scratch["col_hidden"] = pltpu.VMEM((2, padded // CHUNK, len(CHUNKED), rows_all, CHUNK), BF16)
    for name, (matrix, first, last, _) in PARTS.items():
        rows = unit_rows[MATRICES[matrix][0][0]]
        scratch["send_" + name] = pltpu.VMEM((last - first, half, rows, CHUNK), BF16)
        for level in range(bits):
            scratch[f"land_{name}{level}"] = pltpu.VMEM((last - first, half >> level, rows, CHUNK), BF16)
        if name in ("gate", "up"):
            scratch["turn_" + name] = pltpu.VMEM(((last - first) * CHUNK // 128 * rows, 128), F32)
        else:
            scratch["total_" + name] = pltpu.VMEM((last - first, rows, CHUNK), F32)
    sems = {"local_sem": (6,), "ring_sem": (3, depth)}
    sems.update(chunk_send=(1,), chunk_recv=(padded // CHUNK,))
    sems.update(step_send=(len(PARTS), bits), step_recv=(step_layout(bits)[1],))
    for name, number in (("pair", len(ROWS) + len(COLS) - len(CHUNKED)), ("halo", 2), ("gain", bits + 1)):
        sems[name + "_send"] = sems[name + "_recv"] = (number,)
    for name, shape in sems.items():
        scratch[name] = pltpu.SemaphoreType.DMA(shape)

    sizes = (micro, block, width, hidden_width, devices, groups)
    results = pl.pallas_call(
        functools.partial(layer_kernel, sizes, tuple(inputs), tuple(outs), tuple(scratch)),
        out_shape=[jax.ShapeDtypeStruct(*spec) for spec in outs.values()],
        in_specs=in_specs,
        out_specs=[vmem_spec] * len(outs),
        scratch_shapes=list(scratch.values()),
        compiler_params=pltpu.CompilerParams(
            collective_id=0, has_side_effects=True, vmem_limit_bytes=63 * 2**20
        ),
        name="layer",
    )(*inputs.values())
    return dict(zip(outs, handed_on(results)))


def hand_on_kernel(count, *refs):
    sources, targets, passing = (refs[part * count : (part + 1) * count] for part in range(3))
    sems = refs[-1]
    arriving = [
        pltpu.make_async_copy(source, middle, sems.at[0, index])
        for index, (source, middle) in enumerate(zip(sources, passing))
    ]
    leaving = [
        pltpu.make_async_copy(middle, target, sems.at[1, index])
        for index, (middle, target) in enumerate(zip(passing, targets))
    ]
    for copy in arriving:
        copy.start()
    for before, copy in zip(arriving, leaving):
        before.wait()
        copy.start()
    for copy in leaving:
        copy.wait()


def handed_on(arrays):
    any_spec = pl.BlockSpec(memory_space=pl.ANY)
    count = len(arrays)
    return pl.pallas_call(
        functools.partial(hand_on_kernel, count),
        out_shape=[jax.ShapeDtypeStruct(array.shape, array.dtype) for array in arrays],
        in_specs=[any_spec] * count,
        out_specs=[any_spec] * count,
        scratch_shapes=[pltpu.VMEM(array.shape, array.dtype) for array in arrays]
        + [pltpu.SemaphoreType.DMA((2, count))],
        name="hand_on",
    )(*arrays)


def per_device(
    tokens, gain_attn, gain_mlp, w_query, w_key, w_value, w_out, w_gate, w_up, w_down, cotangent, lengths
):
    devices = lax.axis_size("seq")
    groups = min(devices, MOST_GROUPS)
    lower = devices // groups
    micro, block, width = tokens.shape
    weights = dict(
        w_query=w_query, w_key=w_key, w_value=w_value, w_out=w_out, w_gate=w_gate.T, w_up=w_up.T, w_down=w_down
    )
    result = layer(
        tokens.reshape(micro * block, width), gain_attn, gain_mlp, weights,
        cotangent.reshape(micro * block, width), lengths, micro, devices, groups,
    )
    near = [[high * lower + low for low in range(lower)] for high in range(groups)]

    def slice_of(name):
        flat = result["flat_" + name].reshape(-1)
        if lower == 1:
            return flat
        return lax.psum_scatter(flat, "seq", axis_index_groups=near, tiled=True)

    gain_sums = [result["gain_attn_sum"].reshape(-1), result["gain_mlp_sum"].reshape(-1)]
    if lower > 1:
        gain_sums = lax.psum(gain_sums, "seq", axis_index_groups=near)
    return (
        result["output"].reshape(tokens.shape),
        result["input_grad"].reshape(tokens.shape),
        gain_sums[0],
        gain_sums[1],
        slice_of("query"),
        slice_of("keyval"),
        slice_of("value"),
        slice_of("out"),
        slice_of("gate"),
        slice_of("up"),
        slice_of("down"),
    )


def solution(mesh):
    tokens_spec = P(None, "seq", None)
    return jax.shard_map(
        per_device,
        mesh=mesh,
        in_specs=(tokens_spec,) + (P(),) * 9 + (tokens_spec, P()),
        out_specs=(tokens_spec, tokens_spec, P(), P()) + (P("seq"),) * 7,
        check_vma=False,
    )
```

```python
import functools
import math

import jax
import jax.numpy as jnp
from jax import lax
from jax.experimental import pallas as pl
from jax.experimental.pallas import tpu as pltpu
from jax.sharding import PartitionSpec as P

HEAD = 64
WIN = 64
EPSILON = 1e-05
MESH = pl.DeviceIdType.MESH
MOST_GROUPS = 32
CHUNK = 256
BF16 = jnp.bfloat16
F32 = jnp.float32

MATRICES = {
    "down": (("hidden", "cot"),),
    "gate": (("second", "dgate"),),
    "up": (("second", "dup"),),
    "query": (("first", "dquery"),),
    "keyval": (("first", "dkeyval"), ("before", "dkvback")),
    "out": (("attended", "branch"),),
}
ROWS = ("first", "before", "attended", "second", "hidden")
CHUNKED = ("dgate", "dup")
COLS = ("cot", "dgate", "dup", "branch", "dquery", "dkeyval", "dkvback")
PARTS = {
    "gate": ("gate", 0, 4, (2, 1, 4, 3), (1, 2, 4, 4)),
    "gate2": ("gate", 4, 11, (3, 1, 4, 2), (1, 1, 2, 2)),
    "up": ("up", 0, 3, (3, 4, 2, 1), (1, 1, 2, 2)),
    "up2": ("up", 3, 11, (1, 3, 4, 2), (1, 2, 4, 4)),
    "down": ("down", 0, 3, (2, 1, 4, 3), (1, 1, 1, 1)),
    "rest": ("down", 3, 4, (2, 1, 4, 3), (1, 1, 1, 1)),
    "out": ("out", 0, 4, (2, 1, 3, 4), (1, 1, 2, 2)),
    "query": ("query", 0, 4, (1, 3, 2, 4), (1, 1, 2, 2)),
    "key": ("keyval", 0, 4, (2, 3, 1, 4), (1, 1, 2, 2)),
    "keyb": ("keyval", 4, 8, (2, 1, 3, 4), (1, 1, 2, 2)),
}
INDEX = {name: index for index, name in enumerate(PARTS)}
LAG = 2


SCHEDULE = {
    "middle": (
        ("gate", 0, 0),
        ("up", 0, 0),
        ("gate", 0, 2),
        ("up", 0, 1),
        ("up", 0, 2),
        ("gate2", 0, 0),
        ("up2", 0, 0),
        ("gate2", 0, 1),
    ),
    "attend0": (
        ("gate2", 0, 2),
        ("up2", 0, 2),
        ("gate2", 0, 3),
        ("gate2", 0, 4),
    ),
    "attend1": (
        ("gate", 1, 0),
        ("gate2", 0, 5),
        ("gate2", 0, 6),
        ("up2", 0, 4),
        ("down", 0, 0),
    ),
    "attend2": (
        ("gate2", 1, 0),
        ("gate2", 1, 2),
        ("down", 0, 1),
        ("up", 1, 0),
        ("up2", 1, 0),
        ("up", 1, 2),
    ),
    "attend3": (
        ("gate2", 1, 4),
        ("down", 0, 2),
        ("gate2", 1, 6),
    ),
    "back": (
        ("gate", 2, 0),
        ("up2", 0, 6),
    ),
    "first": (
        ("down", 1, 2),
        ("up", 2, 0),
        ("up", 2, 2),
        ("up2", 1, 4),
        ("rest", 0, 0),
        ("out", 0, 0),
        ("out", 0, 1),
    ),
    "key": (
        ("down", 1, 0),
    ),
    "keyb": (
        ("down", 1, 1),
    ),
    "gain0": (
        ("out", 0, 2),
        ("gate2", 2, 0),
        ("gate2", 2, 2),
        ("gate2", 2, 4),
        ("query", 0, 0),
        ("gate2", 2, 6),
        ("up2", 2, 0),
        ("out", 0, 3),
        ("gate", 3, 0),
        ("query", 0, 1),
        ("down", 2, 0),
        ("key", 0, 0),
        ("query", 0, 2),
        ("key", 0, 1),
        ("query", 1, 0),
        ("down", 2, 1),
        ("query", 0, 3),
        ("up", 3, 0),
        ("up", 3, 2),
        ("key", 0, 2),
        ("down", 3, 0),
        ("down", 2, 2),
        ("key", 0, 3),
        ("key", 1, 0),
        ("rest", 1, 0),
        ("down", 3, 1),
        ("keyb", 0, 0),
        ("query", 1, 2),
        ("out", 1, 0),
        ("up2", 2, 4),
        ("keyb", 0, 1),
        ("down", 3, 2),
        ("out", 1, 2),
        ("key", 1, 2),
        ("key", 2, 0),
        ("keyb", 0, 2),
        ("out", 2, 0),
        ("keyb", 1, 0),
        ("keyb", 0, 3),
        ("rest", 2, 0),
        ("out", 2, 2),
        ("key", 2, 2),
    ),
    "gain1": (
        ("gate2", 3, 0),
        ("gate2", 3, 2),
        ("gate2", 3, 4),
        ("gate2", 3, 6),
        ("key", 3, 0),
        ("out", 3, 0),
        ("up2", 3, 0),
        ("keyb", 2, 0),
        ("keyb", 1, 2),
        ("query", 2, 0),
        ("rest", 3, 0),
        ("query", 2, 2),
        ("out", 3, 2),
        ("up2", 3, 4),
        ("key", 3, 2),
        ("keyb", 2, 2),
        ("keyb", 3, 0),
    ),
    "last": (
        ("query", 3, 0),
        ("query", 3, 2),
        ("keyb", 3, 2),
    ),
}


def round_up(value, unit):
    return -(-value // unit) * unit


def length(name):
    return PARTS[name][2] - PARTS[name][1]


def step_span(name, level):
    return PARTS[name][4][level]


def step_layout(bits):
    places, total = {}, 0
    for name in PARTS:
        for level in range(bits):
            places[name, level] = total
            total += -(-length(name) // step_span(name, level))
    return places, total


def stage_copies(bits):
    return 1 + (1 << min(bits, 2)) - 1 + (1 << max(bits - 2, 0)) - 1


def bit_of(number, bit):
    return (number // (1 << bit)) % 2


def flip(number, bit):
    return number + (1 << bit) * (1 - 2 * bit_of(number, bit))


def dot(left, right):
    return jnp.dot(left, right, preferred_element_type=F32)


def dot_rows(left, right):
    return lax.dot_general(left, right, (((1,), (1,)), ((), ())), preferred_element_type=F32)


def dot_cols(left, right):
    return lax.dot_general(left, right, (((0,), (0,)), ((), ())), preferred_element_type=F32)


def at_chunk(index, size=CHUNK):
    return pl.ds(index * size, size)


def loop(first, last, body, **options):
    def step(at, carry):
        body(at)
        return carry

    lax.fori_loop(first, last, step, 0, **options)


def layer_kernel(sizes, in_names, out_names, scratch_names, *refs):
    micro, block, width, hidden_width, devices, groups = sizes
    r = dict(zip(in_names + out_names + scratch_names, refs))
    lower = devices // groups
    bits = groups.bit_length() - 2
    count = 1 << bits
    half = count // 2
    step_places, _ = step_layout(bits)
    orders = {name: [bit for bit in part[3] if bit <= bits] for name, part in PARTS.items()}
    rows_all = micro * block
    chunks = width // CHUNK
    full = hidden_width // CHUNK
    tail = hidden_width % CHUNK
    depth = r["ring_gate"].shape[0]
    kept = full - depth
    scale = 1.0 / math.sqrt(HEAD)

    schedule = SCHEDULE
    if bits != 4:
        schedule = {"last": [
            (name, level, first)
            for level in range(bits) for name in PARTS
            for first in range(0, length(name), step_span(name, min(level + 1, bits - 1)))
        ]}

    position = lax.axis_index("seq")
    me, rest = position // lower, position % lower
    core = me % 2
    my_unit = me // 2
    after = ((position + 1) % devices,)
    behind = ((position + devices - 1) % devices,)

    def partner(*some):
        other = me
        for bit in some:
            other = flip(other, bit)
        return (other * lower + rest,)

    stages = [[0], list(range(1, bits + 1))[:2], list(range(1, bits + 1))[2:]]
    stages = [stage for stage in stages if stage]
    peers = [
        [partner(*[bit for place, bit in enumerate(stage) if mask >> place & 1]) for mask in range(1, 1 << len(stage))]
        for stage in stages
    ]


    def local_copy(source, target, index):
        return pltpu.make_async_copy(source, target, r["local_sem"].at[index])

    def remote_copy(source, target, sems, index, device):
        send, recv = r[sems + "_send"], r[sems + "_recv"]
        return pltpu.make_async_remote_copy(
            src_ref=source, dst_ref=target, send_sem=send.at[index], recv_sem=recv.at[index],
            device_id=device, device_id_type=MESH,
        )

    load_tokens = local_copy(r["tokens"], r["x"], 0)
    load_cot = local_copy(r["cotangent"], r["col_cot"].at[0], 1)
    load_out = local_copy(r["w_out"], r["wo"], 2)
    rings = ("ring_gate", "ring_up", "ring_down")
    past = pl.ds(full * CHUNK, tail)
    load_tails = [
        local_copy(r[name].at[past, :], r["tail_" + name[2:]], 3 + index)
        for index, name in enumerate(("w_gate", "w_up", "w_down"))
    ]
    attention_weights = [
        pltpu.make_async_copy(r[name].at[at_chunk(slot), :], r[ring].at[slot], r["ring_sem"].at[index, slot])
        for index, (name, ring) in enumerate(zip(("w_query", "w_key", "w_value"), rings))
        for slot in range(depth)
    ]

    def hidden_weights(chunk, place):
        slot = place % depth
        return [
            pltpu.make_async_copy(r[name].at[at_chunk(chunk), :], r[ring].at[slot], r["ring_sem"].at[index, slot])
            for index, (name, ring) in enumerate(zip(("w_gate", "w_up", "w_down"), rings))
        ]

    def pair_copies():
        plan = {}
        for name in ROWS:
            plan[name] = (r["row_" + name].at[:, 1 - core], r["peer_" + name])
        plan["cot"] = (r["cotangent"], r["col_cot"].at[1])
        for name in ("branch", "dquery", "dkeyval", "dkvback"):
            plan[name] = (r["col_" + name].at[0], r["col_" + name].at[1])
        return {
            name: remote_copy(source, target, "pair", index, partner(0))
            for index, (name, (source, target)) in enumerate(plan.items())
        }

    pair = pair_copies()
    ready = set()

    def need(name):
        if name not in ready and name not in CHUNKED:
            ready.add(name)
            pair[name].wait_recv()

    def pair_chunk(first, last=None):
        ref = r["col_hidden"]
        some = pl.ds(first, 1 if last is None else last - first)
        return pltpu.make_async_remote_copy(
            src_ref=ref.at[0, some], dst_ref=ref.at[1, some],
            send_sem=r["chunk_send"].at[0], recv_sem=r["chunk_recv"].at[first],
            device_id=partner(0), device_id_type=MESH,
        )

    halo_out = remote_copy(r["x"], r["x_before"], "halo", 0, after)
    halo_back = remote_copy(r["back_out"], r["back_in"], "halo", 1, behind)

    load_tokens.start()
    r["x_before"][...] = jnp.zeros_like(r["x_before"])
    barrier = pltpu.get_barrier_semaphore()
    greeted = [after, behind] + [device for stage in peers for device in stage]
    for device in greeted:
        pl.semaphore_signal(barrier, inc=1, device_id=device, device_id_type=MESH)
    for copy in attention_weights:
        copy.start()
    for part in range(2):
        r["col_hidden"][0, full, part] = jnp.zeros((rows_all, CHUNK), BF16)


    def unit_at(order, slot):
        unit = my_unit
        for place, bit in enumerate(order):
            rel = (slot // (1 << (bits - 1 - place))) % 2
            unit = unit + (1 << (bit - 1)) * rel * (1 - 2 * bit_of(me, bit))
        return unit

    def factors(name, base):
        matrix = PARTS[name][0]
        units = [unit_at(orders[name], base + slot) for slot in range(half)]
        pairs = []
        for row, col in MATRICES[matrix]:
            need(row)
            need(col)
            for source in range(2):
                parts = [
                    r["row_" + row][unit, core] if source == 0 else r["peer_" + row][unit] for unit in units
                ]
                pairs.append((jnp.concatenate(parts, axis=0), col, source))
        return pairs

    def product(pairs, chunk):
        total = None
        for left, col, source in pairs:
            if col in CHUNKED:
                right = r["col_hidden"][source, chunk, CHUNKED.index(col)]
            else:
                right = r["col_" + col][source, :, at_chunk(chunk)]
            term = dot(left, right)
            total = term if total is None else total + term
        return total.reshape(half, total.shape[0] // half, CHUNK)

    def step_copy(name, level, first, last):
        size = half >> level
        some = pl.ds(first, last - first)
        if level == 0:
            source = r["send_" + name].at[some]
        else:
            source = r[f"land_{name}{level - 1}"].at[some, pl.ds(size, size)]
        place = step_places[name, level] + first // step_span(name, level)
        return pltpu.make_async_remote_copy(
            src_ref=source, dst_ref=r[f"land_{name}{level}"].at[some],
            send_sem=r["step_send"].at[INDEX[name], level], recv_sem=r["step_recv"].at[place],
            device_id=partner(orders[name][level]), device_id_type=MESH,
        )

    def send_products(name):
        pairs = factors(name, half)
        for at in range(length(name)):
            r["send_" + name][at] = product(pairs, PARTS[name][1] + at).astype(BF16)
            step_copy(name, 0, at, at + 1).start()

    def arrive(name, level, first):
        last = min(first + step_span(name, min(level + 1, bits - 1)), length(name))
        matrix, base = PARTS[name][:2]
        here = r[f"land_{name}{level}"]
        pairs = factors(name, 0) if level == 0 else None
        size = half >> level
        span = step_span(name, level)
        for at in range(first, last, span):
            step_copy(name, level, at, min(at + span, last)).wait_recv()
        for at in range(first, last):
            if level == 0:
                own = product(pairs, base + at)
            else:
                own = r[f"land_{name}{level - 1}"][at, :size].astype(F32)
            total = own + here[at].astype(F32)
            if level < bits - 1:
                here[at] = total.astype(BF16)
            elif matrix in ("gate", "up"):
                rows = total.shape[1]
                for part in range(CHUNK // 128):
                    place = ((base + at) * (CHUNK // 128) + part) * rows
                    r["turn_" + matrix][pl.ds(place, rows), :] = total[0, :, 128 * part : 128 * (part + 1)]
            else:
                r["total_" + name][at] = total[0]
        if level < bits - 1:
            step_copy(name, level + 1, first, last).start()
        else:
            unfinished[matrix] -= last - first
            if not unfinished[matrix]:
                finish(matrix)

    unfinished = {}
    for name, part in PARTS.items():
        unfinished[part[0]] = unfinished.get(part[0], 0) + length(name)

    def finish(matrix):
        if matrix in ("gate", "up"):
            flat, turn = r["flat_" + matrix], r["turn_" + matrix]
            whole = hidden_width // 128
            steps = hidden_width // 64
            rows = turn.shape[0] // (whole + 1)
            few = rows // 2
            even = [turn[pl.ds(rows * j, few, stride=2), :] for j in range(whole + 1)]
            odd = [pltpu.roll(turn[pl.ds(rows * j + 1, few, stride=2), :], 64, 1) for j in range(whole + 1)]
            low = lax.broadcasted_iota(jnp.int32, (few, 128), 1) < 64
            for j in range(whole):
                flat[pl.ds(j, few, stride=steps), :] = even[j]
                flat[pl.ds(whole + 1 + j, few, stride=steps), :] = jnp.where(low, odd[j], odd[j + 1])
            flat[pl.ds(whole, few, stride=steps), :] = jnp.where(low, even[whole], odd[0])
            return
        per_row = width // 128
        for name, part in PARTS.items():
            if part[0] != matrix:
                continue
            for at in range(length(name)):
                total = r["total_" + name][at]
                for piece in range(CHUNK // 128):
                    column = (part[1] + at) * (CHUNK // 128) + piece
                    target = "flat_value" if column >= per_row else "flat_" + matrix
                    rows = r[target].shape[0] // per_row
                    r[target][pl.ds(column % per_row, rows, stride=per_row), :] = total[:rows, 128 * piece : 128 * (piece + 1)]

    def gain_copy(stage, index):
        base = sum(len(group) + 1 for group in peers[:stage])
        return remote_copy(
            r["gain_buf"].at[base], r["gain_buf"].at[base + 1 + index], "gain", base - stage + index, peers[stage][index]
        )

    def gain_start(stage, value):
        r["gain_buf"][sum(len(group) + 1 for group in peers[:stage])] = value
        for index in range(len(peers[stage])):
            gain_copy(stage, index).start()

    def gain_step(stage):
        base = sum(len(group) + 1 for group in peers[:stage])
        total = r["gain_buf"][base]
        for index in range(len(peers[stage])):
            gain_copy(stage, index).wait_recv()
            total = total + r["gain_buf"][base + 1 + index]
        if stage + 1 < len(peers):
            gain_start(stage + 1, total)
            return
        for row, name in enumerate(("gain_attn_sum", "gain_mlp_sum")):
            for j in range(width // 128):
                r[name][j : j + 1, :] = total[row : row + 1, 128 * j : 128 * (j + 1)]

    def arrivals(point):
        for name, level, first in schedule.get(point, ()):
            arrive(name, level, first)


    def some_rows(at):
        return pl.ds(at * block, block)

    def row_scale(value):
        return lax.rsqrt(jnp.mean(value * value, axis=-1, keepdims=True) + EPSILON)

    def first_norm(source, target):
        def body(at):
            value = source[some_rows(at), :].astype(F32)
            target[some_rows(at), :] = (value * row_scale(value) * r["gain_attn"][...]).astype(BF16)

        loop(0, micro, body)

    def by_owner(name, source):
        ref = r["row_" + name]
        ref[...] = source[...].T.reshape(ref.shape)
        pair[name].start()

    def project(left, ring, target):
        target[...] = dot(left[...], r[ring][...].reshape(width, width)).astype(BF16)

    act, other = r["act"], r["other"]
    load_tokens.wait()
    pl.semaphore_wait(barrier, len(greeted))
    pl.when(position < devices - 1)(halo_out.start)
    first_norm(r["x"], act)
    load_out.start()
    load_cot.start()
    for copy in load_tails:
        copy.start()
    for index, (ring, target) in enumerate(zip(rings, ("queries", "keys", "values"))):
        for copy in attention_weights[index * depth : (index + 1) * depth]:
            copy.wait()
        project(act, ring, r[target])
    pl.when(position > 0)(halo_out.wait_recv)
    first_norm(r["x_before"], other)
    project(other, "ring_up", r["keys_before"])
    project(other, "ring_down", r["values_before"])
    for slot in range(depth):
        for copy in hidden_weights(slot, slot):
            copy.start()

    quad = CHUNK // HEAD
    start = position * block
    lane_head = lax.broadcasted_iota(jnp.int32, (block, CHUNK), 1) // HEAD
    key_at = start - WIN + lax.broadcasted_iota(jnp.int32, (2 * block, CHUNK), 0)
    query_at = start + lax.broadcasted_iota(jnp.int32, (1, CHUNK), 1) % block

    def stacked(value):
        return jnp.concatenate([jnp.where(lane_head == h, value, jnp.zeros_like(value)) for h in range(quad)], axis=0)

    def unstacked(value):
        total = jnp.zeros((block, CHUNK), F32)
        for h in range(quad):
            total = jnp.where(lane_head == h, value[h * block : (h + 1) * block], total)
        return total

    def unit(index):
        return index // chunks, some_rows(index // chunks), at_chunk(index % chunks)

    def both(before, own, rows, lanes):
        return jnp.concatenate([r[before][rows, lanes], r[own][rows, lanes]], axis=0)

    def allowed(which):
        def body(at, carry):
            end, low = carry
            end = end + r["lengths"][which, at]
            return end, jnp.where(query_at >= end, end, low)

        _, low = lax.fori_loop(
            0, r["lengths"].shape[1], body, (jnp.int32(0), jnp.zeros((1, CHUNK), jnp.int32))
        )
        low = jnp.maximum(low, query_at - (WIN - 1))
        return (key_at >= low) & (key_at <= query_at)

    def scores(which, keys, queries):
        return jnp.where(allowed(which), dot_rows(keys, queries) * scale, -1e30)

    def attend(index):
        which, rows, lanes = unit(index)
        logits = scores(which, both("keys_before", "keys", rows, lanes), stacked(r["queries"][rows, lanes]))
        peak = jnp.max(logits, axis=0, keepdims=True)
        powers = jnp.exp(logits - peak)
        total = jnp.sum(powers, axis=0, keepdims=True)
        r["log_sums"][index] = jnp.broadcast_to(peak + jnp.log(total), (8, CHUNK))
        probability = (powers / total).astype(BF16)
        mixed = dot_cols(probability, both("values_before", "values", rows, lanes))
        act[rows, lanes] = unstacked(mixed).astype(BF16)

    pair["cot"].start()
    loop(0, micro * chunks, attend, unroll=2)
    load_out.wait()
    middle = r["input_grad"]

    middle[...] = r["x"][...].astype(F32) + dot(act[...], r["wo"][...])

    def second_norm(at):
        value = middle[some_rows(at), :]
        other[some_rows(at), :] = (value * row_scale(value) * r["gain_mlp"][...]).astype(BF16)

    loop(0, micro, second_norm)
    by_owner("second", other)


    def hidden_part(gate, up, grad_hidden):
        sigmoid = jax.nn.sigmoid(gate)
        silu = gate * sigmoid
        hidden = (silu * up).astype(BF16)
        dgate = (grad_hidden * up * sigmoid * (1.0 + gate * (1.0 - sigmoid))).astype(BF16)
        return hidden, dgate, (grad_hidden * silu).astype(BF16)

    columns = r["columns"]

    def hidden_chunk(at, prefetch):
        slot = at % depth
        for copy in hidden_weights(at, at):
            copy.wait()
        wait_chunk(at - LAG)
        hidden, dgate, dup = hidden_part(
            dot_rows(other[...], r["ring_gate"][slot]),
            dot_rows(other[...], r["ring_up"][slot]),
            dot_rows(r["col_cot"][0], r["ring_down"][slot]),
        )
        lanes = at_chunk(at)
        form_chunk(at - LAG)
        r["hidden"][:, lanes] = hidden
        r["col_hidden"][0, at, 0] = dgate
        r["col_hidden"][0, at, 1] = dup
        columns[lanes, :] = hidden.astype(F32).T
        pair_chunk(at).start()
        send_chunk(at - LAG)
        if prefetch:
            for copy in hidden_weights(at + depth, at + depth):
                copy.start()

    early_factors = {}

    def early(at):
        return [
            (name, at - part[1]) for name, part in PARTS.items() if part[0] in ("gate", "up") and part[1] <= at < part[2]
        ]

    def wait_chunk(at):
        if at >= 0:
            pair_chunk(at).wait_recv()

    def form_chunk(at):
        for name, place in early(at):
            if name not in early_factors:
                early_factors[name] = factors(name, half)
            r["send_" + name][place] = product(early_factors[name], at).astype(BF16)

    def send_chunk(at):
        for name, place in early(at):
            step_copy(name, 0, place, place + 1).start()

    load_cot.wait()
    for copy in load_tails:
        copy.wait()
    for at in range(full):
        hidden_chunk(at, at < kept)
    hidden, dgate, dup = hidden_part(
        dot_rows(other[...], r["tail_gate"][...]),
        dot_rows(other[...], r["tail_up"][...]),
        dot_rows(r["col_cot"][0], r["tail_down"][...]),
    )
    r["hidden"][:, past] = hidden
    r["col_hidden"][0, full, 0, :, :tail] = dgate
    r["col_hidden"][0, full, 1, :, :tail] = dup
    pair_chunk(full).start()
    r["square"][...] = jnp.zeros_like(r["square"])
    r["square"][:, :tail] = hidden.astype(F32)
    columns[pl.ds(full * CHUNK, CHUNK), :] = r["square"][...].T
    own_rows = hidden_width // groups
    held_rows = r["row_hidden"].shape[2]
    for owner in range(groups):
        r["row_hidden"][owner // 2, owner % 2] = columns[pl.ds(owner * own_rows, held_rows), :].astype(BF16)
    pair["hidden"].start()
    for at in range(full - LAG, full + 1):
        wait_chunk(at)
        form_chunk(at)
        send_chunk(at)
    for name, part in PARTS.items():
        if part[0] == "down":
            send_products(name)


    sums = [pl.ds(n * CHUNK, CHUNK) for n in range(2 * chunks)]

    def fold(*pieces):
        back, onward = None, None
        for hidden, dgate, dup, gate_ref, up_ref, down_ref in pieces:
            one = dot(dgate, gate_ref[...]) + dot(dup, up_ref[...])
            two = dot(hidden, down_ref[...])
            back, onward = (one, two) if back is None else (back + one, onward + two)
        for n in range(chunks):
            columns[sums[n], :] += back[:, n * CHUNK : (n + 1) * CHUNK]
            columns[sums[chunks + n], :] += onward[:, n * CHUNK : (n + 1) * CHUNK]

    def fold_chunks(places):
        pieces = []
        for at in places:
            chunk = at - depth if at < full + depth else at - depth - full
            if at >= full + depth:
                for copy in hidden_weights(chunk, at):
                    copy.wait()
            pieces.append((
                r["hidden"][:, at_chunk(chunk)], r["col_hidden"][0, chunk, 0], r["col_hidden"][0, chunk, 1],
                *(r[ring].at[at % depth] for ring in rings),
            ))
        fold(*pieces)
        for at in places:
            if at < full + kept:
                for copy in hidden_weights(at - full, at + depth):
                    copy.start()

    for some in sums:
        columns[some, :] = jnp.zeros((CHUNK, CHUNK), F32)
    fold((
        r["hidden"][:, past], r["col_hidden"][0, full, 0, :, :tail], r["col_hidden"][0, full, 1, :, :tail],
        r["tail_gate"], r["tail_up"], r["tail_down"],
    ))
    for at in range(full, 2 * full, 2):
        fold_chunks(range(at, min(at + 2, 2 * full)))
    for copy in attention_weights:
        copy.start()

    def summed(at, base):
        return jnp.concatenate(
            [columns[pl.ds((base + n) * CHUNK + at * block, block), :] for n in range(chunks)],
            axis=1,
        )

    def norm_backward(grad, value, gain):
        inverse = row_scale(value)
        normed = value * inverse
        scaled = grad * gain
        mean = jnp.mean(scaled * normed, axis=-1, keepdims=True)
        return inverse * (scaled - normed * mean), jnp.sum(grad * normed, axis=0, keepdims=True)

    def middle_backward(at, gain_sum):
        rows = some_rows(at)
        value = middle[rows, :]
        r["output"][rows, :] = (value + summed(at, chunks)).astype(BF16)
        grad, part = norm_backward(summed(at, 0), value, r["gain_mlp"][...])
        grad = grad + r["col_cot"][0, rows, :].astype(F32)
        middle[rows, :] = grad
        r["col_branch"][0, rows, :] = grad.astype(BF16)
        return gain_sum + part

    gain_mlp_sum = lax.fori_loop(0, micro, middle_backward, jnp.zeros((1, width), F32))
    pair["branch"].start()
    by_owner("attended", act)
    for name, source in (("first", "x"), ("before", "x_before")):
        first_norm(r[source], r["back_out"])
        by_owner(name, r["back_out"])

    r["grad_attended"][...] = dot_rows(r["col_branch"][0], r["wo"][...]).astype(BF16)


    def attend_backward(index):
        which, rows, lanes = unit(index)
        keys = both("keys_before", "keys", rows, lanes)
        values = both("values_before", "values", rows, lanes)
        queries = stacked(r["queries"][rows, lanes])
        grads = stacked(r["grad_attended"][rows, lanes])
        probability = jnp.exp(scores(which, keys, queries) - r["log_sums"][index][:1])
        grad_prob = dot_rows(values, grads)
        delta = jnp.sum(probability * grad_prob, axis=0, keepdims=True)
        grad_scores = (scale * probability * (grad_prob - delta)).astype(BF16)
        r["col_dquery"][0, rows, lanes] = unstacked(dot_cols(grad_scores, keys)).astype(BF16)
        dkey = dot(grad_scores, queries).astype(BF16)
        dvalue = dot(probability.astype(BF16), grads).astype(BF16)
        lanes_value = at_chunk(chunks + index % chunks)
        r["col_dkvback"][0, rows, lanes] = dkey[:block]
        r["col_dkvback"][0, rows, lanes_value] = dvalue[:block]
        r["col_dkeyval"][0, rows, lanes] = dkey[block:]
        r["col_dkeyval"][0, rows, lanes_value] = dvalue[block:]

    arrivals("middle")
    for at in range(micro):
        loop(at * chunks, (at + 1) * chunks, attend_backward, unroll=2)
        arrivals("attend" + str(at))
    for name in ("dquery", "dkeyval", "dkvback"):
        pair[name].start()
    def through_keys(ref, at):
        return dot_rows(ref[0, :, :width], r["ring_up"][at]) + dot_rows(ref[0, :, width:], r["ring_down"][at])

    def back_chunk(at):
        r["back_out"][:, at_chunk(at)] = through_keys(r["col_dkvback"], at).astype(BF16)

    def first_chunk(at):
        columns[at_chunk(at), :] = through_keys(r["col_dkeyval"], at) + dot_rows(
            r["col_dquery"][0], r["ring_gate"][at]
        )

    for copy in attention_weights:
        copy.wait()
    loop(0, chunks, back_chunk)
    pl.when(position > 0)(halo_back.start)
    arrivals("back")
    send_products("out")
    arrivals("out")

    def gain_parts(at, gain_sum):
        rows = some_rows(at)
        for grad, name in ((summed(at, 0), "x"), (r["back_out"][rows, :].astype(F32), "x_before")):
            value = r[name][rows, :].astype(F32)
            gain_sum = gain_sum + jnp.sum(grad * (value * row_scale(value)), axis=0, keepdims=True)
        return gain_sum

    for name in ("query", "key", "keyb"):
        send_products(name)
        arrivals(name)
    loop(0, chunks, first_chunk)
    gain_attn_sum = lax.fori_loop(0, micro, gain_parts, jnp.zeros((1, width), F32))
    gain_start(0, jnp.concatenate([gain_attn_sum, gain_mlp_sum, jnp.zeros((6, width), F32)], axis=0))
    arrivals("first")

    def input_backward(at):
        rows = some_rows(at)
        back = jnp.where(position < devices - 1, r["back_in"][rows, :].astype(F32), 0.0)
        grad, _ = norm_backward(summed(at, 0) + back, r["x"][rows, :].astype(F32), r["gain_attn"][...])
        middle[rows, :] = middle[rows, :] + grad

    for stage in range(len(peers)):
        gain_step(stage)
        arrivals("gain" + str(stage))
    pl.when(position < devices - 1)(halo_back.wait_recv)
    loop(0, micro, input_backward)
    arrivals("last")

    pl.when(position < devices - 1)(halo_out.wait_send)
    pl.when(position > 0)(halo_back.wait_send)
    for copy in pair.values():
        copy.wait_send()
    for stage, group in enumerate(peers):
        for index in range(len(group)):
            gain_copy(stage, index).wait_send()
    pair_chunk(0, full + 1).wait_send()
    for name in PARTS:
        for level in range(bits):
            step_copy(name, level, 0, length(name)).wait_send()


def layer(tokens, gain_attn, gain_mlp, weights, cotangent, lengths, micro, devices, groups):
    rows_all, width = tokens.shape
    hidden_width = weights["w_gate"].shape[0]
    block = rows_all // micro
    bits = groups.bit_length() - 2
    count = 1 << bits
    half = count // 2
    chunks = width // CHUNK
    padded = round_up(hidden_width, CHUNK)
    tail = hidden_width % CHUNK
    depth = chunks
    unit_rows = {name: width // groups for name in ROWS}
    unit_rows["hidden"] = round_up(hidden_width // groups, 16)
    widths = {name: width for name in COLS}
    widths.update(dkeyval=2 * width, dkvback=2 * width)

    inputs = {"tokens": tokens, "cotangent": cotangent, **weights}
    any_spec = pl.BlockSpec(memory_space=pl.ANY)
    vmem_spec = pl.BlockSpec(memory_space=pltpu.VMEM)
    in_specs = [any_spec] * len(inputs) + [vmem_spec] * 2 + [pl.BlockSpec(memory_space=pltpu.SMEM)]
    inputs.update(gain_attn=gain_attn[None], gain_mlp=gain_mlp[None], lengths=lengths)

    outs = {
        "output": ((rows_all, width), BF16),
        "input_grad": ((rows_all, width), F32),
        "gain_attn_sum": ((width // 128, 128), F32),
        "gain_mlp_sum": ((width // 128, 128), F32),
    }
    own = {"query": width * width, "keyval": width * width, "value": width * width, "out": width * width}
    own.update(gate=width * hidden_width, up=width * hidden_width, down=width * hidden_width)
    for name, size in own.items():
        outs["flat_" + name] = ((size // groups // 128, 128), F32)

    scratch = {
        "x": pltpu.VMEM((rows_all, width), BF16),
        "x_before": pltpu.VMEM((rows_all, width), BF16),
        "act": pltpu.VMEM((rows_all, width), BF16),
        "other": pltpu.VMEM((rows_all, width), BF16),
        "queries": pltpu.VMEM((rows_all, width), BF16),
        "keys": pltpu.VMEM((rows_all, width), BF16),
        "values": pltpu.VMEM((rows_all, width), BF16),
        "keys_before": pltpu.VMEM((rows_all, width), BF16),
        "values_before": pltpu.VMEM((rows_all, width), BF16),
        "grad_attended": pltpu.VMEM((rows_all, width), BF16),
        "back_out": pltpu.VMEM((rows_all, width), BF16),
        "back_in": pltpu.VMEM((rows_all, width), BF16),
        "log_sums": pltpu.VMEM((micro * chunks, 8, CHUNK), F32),
        "wo": pltpu.VMEM((width, width), BF16),
        "ring_gate": pltpu.VMEM((depth, CHUNK, width), BF16),
        "ring_up": pltpu.VMEM((depth, CHUNK, width), BF16),
        "ring_down": pltpu.VMEM((depth, CHUNK, width), BF16),
        "tail_gate": pltpu.VMEM((tail, width), BF16),
        "tail_up": pltpu.VMEM((tail, width), BF16),
        "tail_down": pltpu.VMEM((tail, width), BF16),
        "hidden": pltpu.VMEM((rows_all, padded), BF16),
        "columns": pltpu.VMEM((padded, rows_all), F32),
        "square": pltpu.VMEM((rows_all, CHUNK), F32),
        "gain_buf": pltpu.VMEM((stage_copies(bits) + 3, 8, width), F32),
    }
    for name in ROWS:
        scratch["row_" + name] = pltpu.VMEM((count, 2, unit_rows[name], rows_all), BF16)
        scratch["peer_" + name] = pltpu.VMEM((count, unit_rows[name], rows_all), BF16)
    for name in COLS:
        if name not in CHUNKED:
            scratch["col_" + name] = pltpu.VMEM((2, rows_all, widths[name]), BF16)
    scratch["col_hidden"] = pltpu.VMEM((2, padded // CHUNK, len(CHUNKED), rows_all, CHUNK), BF16)
    for name, (matrix, first, last, _, _) in PARTS.items():
        rows = unit_rows[MATRICES[matrix][0][0]]
        scratch["send_" + name] = pltpu.VMEM((last - first, half, rows, CHUNK), BF16)
        for level in range(bits):
            scratch[f"land_{name}{level}"] = pltpu.VMEM((last - first, half >> level, rows, CHUNK), BF16)
        if matrix in ("gate", "up"):
            scratch["turn_" + matrix] = pltpu.VMEM((padded // 128 * rows, 128), F32)
        else:
            scratch["total_" + name] = pltpu.VMEM((last - first, rows, CHUNK), F32)
    sems = {"local_sem": (6,), "ring_sem": (3, depth)}
    sems.update(chunk_send=(1,), chunk_recv=(padded // CHUNK,))
    sems.update(step_send=(len(PARTS), bits), step_recv=(step_layout(bits)[1],))
    for name, number in (("pair", len(ROWS) + len(COLS) - len(CHUNKED)), ("halo", 2), ("gain", stage_copies(bits))):
        sems[name + "_send"] = sems[name + "_recv"] = (number,)
    for name, shape in sems.items():
        scratch[name] = pltpu.SemaphoreType.DMA(shape)

    sizes = (micro, block, width, hidden_width, devices, groups)
    results = pl.pallas_call(
        functools.partial(layer_kernel, sizes, tuple(inputs), tuple(outs), tuple(scratch)),
        out_shape=[jax.ShapeDtypeStruct(*spec) for spec in outs.values()],
        in_specs=in_specs,
        out_specs=[vmem_spec] * len(outs),
        scratch_shapes=list(scratch.values()),
        compiler_params=pltpu.CompilerParams(
            collective_id=0, has_side_effects=True, vmem_limit_bytes=63 * 2**20
        ),
        name="layer",
    )(*inputs.values())
    return dict(zip(outs, handed_on(results)))


def hand_on_kernel(count, *refs):
    sources, targets, passing = (refs[part * count : (part + 1) * count] for part in range(3))
    sems = refs[-1]
    arriving = [
        pltpu.make_async_copy(source, middle, sems.at[0, index])
        for index, (source, middle) in enumerate(zip(sources, passing))
    ]
    leaving = [
        pltpu.make_async_copy(middle, target, sems.at[1, index])
        for index, (middle, target) in enumerate(zip(passing, targets))
    ]
    for copy in arriving:
        copy.start()
    for before, copy in zip(arriving, leaving):
        before.wait()
        copy.start()
    for copy in leaving:
        copy.wait()


def handed_on(arrays):
    any_spec = pl.BlockSpec(memory_space=pl.ANY)
    count = len(arrays)
    return pl.pallas_call(
        functools.partial(hand_on_kernel, count),
        out_shape=[jax.ShapeDtypeStruct(array.shape, array.dtype) for array in arrays],
        in_specs=[any_spec] * count,
        out_specs=[any_spec] * count,
        scratch_shapes=[pltpu.VMEM(array.shape, array.dtype) for array in arrays]
        + [pltpu.SemaphoreType.DMA((2, count))],
        name="hand_on",
    )(*arrays)


def per_device(
    tokens, gain_attn, gain_mlp, w_query, w_key, w_value, w_out, w_gate, w_up, w_down, cotangent, lengths
):
    devices = lax.axis_size("seq")
    groups = min(devices, MOST_GROUPS)
    lower = devices // groups
    micro, block, width = tokens.shape
    weights = dict(
        w_query=w_query, w_key=w_key, w_value=w_value, w_out=w_out, w_gate=w_gate.T, w_up=w_up.T, w_down=w_down
    )
    result = layer(
        tokens.reshape(micro * block, width), gain_attn, gain_mlp, weights,
        cotangent.reshape(micro * block, width), lengths, micro, devices, groups,
    )
    near = [[high * lower + low for low in range(lower)] for high in range(groups)]

    def slice_of(name):
        flat = result["flat_" + name].reshape(-1)
        if lower == 1:
            return flat
        return lax.psum_scatter(flat, "seq", axis_index_groups=near, tiled=True)

    gain_sums = [result["gain_attn_sum"].reshape(-1), result["gain_mlp_sum"].reshape(-1)]
    if lower > 1:
        gain_sums = lax.psum(gain_sums, "seq", axis_index_groups=near)
    return (
        result["output"].reshape(tokens.shape),
        result["input_grad"].reshape(tokens.shape),
        gain_sums[0],
        gain_sums[1],
        slice_of("query"),
        slice_of("keyval"),
        slice_of("value"),
        slice_of("out"),
        slice_of("gate"),
        slice_of("up"),
        slice_of("down"),
    )


def solution(mesh):
    tokens_spec = P(None, "seq", None)
    return jax.shard_map(
        per_device,
        mesh=mesh,
        in_specs=(tokens_spec,) + (P(),) * 9 + (tokens_spec, P()),
        out_specs=(tokens_spec, tokens_spec, P(), P()) + (P("seq"),) * 7,
        check_vma=False,
    )
```

```python
import functools
import math

import jax
import jax.numpy as jnp
from jax import lax
from jax.experimental import pallas as pl
from jax.experimental.pallas import tpu as pltpu
from jax.sharding import PartitionSpec as P

HEAD = 64
WIN = 64
EPSILON = 1e-05
MESH = pl.DeviceIdType.MESH
MOST_GROUPS = 32
CHUNK = 256
BF16 = jnp.bfloat16
F32 = jnp.float32

MATRICES = {
    "down": (("hidden", "cot"),),
    "gate": (("second", "dgate"),),
    "up": (("second", "dup"),),
    "query": (("first", "dquery"),),
    "keyval": (("first", "dkeyval"), ("before", "dkvback")),
    "out": (("attended", "branch"),),
}
ROWS = ("first", "before", "attended", "second", "hidden")
CHUNKED = ("dgate", "dup")
COLS = ("cot", "dgate", "dup", "branch", "dquery", "dkeyval", "dkvback")
PARTS = {
    "gate": ("gate", 0, 4, (2, 1, 4, 3), (1, 2, 4, 4)),
    "gate2": ("gate", 4, 11, (3, 1, 4, 2), (1, 1, 2, 2)),
    "up": ("up", 0, 3, (3, 4, 2, 1), (1, 1, 2, 2)),
    "up2": ("up", 3, 11, (1, 3, 4, 2), (1, 2, 4, 4)),
    "down": ("down", 0, 3, (2, 1, 4, 3), (1, 1, 1, 1)),
    "rest": ("down", 3, 4, (2, 1, 4, 3), (1, 1, 1, 1)),
    "out": ("out", 0, 4, (2, 1, 3, 4), (1, 1, 2, 2)),
    "query": ("query", 0, 4, (1, 3, 2, 4), (1, 1, 2, 2)),
    "key": ("keyval", 0, 4, (2, 3, 1, 4), (1, 1, 2, 2)),
    "keyb": ("keyval", 4, 8, (2, 1, 3, 4), (1, 1, 2, 2)),
}
INDEX = {name: index for index, name in enumerate(PARTS)}
LAG = 2


SCHEDULE = {
    "middle": (
        ("gate", 0, 0),
        ("up", 0, 0),
        ("gate", 0, 2),
    ),
    "attend0": (
        ("up", 0, 1),
        ("up", 0, 2),
        ("gate2", 0, 0),
        ("up2", 0, 0),
        ("gate2", 0, 1),
    ),
    "attend1": (
        ("gate2", 0, 2),
        ("up2", 0, 2),
        ("gate2", 0, 3),
        ("gate2", 0, 4),
    ),
    "attend2": (
        ("gate", 1, 0),
        ("gate2", 0, 5),
        ("gate2", 0, 6),
    ),
    "attend3": (
        ("gate2", 1, 0),
        ("down", 0, 0),
        ("up2", 0, 4),
    ),
    "back": (
        ("gate2", 1, 2),
    ),
    "out": (
        ("up2", 1, 0),
    ),
    "first": (
        ("down", 0, 1),
        ("down", 0, 2),
        ("rest", 0, 0),
        ("query", 0, 0),
    ),
    "query": (
        ("gate2", 1, 4),
        ("gate2", 1, 6),
        ("gate", 2, 0),
    ),
    "key": (
        ("down", 1, 0),
    ),
    "keyb": (
        ("up2", 0, 6),
    ),
    "gain0": (
        ("out", 0, 0),
        ("gate2", 2, 0),
        ("gate2", 2, 2),
        ("up2", 2, 0),
        ("query", 0, 1),
        ("up", 1, 0),
        ("out", 0, 1),
        ("up2", 1, 4),
        ("gate2", 2, 4),
        ("up", 1, 2),
        ("gate", 3, 0),
        ("query", 0, 2),
        ("gate2", 2, 6),
        ("out", 0, 2),
        ("query", 1, 0),
        ("query", 0, 3),
        ("out", 0, 3),
        ("down", 2, 0),
        ("key", 0, 0),
        ("down", 1, 1),
        ("query", 1, 2),
        ("down", 3, 0),
        ("key", 0, 1),
        ("up2", 2, 4),
        ("down", 1, 2),
        ("key", 0, 2),
        ("key", 1, 0),
        ("key", 0, 3),
        ("down", 2, 1),
        ("rest", 1, 0),
        ("keyb", 0, 0),
        ("out", 1, 0),
        ("down", 2, 2),
        ("key", 1, 2),
        ("down", 3, 1),
        ("keyb", 0, 1),
        ("out", 1, 2),
        ("key", 2, 0),
        ("keyb", 0, 2),
        ("out", 2, 0),
        ("rest", 2, 0),
        ("down", 3, 2),
        ("key", 2, 2),
        ("keyb", 0, 3),
        ("out", 2, 2),
        ("keyb", 1, 0),
        ("gate2", 3, 0),
        ("gate2", 3, 2),
    ),
    "gain1": (
        ("up", 2, 0),
        ("keyb", 2, 0),
        ("up", 2, 2),
        ("keyb", 1, 2),
        ("query", 2, 0),
        ("gate2", 3, 4),
        ("gate2", 3, 6),
        ("up2", 3, 0),
        ("query", 2, 2),
        ("rest", 3, 0),
        ("out", 3, 0),
        ("up", 3, 0),
        ("up2", 3, 4),
        ("up", 3, 2),
        ("out", 3, 2),
        ("key", 3, 0),
    ),
    "last": (
        ("keyb", 2, 2),
        ("query", 3, 0),
        ("query", 3, 2),
        ("key", 3, 2),
        ("keyb", 3, 0),
        ("keyb", 3, 2),
    ),
}


def round_up(value, unit):
    return -(-value // unit) * unit


def length(name):
    return PARTS[name][2] - PARTS[name][1]


def step_span(name, level):
    return PARTS[name][4][level]


def step_layout(bits):
    places, total = {}, 0
    for name in PARTS:
        for level in range(bits):
            places[name, level] = total
            total += -(-length(name) // step_span(name, level))
    return places, total


def stage_copies(bits):
    return 1 + (1 << min(bits, 2)) - 1 + (1 << max(bits - 2, 0)) - 1


def bit_of(number, bit):
    return (number // (1 << bit)) % 2


def flip(number, bit):
    return number + (1 << bit) * (1 - 2 * bit_of(number, bit))


def dot(left, right):
    return jnp.dot(left, right, preferred_element_type=F32)


def dot_rows(left, right):
    return lax.dot_general(left, right, (((1,), (1,)), ((), ())), preferred_element_type=F32)


def dot_cols(left, right):
    return lax.dot_general(left, right, (((0,), (0,)), ((), ())), preferred_element_type=F32)


def at_chunk(index, size=CHUNK):
    return pl.ds(index * size, size)


def loop(first, last, body, **options):
    def step(at, carry):
        body(at)
        return carry

    lax.fori_loop(first, last, step, 0, **options)


def layer_kernel(sizes, in_names, out_names, scratch_names, *refs):
    micro, block, width, hidden_width, devices, groups = sizes
    r = dict(zip(in_names + out_names + scratch_names, refs))
    lower = devices // groups
    bits = groups.bit_length() - 2
    count = 1 << bits
    half = count // 2
    step_places, _ = step_layout(bits)
    orders = {name: [bit for bit in part[3] if bit <= bits] for name, part in PARTS.items()}
    rows_all = micro * block
    chunks = width // CHUNK
    full = hidden_width // CHUNK
    tail = hidden_width % CHUNK
    depth = r["ring_gate"].shape[0]
    kept = full - depth
    scale = 1.0 / math.sqrt(HEAD)

    schedule = SCHEDULE
    if bits != 4:
        schedule = {"last": [
            (name, level, first)
            for level in range(bits) for name in PARTS
            for first in range(0, length(name), step_span(name, min(level + 1, bits - 1)))
        ]}

    position = lax.axis_index("seq")
    me, rest = position // lower, position % lower
    core = me % 2
    my_unit = me // 2
    after = ((position + 1) % devices,)
    behind = ((position + devices - 1) % devices,)

    def partner(*some):
        other = me
        for bit in some:
            other = flip(other, bit)
        return (other * lower + rest,)

    stages = [[0], list(range(1, bits + 1))[:2], list(range(1, bits + 1))[2:]]
    stages = [stage for stage in stages if stage]
    peers = [
        [partner(*[bit for place, bit in enumerate(stage) if mask >> place & 1]) for mask in range(1, 1 << len(stage))]
        for stage in stages
    ]


    def local_copy(source, target, index):
        return pltpu.make_async_copy(source, target, r["local_sem"].at[index])

    def remote_copy(source, target, sems, index, device):
        send, recv = r[sems + "_send"], r[sems + "_recv"]
        return pltpu.make_async_remote_copy(
            src_ref=source, dst_ref=target, send_sem=send.at[index], recv_sem=recv.at[index],
            device_id=device, device_id_type=MESH,
        )

    load_tokens = local_copy(r["tokens"], r["x"], 0)
    load_cot = local_copy(r["cotangent"], r["col_cot"].at[0], 1)
    load_out = local_copy(r["w_out"], r["wo"], 2)
    rings = ("ring_gate", "ring_up", "ring_down")
    past = pl.ds(full * CHUNK, tail)
    load_tails = [
        local_copy(r[name].at[past, :], r["tail_" + name[2:]], 3 + index)
        for index, name in enumerate(("w_gate", "w_up", "w_down"))
    ]
    attention_weights = [
        pltpu.make_async_copy(r[name].at[at_chunk(slot), :], r[ring].at[slot], r["ring_sem"].at[index, slot])
        for index, (name, ring) in enumerate(zip(("w_query", "w_key", "w_value"), rings))
        for slot in range(depth)
    ]

    def hidden_weights(chunk, place):
        slot = place % depth
        return [
            pltpu.make_async_copy(r[name].at[at_chunk(chunk), :], r[ring].at[slot], r["ring_sem"].at[index, slot])
            for index, (name, ring) in enumerate(zip(("w_gate", "w_up", "w_down"), rings))
        ]

    def pair_copies():
        plan = {}
        for name in ROWS:
            plan[name] = (r["row_" + name].at[:, 1 - core], r["peer_" + name])
        plan["cot"] = (r["cotangent"], r["col_cot"].at[1])
        for name in ("branch", "dquery", "dkeyval", "dkvback"):
            plan[name] = (r["col_" + name].at[0], r["col_" + name].at[1])
        return {
            name: remote_copy(source, target, "pair", index, partner(0))
            for index, (name, (source, target)) in enumerate(plan.items())
        }

    pair = pair_copies()
    ready = set()

    def need(name):
        if name not in ready and name not in CHUNKED:
            ready.add(name)
            pair[name].wait_recv()

    def pair_chunk(first, last=None):
        ref = r["col_hidden"]
        some = pl.ds(first, 1 if last is None else last - first)
        return pltpu.make_async_remote_copy(
            src_ref=ref.at[0, some], dst_ref=ref.at[1, some],
            send_sem=r["chunk_send"].at[0], recv_sem=r["chunk_recv"].at[first],
            device_id=partner(0), device_id_type=MESH,
        )

    halo_out = remote_copy(r["x"], r["x_before"], "halo", 0, after)
    halo_back = remote_copy(r["back_out"], r["back_in"], "halo", 1, behind)

    load_tokens.start()
    r["x_before"][...] = jnp.zeros_like(r["x_before"])
    barrier = pltpu.get_barrier_semaphore()
    greeted = [after, behind] + [device for stage in peers for device in stage]
    for device in greeted:
        pl.semaphore_signal(barrier, inc=1, device_id=device, device_id_type=MESH)
    for copy in attention_weights:
        copy.start()
    for part in range(2):
        r["col_hidden"][0, full, part] = jnp.zeros((rows_all, CHUNK), BF16)


    def unit_at(order, slot):
        unit = my_unit
        for place, bit in enumerate(order):
            rel = (slot // (1 << (bits - 1 - place))) % 2
            unit = unit + (1 << (bit - 1)) * rel * (1 - 2 * bit_of(me, bit))
        return unit

    def factors(name, base):
        matrix = PARTS[name][0]
        units = [unit_at(orders[name], base + slot) for slot in range(half)]
        pairs = []
        for row, col in MATRICES[matrix]:
            need(row)
            need(col)
            for source in range(2):
                parts = [
                    r["row_" + row][unit, core] if source == 0 else r["peer_" + row][unit] for unit in units
                ]
                pairs.append((jnp.concatenate(parts, axis=0), col, source))
        return pairs

    def product(pairs, chunk):
        total = None
        for left, col, source in pairs:
            if col in CHUNKED:
                right = r["col_hidden"][source, chunk, CHUNKED.index(col)]
            else:
                right = r["col_" + col][source, :, at_chunk(chunk)]
            term = dot(left, right)
            total = term if total is None else total + term
        return total.reshape(half, total.shape[0] // half, CHUNK)

    def step_copy(name, level, first, last):
        size = half >> level
        some = pl.ds(first, last - first)
        if level == 0:
            source = r["send_" + name].at[some]
        else:
            source = r[f"land_{name}{level - 1}"].at[some, pl.ds(size, size)]
        place = step_places[name, level] + first // step_span(name, level)
        return pltpu.make_async_remote_copy(
            src_ref=source, dst_ref=r[f"land_{name}{level}"].at[some],
            send_sem=r["step_send"].at[INDEX[name], level], recv_sem=r["step_recv"].at[place],
            device_id=partner(orders[name][level]), device_id_type=MESH,
        )

    def send_products(name):
        pairs = factors(name, half)
        for at in range(length(name)):
            r["send_" + name][at] = product(pairs, PARTS[name][1] + at).astype(BF16)
            step_copy(name, 0, at, at + 1).start()

    def arrive(name, level, first):
        last = min(first + step_span(name, min(level + 1, bits - 1)), length(name))
        matrix, base = PARTS[name][:2]
        here = r[f"land_{name}{level}"]
        pairs = factors(name, 0) if level == 0 else None
        size = half >> level
        span = step_span(name, level)
        for at in range(first, last, span):
            step_copy(name, level, at, min(at + span, last)).wait_recv()
        for at in range(first, last):
            if level == 0:
                own = product(pairs, base + at)
            else:
                own = r[f"land_{name}{level - 1}"][at, :size].astype(F32)
            total = own + here[at].astype(F32)
            if level < bits - 1:
                here[at] = total.astype(BF16)
            elif matrix in ("gate", "up"):
                rows = total.shape[1]
                for part in range(CHUNK // 128):
                    place = ((base + at) * (CHUNK // 128) + part) * rows
                    r["turn_" + matrix][pl.ds(place, rows), :] = total[0, :, 128 * part : 128 * (part + 1)]
            else:
                r["total_" + name][at] = total[0]
        if level < bits - 1:
            step_copy(name, level + 1, first, last).start()
        else:
            unfinished[matrix] -= last - first
            if not unfinished[matrix]:
                finish(matrix)

    unfinished = {}
    for name, part in PARTS.items():
        unfinished[part[0]] = unfinished.get(part[0], 0) + length(name)

    def finish(matrix):
        if matrix in ("gate", "up"):
            flat, turn = r["flat_" + matrix], r["turn_" + matrix]
            whole = hidden_width // 128
            steps = hidden_width // 64
            rows = turn.shape[0] // (whole + 1)
            few = rows // 2
            even = [turn[pl.ds(rows * j, few, stride=2), :] for j in range(whole + 1)]
            odd = [pltpu.roll(turn[pl.ds(rows * j + 1, few, stride=2), :], 64, 1) for j in range(whole + 1)]
            low = lax.broadcasted_iota(jnp.int32, (few, 128), 1) < 64
            for j in range(whole):
                flat[pl.ds(j, few, stride=steps), :] = even[j]
                flat[pl.ds(whole + 1 + j, few, stride=steps), :] = jnp.where(low, odd[j], odd[j + 1])
            flat[pl.ds(whole, few, stride=steps), :] = jnp.where(low, even[whole], odd[0])
            return
        per_row = width // 128
        for name, part in PARTS.items():
            if part[0] != matrix:
                continue
            for at in range(length(name)):
                total = r["total_" + name][at]
                for piece in range(CHUNK // 128):
                    column = (part[1] + at) * (CHUNK // 128) + piece
                    target = "flat_value" if column >= per_row else "flat_" + matrix
                    rows = r[target].shape[0] // per_row
                    r[target][pl.ds(column % per_row, rows, stride=per_row), :] = total[:rows, 128 * piece : 128 * (piece + 1)]

    def gain_copy(stage, index):
        base = sum(len(group) + 1 for group in peers[:stage])
        return remote_copy(
            r["gain_buf"].at[base], r["gain_buf"].at[base + 1 + index], "gain", base - stage + index, peers[stage][index]
        )

    def gain_start(stage, value):
        r["gain_buf"][sum(len(group) + 1 for group in peers[:stage])] = value
        for index in range(len(peers[stage])):
            gain_copy(stage, index).start()

    def gain_step(stage):
        base = sum(len(group) + 1 for group in peers[:stage])
        total = r["gain_buf"][base]
        for index in range(len(peers[stage])):
            gain_copy(stage, index).wait_recv()
            total = total + r["gain_buf"][base + 1 + index]
        if stage + 1 < len(peers):
            gain_start(stage + 1, total)
            return
        for row, name in enumerate(("gain_attn_sum", "gain_mlp_sum")):
            for j in range(width // 128):
                r[name][j : j + 1, :] = total[row : row + 1, 128 * j : 128 * (j + 1)]

    def arrivals(point):
        for name, level, first in schedule.get(point, ()):
            arrive(name, level, first)


    def some_rows(at):
        return pl.ds(at * block, block)

    def row_scale(value):
        return lax.rsqrt(jnp.mean(value * value, axis=-1, keepdims=True) + EPSILON)

    def first_norm(source, target):
        def body(at):
            value = source[some_rows(at), :].astype(F32)
            target[some_rows(at), :] = (value * row_scale(value) * r["gain_attn"][...]).astype(BF16)

        loop(0, micro, body)

    def by_owner(name, source):
        ref = r["row_" + name]
        ref[...] = source[...].T.reshape(ref.shape)
        pair[name].start()

    def project(left, ring, target):
        target[...] = dot(left[...], r[ring][...].reshape(width, width)).astype(BF16)

    act, other = r["act"], r["other"]
    load_tokens.wait()
    pl.semaphore_wait(barrier, len(greeted))
    pl.when(position < devices - 1)(halo_out.start)
    first_norm(r["x"], act)
    load_out.start()
    load_cot.start()
    for copy in load_tails:
        copy.start()
    for index, (ring, target) in enumerate(zip(rings, ("queries", "keys", "values"))):
        for copy in attention_weights[index * depth : (index + 1) * depth]:
            copy.wait()
        project(act, ring, r[target])
    by_owner("first", act)
    pl.when(position > 0)(halo_out.wait_recv)
    first_norm(r["x_before"], other)
    project(other, "ring_up", r["keys_before"])
    project(other, "ring_down", r["values_before"])
    for slot in range(depth):
        for copy in hidden_weights(slot, slot):
            copy.start()

    quad = CHUNK // HEAD
    start = position * block
    lane_head = lax.broadcasted_iota(jnp.int32, (block, CHUNK), 1) // HEAD
    key_at = start - WIN + lax.broadcasted_iota(jnp.int32, (2 * block, CHUNK), 0)
    query_at = start + lax.broadcasted_iota(jnp.int32, (1, CHUNK), 1) % block

    def stacked(value):
        return jnp.concatenate([jnp.where(lane_head == h, value, jnp.zeros_like(value)) for h in range(quad)], axis=0)

    def unstacked(value):
        total = jnp.zeros((block, CHUNK), F32)
        for h in range(quad):
            total = jnp.where(lane_head == h, value[h * block : (h + 1) * block], total)
        return total

    def unit(index):
        return index // chunks, some_rows(index // chunks), at_chunk(index % chunks)

    def both(before, own, rows, lanes):
        return jnp.concatenate([r[before][rows, lanes], r[own][rows, lanes]], axis=0)

    def allowed(which):
        def body(at, carry):
            end, low = carry
            end = end + r["lengths"][which, at]
            return end, jnp.where(query_at >= end, end, low)

        _, low = lax.fori_loop(
            0, r["lengths"].shape[1], body, (jnp.int32(0), jnp.zeros((1, CHUNK), jnp.int32))
        )
        low = jnp.maximum(low, query_at - (WIN - 1))
        return (key_at >= low) & (key_at <= query_at)

    def scores(which, keys, queries):
        return jnp.where(allowed(which), dot_rows(keys, queries) * scale, -1e30)

    def attend(index):
        which, rows, lanes = unit(index)
        logits = scores(which, both("keys_before", "keys", rows, lanes), stacked(r["queries"][rows, lanes]))
        peak = jnp.max(logits, axis=0, keepdims=True)
        powers = jnp.exp(logits - peak)
        total = jnp.sum(powers, axis=0, keepdims=True)
        r["log_sums"][index] = jnp.broadcast_to(peak + jnp.log(total), (8, CHUNK))
        probability = (powers / total).astype(BF16)
        mixed = dot_cols(probability, both("values_before", "values", rows, lanes))
        act[rows, lanes] = unstacked(mixed).astype(BF16)

    pair["cot"].start()
    loop(0, micro * chunks, attend, unroll=4)
    load_out.wait()
    middle = r["input_grad"]

    middle[...] = r["x"][...].astype(F32) + dot(act[...], r["wo"][...])

    def second_norm(at):
        value = middle[some_rows(at), :]
        other[some_rows(at), :] = (value * row_scale(value) * r["gain_mlp"][...]).astype(BF16)

    loop(0, micro, second_norm)
    by_owner("second", other)


    def hidden_part(gate, up, grad_hidden):
        sigmoid = jax.nn.sigmoid(gate)
        silu = gate * sigmoid
        hidden = (silu * up).astype(BF16)
        dgate = (grad_hidden * up * sigmoid * (1.0 + gate * (1.0 - sigmoid))).astype(BF16)
        return hidden, dgate, (grad_hidden * silu).astype(BF16)

    columns = r["columns"]

    def hidden_chunk(at, prefetch):
        slot = at % depth
        for copy in hidden_weights(at, at):
            copy.wait()
        wait_chunk(at - LAG)
        hidden, dgate, dup = hidden_part(
            dot_rows(other[...], r["ring_gate"][slot]),
            dot_rows(other[...], r["ring_up"][slot]),
            dot_rows(r["col_cot"][0], r["ring_down"][slot]),
        )
        lanes = at_chunk(at)
        form_chunk(at - LAG)
        r["hidden"][:, lanes] = hidden
        r["col_hidden"][0, at, 0] = dgate
        r["col_hidden"][0, at, 1] = dup
        columns[lanes, :] = hidden.astype(F32).T
        pair_chunk(at).start()
        send_chunk(at - LAG)
        if prefetch:
            for copy in hidden_weights(at + depth, at + depth):
                copy.start()

    early_factors = {}

    def early(at):
        return [
            (name, at - part[1]) for name, part in PARTS.items() if part[0] in ("gate", "up") and part[1] <= at < part[2]
        ]

    def wait_chunk(at):
        if at >= 0:
            pair_chunk(at).wait_recv()

    def form_chunk(at):
        for name, place in early(at):
            if name not in early_factors:
                early_factors[name] = factors(name, half)
            r["send_" + name][place] = product(early_factors[name], at).astype(BF16)

    def send_chunk(at):
        for name, place in early(at):
            step_copy(name, 0, place, place + 1).start()

    load_cot.wait()
    for copy in load_tails:
        copy.wait()
    for at in range(full):
        hidden_chunk(at, at < kept)
    hidden, dgate, dup = hidden_part(
        dot_rows(other[...], r["tail_gate"][...]),
        dot_rows(other[...], r["tail_up"][...]),
        dot_rows(r["col_cot"][0], r["tail_down"][...]),
    )
    r["hidden"][:, past] = hidden
    r["col_hidden"][0, full, 0, :, :tail] = dgate
    r["col_hidden"][0, full, 1, :, :tail] = dup
    pair_chunk(full).start()
    r["square"][...] = jnp.zeros_like(r["square"])
    r["square"][:, :tail] = hidden.astype(F32)
    columns[pl.ds(full * CHUNK, CHUNK), :] = r["square"][...].T
    own_rows = hidden_width // groups
    held_rows = r["row_hidden"].shape[2]
    for owner in range(groups):
        r["row_hidden"][owner // 2, owner % 2] = columns[pl.ds(owner * own_rows, held_rows), :].astype(BF16)
    pair["hidden"].start()
    for at in range(full - LAG, full + 1):
        wait_chunk(at)
        form_chunk(at)
        send_chunk(at)
    for name, part in PARTS.items():
        if part[0] == "down":
            send_products(name)


    sums = [pl.ds(n * CHUNK, CHUNK) for n in range(2 * chunks)]

    def fold(*pieces):
        back = None
        for dgate, dup, gate_ref, up_ref in pieces:
            one = dot(dgate, gate_ref[...]) + dot(dup, up_ref[...])
            back = one if back is None else back + one
        for n in range(chunks):
            columns[sums[n], :] += back[:, n * CHUNK : (n + 1) * CHUNK]

    def fold_chunks(places):
        pieces = []
        for at in places:
            chunk = at - depth if at < full + depth else at - depth - full
            if at >= full + depth:
                for copy in hidden_weights(chunk, at)[:2]:
                    copy.wait()
            pieces.append((
                r["col_hidden"][0, chunk, 0], r["col_hidden"][0, chunk, 1],
                *(r[ring].at[at % depth] for ring in rings[:2]),
            ))
        fold(*pieces)
        for at in places:
            if at < full + kept:
                for copy in hidden_weights(at - full, at + depth)[:2]:
                    copy.start()

    for some in sums[:chunks]:
        columns[some, :] = jnp.zeros((CHUNK, CHUNK), F32)
    fold((
        r["col_hidden"][0, full, 0, :, :tail], r["col_hidden"][0, full, 1, :, :tail], r["tail_gate"], r["tail_up"],
    ))
    for at in range(full, 2 * full, 2):
        fold_chunks(range(at, min(at + 2, 2 * full)))
    for copy in attention_weights:
        copy.start()

    def output_load(chunk):
        return hidden_weights(chunk, chunk)[2]

    def output_chunks(first, last):
        for chunk in range(first, last):
            output_load(chunk).wait()
        total = None
        for chunk in range(first, last):
            term = dot(r["hidden"][:, at_chunk(chunk)], r["ring_down"][chunk % depth])
            total = term if total is None else total + term
        for n in range(chunks):
            columns[sums[chunks + n], :] += total[:, n * CHUNK : (n + 1) * CHUNK]
        for chunk in range(first + depth, min(last + depth, full)):
            output_load(chunk).start()

    def form_output():
        rest = dot(r["hidden"][:, past], r["tail_down"][...])
        for n in range(chunks):
            columns[sums[chunks + n], :] += rest[:, n * CHUNK : (n + 1) * CHUNK]
        for first in range(0, full, 2):
            output_chunks(first, min(first + 2, full))
        for n in range(chunks):
            r["output"][:, at_chunk(n)] = columns[sums[chunks + n], :].astype(BF16)

    def summed(at, base):
        return jnp.concatenate(
            [columns[pl.ds((base + n) * CHUNK + at * block, block), :] for n in range(chunks)],
            axis=1,
        )

    def norm_backward(grad, value, gain):
        inverse = row_scale(value)
        normed = value * inverse
        scaled = grad * gain
        mean = jnp.mean(scaled * normed, axis=-1, keepdims=True)
        return inverse * (scaled - normed * mean), jnp.sum(grad * normed, axis=0, keepdims=True)

    def middle_backward(at, gain_sum):
        rows = some_rows(at)
        value = middle[rows, :]
        for n in range(chunks):
            place = pl.ds((chunks + n) * CHUNK + at * block, block)
            columns[place, :] = value[:, n * CHUNK : (n + 1) * CHUNK]
        grad, part = norm_backward(summed(at, 0), value, r["gain_mlp"][...])
        grad = grad + r["col_cot"][0, rows, :].astype(F32)
        middle[rows, :] = grad
        r["col_branch"][0, rows, :] = grad.astype(BF16)
        return gain_sum + part

    gain_mlp_sum = lax.fori_loop(0, micro, middle_backward, jnp.zeros((1, width), F32))
    pair["branch"].start()
    by_owner("attended", act)
    first_norm(r["x_before"], r["back_out"])
    by_owner("before", r["back_out"])

    r["grad_attended"][...] = dot_rows(r["col_branch"][0], r["wo"][...]).astype(BF16)


    def attend_backward(index):
        which, rows, lanes = unit(index)
        keys = both("keys_before", "keys", rows, lanes)
        values = both("values_before", "values", rows, lanes)
        queries = stacked(r["queries"][rows, lanes])
        grads = stacked(r["grad_attended"][rows, lanes])
        probability = jnp.exp(scores(which, keys, queries) - r["log_sums"][index][:1])
        grad_prob = dot_rows(values, grads)
        delta = jnp.sum(probability * grad_prob, axis=0, keepdims=True)
        grad_scores = (scale * probability * (grad_prob - delta)).astype(BF16)
        r["col_dquery"][0, rows, lanes] = unstacked(dot_cols(grad_scores, keys)).astype(BF16)
        dkey = dot(grad_scores, queries).astype(BF16)
        dvalue = dot(probability.astype(BF16), grads).astype(BF16)
        lanes_value = at_chunk(chunks + index % chunks)
        r["col_dkvback"][0, rows, lanes] = dkey[:block]
        r["col_dkvback"][0, rows, lanes_value] = dvalue[:block]
        r["col_dkeyval"][0, rows, lanes] = dkey[block:]
        r["col_dkeyval"][0, rows, lanes_value] = dvalue[block:]

    arrivals("middle")
    for at in range(micro):
        loop(at * chunks, (at + 1) * chunks, attend_backward, unroll=4)
        arrivals("attend" + str(at))
    for name in ("dquery", "dkeyval", "dkvback"):
        pair[name].start()
    def through_keys(ref, at):
        return dot_rows(ref[0, :, :width], r["ring_up"][at]) + dot_rows(ref[0, :, width:], r["ring_down"][at])

    def back_chunk(at):
        r["back_out"][:, at_chunk(at)] = through_keys(r["col_dkvback"], at).astype(BF16)

    def first_chunk(at):
        columns[at_chunk(at), :] = through_keys(r["col_dkeyval"], at) + dot_rows(
            r["col_dquery"][0], r["ring_gate"][at]
        )

    for copy in attention_weights:
        copy.wait()
    loop(0, chunks, back_chunk)
    pl.when(position > 0)(halo_back.start)
    arrivals("back")
    send_products("out")
    arrivals("out")

    def gain_parts(at, gain_sum):
        rows = some_rows(at)
        for grad, name in ((summed(at, 0), "x"), (r["back_out"][rows, :].astype(F32), "x_before")):
            value = r[name][rows, :].astype(F32)
            gain_sum = gain_sum + jnp.sum(grad * (value * row_scale(value)), axis=0, keepdims=True)
        return gain_sum

    for name in ("query", "key", "keyb"):
        send_products(name)
        arrivals(name)
    loop(0, chunks, first_chunk)
    gain_attn_sum = lax.fori_loop(0, micro, gain_parts, jnp.zeros((1, width), F32))
    gain_start(0, jnp.concatenate([gain_attn_sum, gain_mlp_sum, jnp.zeros((6, width), F32)], axis=0))
    arrivals("first")
    for chunk in range(depth):
        output_load(chunk).start()

    def input_backward(at):
        rows = some_rows(at)
        back = jnp.where(position < devices - 1, r["back_in"][rows, :].astype(F32), 0.0)
        grad, _ = norm_backward(summed(at, 0) + back, r["x"][rows, :].astype(F32), r["gain_attn"][...])
        middle[rows, :] = middle[rows, :] + grad

    for stage in range(len(peers)):
        if stage == 1:
            form_output()
        gain_step(stage)
        arrivals("gain" + str(stage))
    pl.when(position < devices - 1)(halo_back.wait_recv)
    loop(0, micro, input_backward)
    arrivals("last")

    pl.when(position < devices - 1)(halo_out.wait_send)
    pl.when(position > 0)(halo_back.wait_send)
    for copy in pair.values():
        copy.wait_send()
    for stage, group in enumerate(peers):
        for index in range(len(group)):
            gain_copy(stage, index).wait_send()
    pair_chunk(0, full + 1).wait_send()
    for name in PARTS:
        for level in range(bits):
            step_copy(name, level, 0, length(name)).wait_send()


def layer(tokens, gain_attn, gain_mlp, weights, cotangent, lengths, micro, devices, groups):
    rows_all, width = tokens.shape
    hidden_width = weights["w_gate"].shape[0]
    block = rows_all // micro
    bits = groups.bit_length() - 2
    count = 1 << bits
    half = count // 2
    chunks = width // CHUNK
    padded = round_up(hidden_width, CHUNK)
    tail = hidden_width % CHUNK
    depth = chunks
    unit_rows = {name: width // groups for name in ROWS}
    unit_rows["hidden"] = round_up(hidden_width // groups, 16)
    widths = {name: width for name in COLS}
    widths.update(dkeyval=2 * width, dkvback=2 * width)

    inputs = {"tokens": tokens, "cotangent": cotangent, **weights}
    any_spec = pl.BlockSpec(memory_space=pl.ANY)
    vmem_spec = pl.BlockSpec(memory_space=pltpu.VMEM)
    in_specs = [any_spec] * len(inputs) + [vmem_spec] * 2 + [pl.BlockSpec(memory_space=pltpu.SMEM)]
    inputs.update(gain_attn=gain_attn[None], gain_mlp=gain_mlp[None], lengths=lengths)

    outs = {
        "output": ((rows_all, width), BF16),
        "input_grad": ((rows_all, width), F32),
        "gain_attn_sum": ((width // 128, 128), F32),
        "gain_mlp_sum": ((width // 128, 128), F32),
    }
    own = {"query": width * width, "keyval": width * width, "value": width * width, "out": width * width}
    own.update(gate=width * hidden_width, up=width * hidden_width, down=width * hidden_width)
    for name, size in own.items():
        outs["flat_" + name] = ((size // groups // 128, 128), F32)

    scratch = {
        "x": pltpu.VMEM((rows_all, width), BF16),
        "x_before": pltpu.VMEM((rows_all, width), BF16),
        "act": pltpu.VMEM((rows_all, width), BF16),
        "other": pltpu.VMEM((rows_all, width), BF16),
        "queries": pltpu.VMEM((rows_all, width), BF16),
        "keys": pltpu.VMEM((rows_all, width), BF16),
        "values": pltpu.VMEM((rows_all, width), BF16),
        "keys_before": pltpu.VMEM((rows_all, width), BF16),
        "values_before": pltpu.VMEM((rows_all, width), BF16),
        "grad_attended": pltpu.VMEM((rows_all, width), BF16),
        "back_out": pltpu.VMEM((rows_all, width), BF16),
        "back_in": pltpu.VMEM((rows_all, width), BF16),
        "log_sums": pltpu.VMEM((micro * chunks, 8, CHUNK), F32),
        "wo": pltpu.VMEM((width, width), BF16),
        "ring_gate": pltpu.VMEM((depth, CHUNK, width), BF16),
        "ring_up": pltpu.VMEM((depth, CHUNK, width), BF16),
        "ring_down": pltpu.VMEM((depth, CHUNK, width), BF16),
        "tail_gate": pltpu.VMEM((tail, width), BF16),
        "tail_up": pltpu.VMEM((tail, width), BF16),
        "tail_down": pltpu.VMEM((tail, width), BF16),
        "hidden": pltpu.VMEM((rows_all, padded), BF16),
        "columns": pltpu.VMEM((padded, rows_all), F32),
        "square": pltpu.VMEM((rows_all, CHUNK), F32),
        "gain_buf": pltpu.VMEM((stage_copies(bits) + 3, 8, width), F32),
    }
    for name in ROWS:
        scratch["row_" + name] = pltpu.VMEM((count, 2, unit_rows[name], rows_all), BF16)
        scratch["peer_" + name] = pltpu.VMEM((count, unit_rows[name], rows_all), BF16)
    for name in COLS:
        if name not in CHUNKED:
            scratch["col_" + name] = pltpu.VMEM((2, rows_all, widths[name]), BF16)
    scratch["col_hidden"] = pltpu.VMEM((2, padded // CHUNK, len(CHUNKED), rows_all, CHUNK), BF16)
    for name, (matrix, first, last, _, _) in PARTS.items():
        rows = unit_rows[MATRICES[matrix][0][0]]
        scratch["send_" + name] = pltpu.VMEM((last - first, half, rows, CHUNK), BF16)
        for level in range(bits):
            scratch[f"land_{name}{level}"] = pltpu.VMEM((last - first, half >> level, rows, CHUNK), BF16)
        if matrix in ("gate", "up"):
            scratch["turn_" + matrix] = pltpu.VMEM((padded // 128 * rows, 128), F32)
        else:
            scratch["total_" + name] = pltpu.VMEM((last - first, rows, CHUNK), F32)
    sems = {"local_sem": (6,), "ring_sem": (3, depth)}
    sems.update(chunk_send=(1,), chunk_recv=(padded // CHUNK,))
    sems.update(step_send=(len(PARTS), bits), step_recv=(step_layout(bits)[1],))
    for name, number in (("pair", len(ROWS) + len(COLS) - len(CHUNKED)), ("halo", 2), ("gain", stage_copies(bits))):
        sems[name + "_send"] = sems[name + "_recv"] = (number,)
    for name, shape in sems.items():
        scratch[name] = pltpu.SemaphoreType.DMA(shape)

    sizes = (micro, block, width, hidden_width, devices, groups)
    results = pl.pallas_call(
        functools.partial(layer_kernel, sizes, tuple(inputs), tuple(outs), tuple(scratch)),
        out_shape=[jax.ShapeDtypeStruct(*spec) for spec in outs.values()],
        in_specs=in_specs,
        out_specs=[vmem_spec] * len(outs),
        scratch_shapes=list(scratch.values()),
        compiler_params=pltpu.CompilerParams(
            collective_id=0, has_side_effects=True, vmem_limit_bytes=63 * 2**20
        ),
        name="layer",
    )(*inputs.values())
    return dict(zip(outs, handed_on(results)))


def hand_on_kernel(count, *refs):
    sources, targets, passing = (refs[part * count : (part + 1) * count] for part in range(3))
    sems = refs[-1]
    arriving = [
        pltpu.make_async_copy(source, middle, sems.at[0, index])
        for index, (source, middle) in enumerate(zip(sources, passing))
    ]
    leaving = [
        pltpu.make_async_copy(middle, target, sems.at[1, index])
        for index, (middle, target) in enumerate(zip(passing, targets))
    ]
    for copy in arriving:
        copy.start()
    for before, copy in zip(arriving, leaving):
        before.wait()
        copy.start()
    for copy in leaving:
        copy.wait()


def handed_on(arrays):
    any_spec = pl.BlockSpec(memory_space=pl.ANY)
    count = len(arrays)
    return pl.pallas_call(
        functools.partial(hand_on_kernel, count),
        out_shape=[jax.ShapeDtypeStruct(array.shape, array.dtype) for array in arrays],
        in_specs=[any_spec] * count,
        out_specs=[any_spec] * count,
        scratch_shapes=[pltpu.VMEM(array.shape, array.dtype) for array in arrays]
        + [pltpu.SemaphoreType.DMA((2, count))],
        name="hand_on",
    )(*arrays)


def per_device(
    tokens, gain_attn, gain_mlp, w_query, w_key, w_value, w_out, w_gate, w_up, w_down, cotangent, lengths
):
    devices = lax.axis_size("seq")
    groups = min(devices, MOST_GROUPS)
    lower = devices // groups
    micro, block, width = tokens.shape
    weights = dict(
        w_query=w_query, w_key=w_key, w_value=w_value, w_out=w_out, w_gate=w_gate.T, w_up=w_up.T, w_down=w_down
    )
    result = layer(
        tokens.reshape(micro * block, width), gain_attn, gain_mlp, weights,
        cotangent.reshape(micro * block, width), lengths, micro, devices, groups,
    )
    near = [[high * lower + low for low in range(lower)] for high in range(groups)]

    def slice_of(name):
        flat = result["flat_" + name].reshape(-1)
        if lower == 1:
            return flat
        return lax.psum_scatter(flat, "seq", axis_index_groups=near, tiled=True)

    gain_sums = [result["gain_attn_sum"].reshape(-1), result["gain_mlp_sum"].reshape(-1)]
    if lower > 1:
        gain_sums = lax.psum(gain_sums, "seq", axis_index_groups=near)
    return (
        result["output"].reshape(tokens.shape),
        result["input_grad"].reshape(tokens.shape),
        gain_sums[0],
        gain_sums[1],
        slice_of("query"),
        slice_of("keyval"),
        slice_of("value"),
        slice_of("out"),
        slice_of("gate"),
        slice_of("up"),
        slice_of("down"),
    )


def solution(mesh):
    tokens_spec = P(None, "seq", None)
    return jax.shard_map(
        per_device,
        mesh=mesh,
        in_specs=(tokens_spec,) + (P(),) * 9 + (tokens_spec, P()),
        out_specs=(tokens_spec, tokens_spec, P(), P()) + (P("seq"),) * 7,
        check_vma=False,
    )
```

```python
import functools
import math

import jax
import jax.numpy as jnp
from jax import lax
from jax.experimental import pallas as pl
from jax.experimental.pallas import tpu as pltpu
from jax.sharding import PartitionSpec as P

HEAD = 64
WIN = 64
EPSILON = 1e-05
MESH = pl.DeviceIdType.MESH
MOST_GROUPS = 32
CHUNK = 256
BF16 = jnp.bfloat16
F32 = jnp.float32

MATRICES = {
    "down": (("hidden", "cot"),),
    "gate": (("second", "dgate"),),
    "up": (("second", "dup"),),
    "query": (("first", "dquery"),),
    "keyval": (("first", "dkeyval"), ("before", "dkvback")),
    "out": (("attended", "branch"),),
}
ROWS = ("first", "before", "attended", "second", "hidden")
CHUNKED = ("dgate", "dup")
COLS = ("cot", "dgate", "dup", "branch", "dquery", "dkeyval", "dkvback")
PARTS = {
    "gate": ("gate", 0, 1, (2, 1, 4, 3), (1, 2, 4, 4)),
    "gate2": ("gate", 1, 11, (1, 2, 4, 3), (1, 1, 2, 2)),
    "up": ("up", 0, 4, (3, 4, 1, 2), (1, 2, 4, 4)),
    "up2": ("up", 4, 11, (2, 3, 4, 1), (1, 1, 2, 4)),
    "down": ("down", 0, 3, (3, 1, 2, 4), (1, 1, 1, 1)),
    "rest": ("down", 3, 4, (1, 2, 3, 4), (1, 1, 1, 1)),
    "out": ("out", 0, 4, (2, 1, 3, 4), (1, 1, 2, 2)),
    "query": ("query", 0, 4, (2, 3, 4, 1), (1, 1, 2, 4)),
    "key": ("keyval", 0, 4, (1, 2, 4, 3), (1, 2, 4, 4)),
    "keyb": ("keyval", 4, 8, (1, 2, 3, 4), (1, 1, 2, 2)),
}
INDEX = {name: index for index, name in enumerate(PARTS)}
LAG = 2


SCHEDULE = {
    "middle": (
        ("gate2", 0, 0),
        ("gate2", 0, 1),
        ("gate2", 0, 2),
    ),
    "attend0": (
        ("gate2", 0, 3),
        ("gate2", 0, 4),
    ),
    "attend1": (
        ("gate2", 0, 5),
    ),
    "attend2": (
        ("gate2", 0, 6),
        ("gate2", 0, 7),
    ),
    "attend3": (
        ("gate2", 0, 8),
    ),
    "back": (
        ("gate2", 1, 0),
        ("gate2", 1, 2),
    ),
    "first": (
        ("gate2", 2, 2),
        ("gate", 1, 0),
        ("gate2", 2, 4),
        ("up2", 0, 1),
        ("up2", 0, 2),
        ("up2", 0, 3),
        ("up2", 0, 4),
        ("up2", 0, 5),
        ("up2", 0, 6),
    ),
    "query": (
        ("gate2", 1, 4),
        ("gate2", 1, 6),
        ("gate", 0, 0),
        ("up", 0, 0),
        ("down", 0, 0),
        ("up", 0, 2),
    ),
    "keyb": (
        ("gate2", 2, 0),
        ("up2", 0, 0),
    ),
    "gain0": (
        ("gate2", 2, 6),
        ("down", 1, 0),
        ("gate2", 0, 9),
        ("rest", 0, 0),
        ("down", 0, 1),
        ("down", 0, 2),
        ("out", 0, 0),
        ("out", 0, 1),
        ("out", 0, 2),
        ("out", 0, 3),
        ("key", 0, 0),
        ("up2", 1, 0),
        ("gate2", 3, 0),
        ("gate2", 3, 2),
        ("query", 0, 0),
        ("gate2", 3, 4),
        ("up2", 1, 2),
        ("query", 0, 1),
        ("key", 0, 2),
        ("up2", 1, 4),
        ("up", 1, 0),
        ("gate", 2, 0),
        ("up2", 1, 6),
        ("query", 0, 2),
        ("gate2", 3, 6),
        ("keyb", 0, 0),
        ("query", 0, 3),
        ("keyb", 0, 1),
        ("down", 2, 0),
        ("gate2", 1, 8),
        ("query", 1, 0),
        ("keyb", 0, 2),
        ("up2", 2, 0),
        ("gate", 3, 0),
    ),
    "gain1": (
        ("rest", 1, 0),
        ("keyb", 0, 3),
        ("query", 1, 2),
        ("down", 1, 1),
        ("up2", 2, 4),
        ("down", 3, 0),
        ("key", 1, 0),
        ("gate2", 2, 8),
        ("down", 1, 2),
    ),
    "last": (
        ("rest", 2, 0),
        ("out", 1, 0),
        ("keyb", 1, 0),
        ("keyb", 1, 2),
        ("out", 1, 2),
        ("query", 2, 0),
        ("down", 2, 1),
        ("gate2", 3, 8),
        ("down", 2, 2),
        ("up", 2, 0),
        ("up2", 3, 0),
        ("up2", 3, 4),
        ("out", 2, 0),
        ("key", 2, 0),
        ("keyb", 2, 0),
        ("query", 3, 0),
        ("rest", 3, 0),
        ("keyb", 2, 2),
        ("out", 2, 2),
        ("up", 3, 0),
        ("down", 3, 1),
        ("down", 3, 2),
        ("key", 3, 0),
        ("out", 3, 0),
        ("keyb", 3, 0),
        ("keyb", 3, 2),
        ("out", 3, 2),
    ),
}


def round_up(value, unit):
    return -(-value // unit) * unit


def length(name):
    return PARTS[name][2] - PARTS[name][1]


def step_span(name, level):
    return PARTS[name][4][level]


def step_layout(bits):
    places, total = {}, 0
    for name in PARTS:
        for level in range(bits):
            places[name, level] = total
            total += -(-length(name) // step_span(name, level))
    return places, total


def stage_copies(bits):
    return 1 + (1 << min(bits, 2)) - 1 + (1 << max(bits - 2, 0)) - 1


def bit_of(number, bit):
    return (number // (1 << bit)) % 2


def flip(number, bit):
    return number + (1 << bit) * (1 - 2 * bit_of(number, bit))


def dot(left, right):
    return jnp.dot(left, right, preferred_element_type=F32)


def dot_rows(left, right):
    return lax.dot_general(left, right, (((1,), (1,)), ((), ())), preferred_element_type=F32)


def dot_cols(left, right):
    return lax.dot_general(left, right, (((0,), (0,)), ((), ())), preferred_element_type=F32)


def at_chunk(index, size=CHUNK):
    return pl.ds(index * size, size)


def loop(first, last, body, **options):
    def step(at, carry):
        body(at)
        return carry

    lax.fori_loop(first, last, step, 0, **options)


def layer_kernel(sizes, in_names, out_names, scratch_names, *refs):
    micro, block, width, hidden_width, devices, groups = sizes
    r = dict(zip(in_names + out_names + scratch_names, refs))
    lower = devices // groups
    bits = groups.bit_length() - 2
    count = 1 << bits
    half = count // 2
    step_places, _ = step_layout(bits)
    orders = {name: [bit for bit in part[3] if bit <= bits] for name, part in PARTS.items()}
    rows_all = micro * block
    chunks = width // CHUNK
    full = hidden_width // CHUNK
    tail = hidden_width % CHUNK
    depth = r["ring_gate"].shape[0]
    kept = full - depth
    scale = 1.0 / math.sqrt(HEAD)

    schedule = SCHEDULE
    if bits != 4:
        schedule = {"last": [
            (name, level, first)
            for level in range(bits) for name in PARTS
            for first in range(0, length(name), step_span(name, min(level + 1, bits - 1)))
        ]}

    position = lax.axis_index("seq")
    me, rest = position // lower, position % lower
    core = me % 2
    my_unit = me // 2
    after = ((position + 1) % devices,)
    behind = ((position + devices - 1) % devices,)

    def partner(*some):
        other = me
        for bit in some:
            other = flip(other, bit)
        return (other * lower + rest,)

    stages = [[0], list(range(1, bits + 1))[:2], list(range(1, bits + 1))[2:]]
    stages = [stage for stage in stages if stage]
    peers = [
        [partner(*[bit for place, bit in enumerate(stage) if mask >> place & 1]) for mask in range(1, 1 << len(stage))]
        for stage in stages
    ]


    def local_copy(source, target, index):
        return pltpu.make_async_copy(source, target, r["local_sem"].at[index])

    def remote_copy(source, target, sems, index, device):
        send, recv = r[sems + "_send"], r[sems + "_recv"]
        return pltpu.make_async_remote_copy(
            src_ref=source, dst_ref=target, send_sem=send.at[index], recv_sem=recv.at[index],
            device_id=device, device_id_type=MESH,
        )

    load_tokens = local_copy(r["tokens"], r["x"], 0)
    load_cot = local_copy(r["cotangent"], r["col_cot"].at[0], 1)
    load_out = local_copy(r["w_out"], r["wo"], 2)
    rings = ("ring_gate", "ring_up", "ring_down")
    past = pl.ds(full * CHUNK, tail)
    load_tails = [
        local_copy(r[name].at[past, :], r["tail_" + name[2:]], 3 + index)
        for index, name in enumerate(("w_gate", "w_up", "w_down"))
    ]
    attention_weights = [
        pltpu.make_async_copy(r[name].at[at_chunk(slot), :], r[ring].at[slot], r["ring_sem"].at[index, slot])
        for index, (name, ring) in enumerate(zip(("w_query", "w_key", "w_value"), rings))
        for slot in range(depth)
    ]

    def hidden_weights(chunk, place):
        slot = place % depth
        return [
            pltpu.make_async_copy(r[name].at[at_chunk(chunk), :], r[ring].at[slot], r["ring_sem"].at[index, slot])
            for index, (name, ring) in enumerate(zip(("w_gate", "w_up", "w_down"), rings))
        ]

    def pair_copies():
        plan = {}
        for name in ROWS:
            plan[name] = (r["row_" + name].at[:, 1 - core], r["peer_" + name])
        plan["cot"] = (r["cotangent"], r["col_cot"].at[1])
        for name in ("branch", "dquery", "dkeyval", "dkvback"):
            plan[name] = (r["col_" + name].at[0], r["col_" + name].at[1])
        return {
            name: remote_copy(source, target, "pair", index, partner(0))
            for index, (name, (source, target)) in enumerate(plan.items())
        }

    pair = pair_copies()
    ready = set()

    def need(name):
        if name not in ready and name not in CHUNKED:
            ready.add(name)
            pair[name].wait_recv()

    def pair_chunk(first, last=None):
        ref = r["col_hidden"]
        some = pl.ds(first, 1 if last is None else last - first)
        return pltpu.make_async_remote_copy(
            src_ref=ref.at[0, some], dst_ref=ref.at[1, some],
            send_sem=r["chunk_send"].at[0], recv_sem=r["chunk_recv"].at[first],
            device_id=partner(0), device_id_type=MESH,
        )

    halo_out = remote_copy(r["x"], r["x_before"], "halo", 0, after)
    halo_back = remote_copy(r["back_out"], r["back_in"], "halo", 1, behind)

    load_tokens.start()
    r["x_before"][...] = jnp.zeros_like(r["x_before"])
    barrier = pltpu.get_barrier_semaphore()
    greeted = [after, behind] + [device for stage in peers for device in stage]
    for device in greeted:
        pl.semaphore_signal(barrier, inc=1, device_id=device, device_id_type=MESH)
    for copy in attention_weights:
        copy.start()
    for part in range(2):
        r["col_hidden"][0, full, part] = jnp.zeros((rows_all, CHUNK), BF16)


    def unit_at(order, slot):
        unit = my_unit
        for place, bit in enumerate(order):
            rel = (slot // (1 << (bits - 1 - place))) % 2
            unit = unit + (1 << (bit - 1)) * rel * (1 - 2 * bit_of(me, bit))
        return unit

    def factors(name, base):
        matrix = PARTS[name][0]
        units = [unit_at(orders[name], base + slot) for slot in range(half)]
        pairs = []
        for row, col in MATRICES[matrix]:
            need(row)
            need(col)
            for source in range(2):
                parts = [
                    r["row_" + row][unit, core] if source == 0 else r["peer_" + row][unit] for unit in units
                ]
                pairs.append((jnp.concatenate(parts, axis=0), col, source))
        return pairs

    def product(pairs, chunk):
        total = None
        for left, col, source in pairs:
            if col in CHUNKED:
                right = r["col_hidden"][source, chunk, CHUNKED.index(col)]
            else:
                right = r["col_" + col][source, :, at_chunk(chunk)]
            term = dot(left, right)
            total = term if total is None else total + term
        return total.reshape(half, total.shape[0] // half, CHUNK)

    def step_copy(name, level, first, last):
        size = half >> level
        some = pl.ds(first, last - first)
        if level == 0:
            source = r["send_" + name].at[some]
        else:
            source = r[f"land_{name}{level - 1}"].at[some, pl.ds(size, size)]
        place = step_places[name, level] + first // step_span(name, level)
        return pltpu.make_async_remote_copy(
            src_ref=source, dst_ref=r[f"land_{name}{level}"].at[some],
            send_sem=r["step_send"].at[INDEX[name], level], recv_sem=r["step_recv"].at[place],
            device_id=partner(orders[name][level]), device_id_type=MESH,
        )

    def send_products(name):
        pairs = factors(name, half)
        for at in range(length(name)):
            r["send_" + name][at] = product(pairs, PARTS[name][1] + at).astype(BF16)
            step_copy(name, 0, at, at + 1).start()

    def arrive(name, level, first):
        last = min(first + step_span(name, min(level + 1, bits - 1)), length(name))
        matrix, base = PARTS[name][:2]
        here = r[f"land_{name}{level}"]
        pairs = factors(name, 0) if level == 0 else None
        size = half >> level
        span = step_span(name, level)
        for at in range(first, last, span):
            step_copy(name, level, at, min(at + span, last)).wait_recv()
        for at in range(first, last):
            if level == 0:
                own = product(pairs, base + at)
            else:
                own = r[f"land_{name}{level - 1}"][at, :size].astype(F32)
            total = own + here[at].astype(F32)
            if level < bits - 1:
                here[at] = total.astype(BF16)
            elif matrix in ("gate", "up"):
                rows = total.shape[1]
                for part in range(CHUNK // 128):
                    place = ((base + at) * (CHUNK // 128) + part) * rows
                    r["turn_" + matrix][pl.ds(place, rows), :] = total[0, :, 128 * part : 128 * (part + 1)]
            else:
                r["total_" + name][at] = total[0]
        if level < bits - 1:
            step_copy(name, level + 1, first, last).start()
        else:
            unfinished[matrix] -= last - first
            if not unfinished[matrix]:
                finish(matrix)

    unfinished = {}
    for name, part in PARTS.items():
        unfinished[part[0]] = unfinished.get(part[0], 0) + length(name)

    def finish(matrix):
        if matrix in ("gate", "up"):
            flat, turn = r["flat_" + matrix], r["turn_" + matrix]
            whole = hidden_width // 128
            steps = hidden_width // 64
            rows = turn.shape[0] // (whole + 1)
            few = rows // 2
            even = [turn[pl.ds(rows * j, few, stride=2), :] for j in range(whole + 1)]
            odd = [pltpu.roll(turn[pl.ds(rows * j + 1, few, stride=2), :], 64, 1) for j in range(whole + 1)]
            low = lax.broadcasted_iota(jnp.int32, (few, 128), 1) < 64
            for j in range(whole):
                flat[pl.ds(j, few, stride=steps), :] = even[j]
                flat[pl.ds(whole + 1 + j, few, stride=steps), :] = jnp.where(low, odd[j], odd[j + 1])
            flat[pl.ds(whole, few, stride=steps), :] = jnp.where(low, even[whole], odd[0])
            return
        per_row = width // 128
        for name, part in PARTS.items():
            if part[0] != matrix:
                continue
            for at in range(length(name)):
                total = r["total_" + name][at]
                for piece in range(CHUNK // 128):
                    column = (part[1] + at) * (CHUNK // 128) + piece
                    target = "flat_value" if column >= per_row else "flat_" + matrix
                    rows = r[target].shape[0] // per_row
                    r[target][pl.ds(column % per_row, rows, stride=per_row), :] = total[:rows, 128 * piece : 128 * (piece + 1)]

    def gain_copy(stage, index):
        base = sum(len(group) + 1 for group in peers[:stage])
        return remote_copy(
            r["gain_buf"].at[base], r["gain_buf"].at[base + 1 + index], "gain", base - stage + index, peers[stage][index]
        )

    def gain_start(stage, value):
        r["gain_buf"][sum(len(group) + 1 for group in peers[:stage])] = value
        for index in range(len(peers[stage])):
            gain_copy(stage, index).start()

    def gain_step(stage):
        base = sum(len(group) + 1 for group in peers[:stage])
        total = r["gain_buf"][base]
        for index in range(len(peers[stage])):
            gain_copy(stage, index).wait_recv()
            total = total + r["gain_buf"][base + 1 + index]
        if stage + 1 < len(peers):
            gain_start(stage + 1, total)
            return
        for row, name in enumerate(("gain_attn_sum", "gain_mlp_sum")):
            for j in range(width // 128):
                r[name][j : j + 1, :] = total[row : row + 1, 128 * j : 128 * (j + 1)]

    def arrivals(point):
        for name, level, first in schedule.get(point, ()):
            arrive(name, level, first)


    def some_rows(at):
        return pl.ds(at * block, block)

    def row_scale(value):
        return lax.rsqrt(jnp.mean(value * value, axis=-1, keepdims=True) + EPSILON)

    def first_norm(source, target):
        def body(at):
            value = source[some_rows(at), :].astype(F32)
            target[some_rows(at), :] = (value * row_scale(value) * r["gain_attn"][...]).astype(BF16)

        loop(0, micro, body)

    def by_owner(name, source):
        ref = r["row_" + name]
        ref[...] = source[...].T.reshape(ref.shape)
        pair[name].start()

    def project(left, ring, target):
        target[...] = dot(left[...], r[ring][...].reshape(width, width)).astype(BF16)

    act, other = r["act"], r["other"]
    load_tokens.wait()
    pl.semaphore_wait(barrier, len(greeted))
    pl.when(position < devices - 1)(halo_out.start)
    first_norm(r["x"], act)
    load_out.start()
    load_cot.start()
    for copy in load_tails:
        copy.start()
    for index, (ring, target) in enumerate(zip(rings, ("queries", "keys", "values"))):
        for copy in attention_weights[index * depth : (index + 1) * depth]:
            copy.wait()
        project(act, ring, r[target])
    by_owner("first", act)
    pl.when(position > 0)(halo_out.wait_recv)
    first_norm(r["x_before"], other)
    project(other, "ring_up", r["keys_before"])
    project(other, "ring_down", r["values_before"])
    for slot in range(depth):
        for copy in hidden_weights(slot, slot):
            copy.start()

    quad = CHUNK // HEAD
    start = position * block
    lane_head = lax.broadcasted_iota(jnp.int32, (block, CHUNK), 1) // HEAD
    key_at = start - WIN + lax.broadcasted_iota(jnp.int32, (2 * block, CHUNK), 0)
    query_at = start + lax.broadcasted_iota(jnp.int32, (1, CHUNK), 1) % block

    def stacked(value):
        return jnp.concatenate([jnp.where(lane_head == h, value, jnp.zeros_like(value)) for h in range(quad)], axis=0)

    def unstacked(value):
        total = jnp.zeros((block, CHUNK), F32)
        for h in range(quad):
            total = jnp.where(lane_head == h, value[h * block : (h + 1) * block], total)
        return total

    def unit(index):
        return index // chunks, some_rows(index // chunks), at_chunk(index % chunks)

    def both(before, own, rows, lanes):
        return jnp.concatenate([r[before][rows, lanes], r[own][rows, lanes]], axis=0)

    def allowed(which):
        def body(at, carry):
            end, low = carry
            end = end + r["lengths"][which, at]
            return end, jnp.where(query_at >= end, end, low)

        _, low = lax.fori_loop(
            0, r["lengths"].shape[1], body, (jnp.int32(0), jnp.zeros((1, CHUNK), jnp.int32))
        )
        low = jnp.maximum(low, query_at - (WIN - 1))
        return (key_at >= low) & (key_at <= query_at)

    def scores(which, keys, queries):
        return jnp.where(allowed(which), dot_rows(keys, queries) * scale, -1e30)

    def attend(index):
        which, rows, lanes = unit(index)
        logits = scores(which, both("keys_before", "keys", rows, lanes), stacked(r["queries"][rows, lanes]))
        peak = jnp.max(logits, axis=0, keepdims=True)
        powers = jnp.exp(logits - peak)
        total = jnp.sum(powers, axis=0, keepdims=True)
        r["log_sums"][index] = jnp.broadcast_to(peak + jnp.log(total), (8, CHUNK))
        probability = (powers / total).astype(BF16)
        mixed = dot_cols(probability, both("values_before", "values", rows, lanes))
        act[rows, lanes] = unstacked(mixed).astype(BF16)

    pair["cot"].start()
    loop(0, micro * chunks, attend, unroll=2)
    load_out.wait()
    middle = r["input_grad"]

    middle[...] = r["x"][...].astype(F32) + dot(act[...], r["wo"][...])

    def second_norm(at):
        value = middle[some_rows(at), :]
        other[some_rows(at), :] = (value * row_scale(value) * r["gain_mlp"][...]).astype(BF16)

    loop(0, micro, second_norm)
    by_owner("second", other)


    def hidden_part(gate, up, grad_hidden):
        sigmoid = jax.nn.sigmoid(gate)
        silu = gate * sigmoid
        hidden = (silu * up).astype(BF16)
        dgate = (grad_hidden * up * sigmoid * (1.0 + gate * (1.0 - sigmoid))).astype(BF16)
        return hidden, dgate, (grad_hidden * silu).astype(BF16)

    columns = r["columns"]

    def hidden_chunk(at, prefetch):
        slot = at % depth
        for copy in hidden_weights(at, at):
            copy.wait()
        wait_chunk(at - LAG)
        hidden, dgate, dup = hidden_part(
            dot_rows(other[...], r["ring_gate"][slot]),
            dot_rows(other[...], r["ring_up"][slot]),
            dot_rows(r["col_cot"][0], r["ring_down"][slot]),
        )
        lanes = at_chunk(at)
        form_chunk(at - LAG)
        r["hidden"][:, lanes] = hidden
        r["col_hidden"][0, at, 0] = dgate
        r["col_hidden"][0, at, 1] = dup
        columns[lanes, :] = hidden.astype(F32).T
        pair_chunk(at).start()
        send_chunk(at - LAG)
        if prefetch:
            for copy in hidden_weights(at + depth, at + depth):
                copy.start()

    early_factors = {}

    def early(at):
        return [
            (name, at - part[1]) for name, part in PARTS.items() if part[0] in ("gate", "up") and part[1] <= at < part[2]
        ]

    def wait_chunk(at):
        if at >= 0:
            pair_chunk(at).wait_recv()

    def form_chunk(at):
        for name, place in early(at):
            if name not in early_factors:
                early_factors[name] = factors(name, half)
            r["send_" + name][place] = product(early_factors[name], at).astype(BF16)

    def send_chunk(at):
        for name, place in early(at):
            step_copy(name, 0, place, place + 1).start()

    load_cot.wait()
    for copy in load_tails:
        copy.wait()
    for at in range(full):
        hidden_chunk(at, at < kept)
    hidden, dgate, dup = hidden_part(
        dot_rows(other[...], r["tail_gate"][...]),
        dot_rows(other[...], r["tail_up"][...]),
        dot_rows(r["col_cot"][0], r["tail_down"][...]),
    )
    r["hidden"][:, past] = hidden
    r["col_hidden"][0, full, 0, :, :tail] = dgate
    r["col_hidden"][0, full, 1, :, :tail] = dup
    pair_chunk(full).start()
    r["square"][...] = jnp.zeros_like(r["square"])
    r["square"][:, :tail] = hidden.astype(F32)
    columns[pl.ds(full * CHUNK, CHUNK), :] = r["square"][...].T
    own_rows = hidden_width // groups
    held_rows = r["row_hidden"].shape[2]
    for owner in range(groups):
        r["row_hidden"][owner // 2, owner % 2] = columns[pl.ds(owner * own_rows, held_rows), :].astype(BF16)
    pair["hidden"].start()
    for at in range(full - LAG, full + 1):
        wait_chunk(at)
        form_chunk(at)
        send_chunk(at)
    for name, part in PARTS.items():
        if part[0] == "down":
            send_products(name)


    sums = [pl.ds(n * CHUNK, CHUNK) for n in range(2 * chunks)]

    def fold(*pieces):
        back = None
        for dgate, dup, gate_ref, up_ref in pieces:
            one = dot(dgate, gate_ref[...]) + dot(dup, up_ref[...])
            back = one if back is None else back + one
        for n in range(chunks):
            columns[sums[n], :] += back[:, n * CHUNK : (n + 1) * CHUNK]

    def fold_chunks(places):
        pieces = []
        for at in places:
            chunk = at - depth if at < full + depth else at - depth - full
            if at >= full + depth:
                for copy in hidden_weights(chunk, at)[:2]:
                    copy.wait()
            pieces.append((
                r["col_hidden"][0, chunk, 0], r["col_hidden"][0, chunk, 1],
                *(r[ring].at[at % depth] for ring in rings[:2]),
            ))
        fold(*pieces)
        for at in places:
            if at < full + kept:
                for copy in hidden_weights(at - full, at + depth)[:2]:
                    copy.start()

    for some in sums[:chunks]:
        columns[some, :] = jnp.zeros((CHUNK, CHUNK), F32)
    fold((
        r["col_hidden"][0, full, 0, :, :tail], r["col_hidden"][0, full, 1, :, :tail], r["tail_gate"], r["tail_up"],
    ))
    for at in range(full, 2 * full, 2):
        fold_chunks(range(at, min(at + 2, 2 * full)))
    for copy in attention_weights:
        copy.start()

    def output_load(chunk):
        return hidden_weights(chunk, chunk)[2]

    def output_chunks(first, last):
        for chunk in range(first, last):
            output_load(chunk).wait()
        total = None
        for chunk in range(first, last):
            term = dot(r["hidden"][:, at_chunk(chunk)], r["ring_down"][chunk % depth])
            total = term if total is None else total + term
        for n in range(chunks):
            columns[sums[chunks + n], :] += total[:, n * CHUNK : (n + 1) * CHUNK]
        for chunk in range(first + depth, min(last + depth, full)):
            output_load(chunk).start()

    def form_output():
        rest = dot(r["hidden"][:, past], r["tail_down"][...])
        for n in range(chunks):
            columns[sums[chunks + n], :] += rest[:, n * CHUNK : (n + 1) * CHUNK]
        for first in range(0, full, 2):
            output_chunks(first, min(first + 2, full))
        for n in range(chunks):
            r["output"][:, at_chunk(n)] = columns[sums[chunks + n], :].astype(BF16)

    def summed(at, base):
        return jnp.concatenate(
            [columns[pl.ds((base + n) * CHUNK + at * block, block), :] for n in range(chunks)],
            axis=1,
        )

    def norm_backward(grad, value, gain):
        inverse = row_scale(value)
        normed = value * inverse
        scaled = grad * gain
        mean = jnp.mean(scaled * normed, axis=-1, keepdims=True)
        return inverse * (scaled - normed * mean), jnp.sum(grad * normed, axis=0, keepdims=True)

    def middle_backward(at, gain_sum):
        rows = some_rows(at)
        value = middle[rows, :]
        for n in range(chunks):
            place = pl.ds((chunks + n) * CHUNK + at * block, block)
            columns[place, :] = value[:, n * CHUNK : (n + 1) * CHUNK]
        grad, part = norm_backward(summed(at, 0), value, r["gain_mlp"][...])
        grad = grad + r["col_cot"][0, rows, :].astype(F32)
        middle[rows, :] = grad
        r["col_branch"][0, rows, :] = grad.astype(BF16)
        return gain_sum + part

    gain_mlp_sum = lax.fori_loop(0, micro, middle_backward, jnp.zeros((1, width), F32))
    pair["branch"].start()
    by_owner("attended", act)
    first_norm(r["x_before"], r["back_out"])
    by_owner("before", r["back_out"])

    r["grad_attended"][...] = dot_rows(r["col_branch"][0], r["wo"][...]).astype(BF16)


    def attend_backward(index):
        which, rows, lanes = unit(index)
        keys = both("keys_before", "keys", rows, lanes)
        values = both("values_before", "values", rows, lanes)
        queries = stacked(r["queries"][rows, lanes])
        grads = stacked(r["grad_attended"][rows, lanes])
        probability = jnp.exp(scores(which, keys, queries) - r["log_sums"][index][:1])
        grad_prob = dot_rows(values, grads)
        delta = jnp.sum(probability * grad_prob, axis=0, keepdims=True)
        grad_scores = (scale * probability * (grad_prob - delta)).astype(BF16)
        r["col_dquery"][0, rows, lanes] = unstacked(dot_cols(grad_scores, keys)).astype(BF16)
        dkey = dot(grad_scores, queries).astype(BF16)
        dvalue = dot(probability.astype(BF16), grads).astype(BF16)
        lanes_value = at_chunk(chunks + index % chunks)
        r["col_dkvback"][0, rows, lanes] = dkey[:block]
        r["col_dkvback"][0, rows, lanes_value] = dvalue[:block]
        r["col_dkeyval"][0, rows, lanes] = dkey[block:]
        r["col_dkeyval"][0, rows, lanes_value] = dvalue[block:]

    arrivals("middle")
    for at in range(micro):
        loop(at * chunks, (at + 1) * chunks, attend_backward, unroll=2)
        arrivals("attend" + str(at))
    for name in ("dquery", "dkeyval", "dkvback"):
        pair[name].start()
    def through_keys(ref, at):
        return dot_rows(ref[0, :, :width], r["ring_up"][at]) + dot_rows(ref[0, :, width:], r["ring_down"][at])

    def back_chunk(at):
        r["back_out"][:, at_chunk(at)] = through_keys(r["col_dkvback"], at).astype(BF16)

    def first_chunk(at):
        columns[at_chunk(at), :] = through_keys(r["col_dkeyval"], at) + dot_rows(
            r["col_dquery"][0], r["ring_gate"][at]
        )

    for copy in attention_weights:
        copy.wait()
    loop(0, chunks, back_chunk)
    pl.when(position > 0)(halo_back.start)
    arrivals("back")
    send_products("out")
    arrivals("out")

    def gain_parts(at, gain_sum):
        rows = some_rows(at)
        for grad, name in ((summed(at, 0), "x"), (r["back_out"][rows, :].astype(F32), "x_before")):
            value = r[name][rows, :].astype(F32)
            gain_sum = gain_sum + jnp.sum(grad * (value * row_scale(value)), axis=0, keepdims=True)
        return gain_sum

    for name in ("query", "key", "keyb"):
        send_products(name)
        arrivals(name)
    loop(0, chunks, first_chunk)
    gain_attn_sum = lax.fori_loop(0, micro, gain_parts, jnp.zeros((1, width), F32))
    gain_start(0, jnp.concatenate([gain_attn_sum, gain_mlp_sum, jnp.zeros((6, width), F32)], axis=0))
    arrivals("first")
    for chunk in range(depth):
        output_load(chunk).start()

    def input_backward(at):
        rows = some_rows(at)
        back = jnp.where(position < devices - 1, r["back_in"][rows, :].astype(F32), 0.0)
        grad, _ = norm_backward(summed(at, 0) + back, r["x"][rows, :].astype(F32), r["gain_attn"][...])
        middle[rows, :] = middle[rows, :] + grad

    for stage in range(len(peers)):
        if stage == 1:
            form_output()
        gain_step(stage)
        arrivals("gain" + str(stage))
    pl.when(position < devices - 1)(halo_back.wait_recv)
    loop(0, micro, input_backward)
    arrivals("last")

    pl.when(position < devices - 1)(halo_out.wait_send)
    pl.when(position > 0)(halo_back.wait_send)
    for copy in pair.values():
        copy.wait_send()
    for stage, group in enumerate(peers):
        for index in range(len(group)):
            gain_copy(stage, index).wait_send()
    pair_chunk(0, full + 1).wait_send()
    for name in PARTS:
        for level in range(bits):
            step_copy(name, level, 0, length(name)).wait_send()


def layer(tokens, gain_attn, gain_mlp, weights, cotangent, lengths, micro, devices, groups):
    rows_all, width = tokens.shape
    hidden_width = weights["w_gate"].shape[0]
    block = rows_all // micro
    bits = groups.bit_length() - 2
    count = 1 << bits
    half = count // 2
    chunks = width // CHUNK
    padded = round_up(hidden_width, CHUNK)
    tail = hidden_width % CHUNK
    depth = chunks
    unit_rows = {name: width // groups for name in ROWS}
    unit_rows["hidden"] = round_up(hidden_width // groups, 16)
    widths = {name: width for name in COLS}
    widths.update(dkeyval=2 * width, dkvback=2 * width)

    inputs = {"tokens": tokens, "cotangent": cotangent, **weights}
    any_spec = pl.BlockSpec(memory_space=pl.ANY)
    vmem_spec = pl.BlockSpec(memory_space=pltpu.VMEM)
    in_specs = [any_spec] * len(inputs) + [vmem_spec] * 2 + [pl.BlockSpec(memory_space=pltpu.SMEM)]
    inputs.update(gain_attn=gain_attn[None], gain_mlp=gain_mlp[None], lengths=lengths)

    outs = {
        "output": ((rows_all, width), BF16),
        "input_grad": ((rows_all, width), F32),
        "gain_attn_sum": ((width // 128, 128), F32),
        "gain_mlp_sum": ((width // 128, 128), F32),
    }
    own = {"query": width * width, "keyval": width * width, "value": width * width, "out": width * width}
    own.update(gate=width * hidden_width, up=width * hidden_width, down=width * hidden_width)
    for name, size in own.items():
        outs["flat_" + name] = ((size // groups // 128, 128), F32)

    scratch = {
        "x": pltpu.VMEM((rows_all, width), BF16),
        "x_before": pltpu.VMEM((rows_all, width), BF16),
        "act": pltpu.VMEM((rows_all, width), BF16),
        "other": pltpu.VMEM((rows_all, width), BF16),
        "queries": pltpu.VMEM((rows_all, width), BF16),
        "keys": pltpu.VMEM((rows_all, width), BF16),
        "values": pltpu.VMEM((rows_all, width), BF16),
        "keys_before": pltpu.VMEM((rows_all, width), BF16),
        "values_before": pltpu.VMEM((rows_all, width), BF16),
        "grad_attended": pltpu.VMEM((rows_all, width), BF16),
        "back_out": pltpu.VMEM((rows_all, width), BF16),
        "back_in": pltpu.VMEM((rows_all, width), BF16),
        "log_sums": pltpu.VMEM((micro * chunks, 8, CHUNK), F32),
        "wo": pltpu.VMEM((width, width), BF16),
        "ring_gate": pltpu.VMEM((depth, CHUNK, width), BF16),
        "ring_up": pltpu.VMEM((depth, CHUNK, width), BF16),
        "ring_down": pltpu.VMEM((depth, CHUNK, width), BF16),
        "tail_gate": pltpu.VMEM((tail, width), BF16),
        "tail_up": pltpu.VMEM((tail, width), BF16),
        "tail_down": pltpu.VMEM((tail, width), BF16),
        "hidden": pltpu.VMEM((rows_all, padded), BF16),
        "columns": pltpu.VMEM((padded, rows_all), F32),
        "square": pltpu.VMEM((rows_all, CHUNK), F32),
        "gain_buf": pltpu.VMEM((stage_copies(bits) + 3, 8, width), F32),
    }
    for name in ROWS:
        scratch["row_" + name] = pltpu.VMEM((count, 2, unit_rows[name], rows_all), BF16)
        scratch["peer_" + name] = pltpu.VMEM((count, unit_rows[name], rows_all), BF16)
    for name in COLS:
        if name not in CHUNKED:
            scratch["col_" + name] = pltpu.VMEM((2, rows_all, widths[name]), BF16)
    scratch["col_hidden"] = pltpu.VMEM((2, padded // CHUNK, len(CHUNKED), rows_all, CHUNK), BF16)
    for name, (matrix, first, last, _, _) in PARTS.items():
        rows = unit_rows[MATRICES[matrix][0][0]]
        scratch["send_" + name] = pltpu.VMEM((last - first, half, rows, CHUNK), BF16)
        for level in range(bits):
            scratch[f"land_{name}{level}"] = pltpu.VMEM((last - first, half >> level, rows, CHUNK), BF16)
        if matrix in ("gate", "up"):
            scratch["turn_" + matrix] = pltpu.VMEM((padded // 128 * rows, 128), F32)
        else:
            scratch["total_" + name] = pltpu.VMEM((last - first, rows, CHUNK), F32)
    sems = {"local_sem": (6,), "ring_sem": (3, depth)}
    sems.update(chunk_send=(1,), chunk_recv=(padded // CHUNK,))
    sems.update(step_send=(len(PARTS), bits), step_recv=(step_layout(bits)[1],))
    for name, number in (("pair", len(ROWS) + len(COLS) - len(CHUNKED)), ("halo", 2), ("gain", stage_copies(bits))):
        sems[name + "_send"] = sems[name + "_recv"] = (number,)
    for name, shape in sems.items():
        scratch[name] = pltpu.SemaphoreType.DMA(shape)

    sizes = (micro, block, width, hidden_width, devices, groups)
    results = pl.pallas_call(
        functools.partial(layer_kernel, sizes, tuple(inputs), tuple(outs), tuple(scratch)),
        out_shape=[jax.ShapeDtypeStruct(*spec) for spec in outs.values()],
        in_specs=in_specs,
        out_specs=[vmem_spec] * len(outs),
        scratch_shapes=list(scratch.values()),
        compiler_params=pltpu.CompilerParams(
            collective_id=0, has_side_effects=True, vmem_limit_bytes=63 * 2**20
        ),
        name="layer",
    )(*inputs.values())
    return dict(zip(outs, handed_on(results)))


def hand_on_kernel(count, *refs):
    sources, targets, passing = (refs[part * count : (part + 1) * count] for part in range(3))
    sems = refs[-1]
    arriving = [
        pltpu.make_async_copy(source, middle, sems.at[0, index])
        for index, (source, middle) in enumerate(zip(sources, passing))
    ]
    leaving = [
        pltpu.make_async_copy(middle, target, sems.at[1, index])
        for index, (middle, target) in enumerate(zip(passing, targets))
    ]
    for copy in arriving:
        copy.start()
    for before, copy in zip(arriving, leaving):
        before.wait()
        copy.start()
    for copy in leaving:
        copy.wait()


def handed_on(arrays):
    any_spec = pl.BlockSpec(memory_space=pl.ANY)
    count = len(arrays)
    return pl.pallas_call(
        functools.partial(hand_on_kernel, count),
        out_shape=[jax.ShapeDtypeStruct(array.shape, array.dtype) for array in arrays],
        in_specs=[any_spec] * count,
        out_specs=[any_spec] * count,
        scratch_shapes=[pltpu.VMEM(array.shape, array.dtype) for array in arrays]
        + [pltpu.SemaphoreType.DMA((2, count))],
        name="hand_on",
    )(*arrays)


def per_device(
    tokens, gain_attn, gain_mlp, w_query, w_key, w_value, w_out, w_gate, w_up, w_down, cotangent, lengths
):
    devices = lax.axis_size("seq")
    groups = min(devices, MOST_GROUPS)
    lower = devices // groups
    micro, block, width = tokens.shape
    weights = dict(
        w_query=w_query, w_key=w_key, w_value=w_value, w_out=w_out, w_gate=w_gate.T, w_up=w_up.T, w_down=w_down
    )
    result = layer(
        tokens.reshape(micro * block, width), gain_attn, gain_mlp, weights,
        cotangent.reshape(micro * block, width), lengths, micro, devices, groups,
    )
    near = [[high * lower + low for low in range(lower)] for high in range(groups)]

    def slice_of(name):
        flat = result["flat_" + name].reshape(-1)
        if lower == 1:
            return flat
        return lax.psum_scatter(flat, "seq", axis_index_groups=near, tiled=True)

    gain_sums = [result["gain_attn_sum"].reshape(-1), result["gain_mlp_sum"].reshape(-1)]
    if lower > 1:
        gain_sums = lax.psum(gain_sums, "seq", axis_index_groups=near)
    return (
        result["output"].reshape(tokens.shape),
        result["input_grad"].reshape(tokens.shape),
        gain_sums[0],
        gain_sums[1],
        slice_of("query"),
        slice_of("keyval"),
        slice_of("value"),
        slice_of("out"),
        slice_of("gate"),
        slice_of("up"),
        slice_of("down"),
    )


def solution(mesh):
    tokens_spec = P(None, "seq", None)
    return jax.shard_map(
        per_device,
        mesh=mesh,
        in_specs=(tokens_spec,) + (P(),) * 9 + (tokens_spec, P()),
        out_specs=(tokens_spec, tokens_spec, P(), P()) + (P("seq"),) * 7,
        check_vma=False,
    )
```

```python
import functools
import math

import jax
import jax.numpy as jnp
from jax import lax
from jax.experimental import pallas as pl
from jax.experimental.pallas import tpu as pltpu
from jax.sharding import PartitionSpec as P

HEAD = 64
WIN = 64
EPSILON = 1e-05
MESH = pl.DeviceIdType.MESH
MOST_GROUPS = 32
CHUNK = 256
BF16 = jnp.bfloat16
F32 = jnp.float32

MATRICES = {
    "down": (("hidden", "cot"),),
    "gate": (("second", "dgate"),),
    "up": (("second", "dup"),),
    "query": (("first", "dquery"),),
    "keyval": (("first", "dkeyval"), ("before", "dkvback")),
    "out": (("attended", "branch"),),
}
ROWS = ("first", "before", "attended", "second", "hidden")
CHUNKED = ("dgate", "dup")
COLS = ("cot", "dgate", "dup", "branch", "dquery", "dkeyval", "dkvback")
PARTS = {
    "gate": ("gate", 0, 1, (2, 1, 4, 3), (1, 2, 4, 4)),
    "gate2": ("gate", 1, 11, (1, 2, 4, 3), (1, 1, 2, 2)),
    "up": ("up", 0, 4, (3, 4, 1, 2), (1, 2, 4, 4)),
    "up2": ("up", 4, 11, (2, 3, 4, 1), (1, 1, 2, 4)),
    "down": ("down", 0, 3, (3, 1, 2, 4), (1, 1, 1, 1)),
    "rest": ("down", 3, 4, (1, 2, 3, 4), (1, 1, 1, 1)),
    "out": ("out", 0, 4, (2, 1, 3, 4), (1, 1, 2, 2)),
    "query": ("query", 0, 4, (2, 3, 4, 1), (1, 1, 2, 4)),
    "key": ("keyval", 0, 4, (1, 2, 4, 3), (1, 2, 4, 4)),
    "keyb": ("keyval", 4, 8, (1, 2, 3, 4), (1, 1, 2, 2)),
}
INDEX = {name: index for index, name in enumerate(PARTS)}
LAG = 2


SCHEDULE = {
    "middle": (
        (1, 0, 0),
        (1, 0, 1),
        (1, 0, 2),
        (1, 0, 3),
        (1, 0, 4),
    ),
    "attend0": (
        (1, 0, 5),
    ),
    "attend1": (
        (1, 0, 6),
    ),
    "attend2": (
        (1, 0, 7),
    ),
    "attend3": (
        (1, 0, 8),
        (0, 0, 0),
        (1, 1, 0),
        (4, 0, 0),
        (2, 0, 0),
        (1, 0, 9),
        (1, 1, 2),
    ),
    "back": (
        (2, 0, 2),
    ),
    "first": (
        (3, 0, 3),
        (3, 0, 4),
        (3, 0, 5),
        (3, 0, 6),
        (1, 2, 2),
        (4, 1, 0),
        (5, 0, 0),
    ),
    "query": (
        (1, 1, 4),
        (1, 1, 6),
        (4, 0, 1),
        (1, 1, 8),
        (0, 1, 0),
        (3, 0, 0),
    ),
    "key": (
        (1, 2, 0),
        (3, 0, 1),
    ),
    "keyb": (
        (3, 0, 2),
    ),
    "gain0": (
        (4, 0, 2),
        (6, 0, 0),
        (6, 0, 1),
        (6, 0, 2),
        (4, 1, 1),
        (1, 3, 0),
        (3, 1, 0),
        (2, 1, 0),
        (6, 0, 3),
        (3, 1, 2),
        (1, 2, 4),
        (7, 0, 0),
        (8, 0, 0),
        (3, 1, 4),
        (1, 2, 6),
        (7, 0, 1),
        (3, 1, 6),
        (1, 3, 2),
        (1, 2, 8),
        (7, 0, 2),
        (8, 0, 2),
        (0, 2, 0),
        (7, 0, 3),
        (1, 3, 4),
        (9, 0, 0),
        (4, 2, 0),
        (1, 3, 6),
        (9, 0, 1),
        (3, 2, 0),
        (7, 1, 0),
        (5, 1, 0),
        (9, 0, 2),
    ),
    "gain1": (
        (4, 2, 1),
        (9, 0, 3),
        (7, 1, 2),
        (3, 2, 4),
        (0, 3, 0),
        (4, 1, 2),
        (8, 1, 0),
        (1, 3, 8),
        (4, 3, 0),
        (5, 2, 0),
        (6, 1, 0),
        (9, 1, 0),
    ),
    "last": (
        (9, 1, 2),
        (2, 2, 0),
        (4, 3, 1),
        (6, 1, 2),
        (4, 2, 2),
        (3, 3, 0),
        (7, 2, 0),
        (3, 3, 4),
        (6, 2, 0),
        (9, 2, 0),
        (8, 2, 0),
        (9, 2, 2),
        (2, 3, 0),
        (6, 2, 2),
        (5, 3, 0),
        (7, 3, 0),
        (4, 3, 2),
        (6, 3, 0),
        (9, 3, 0),
        (8, 3, 0),
        (9, 3, 2),
        (6, 3, 2),
    ),
}


def round_up(value, unit):
    return -(-value // unit) * unit


def length(name):
    return PARTS[name][2] - PARTS[name][1]


def step_span(name, level):
    return PARTS[name][4][level]


def step_layout(bits):
    places, total = {}, 0
    for name in PARTS:
        for level in range(bits):
            places[name, level] = total
            total += -(-length(name) // step_span(name, level))
    return places, total


def stage_copies(bits):
    return 1 + (1 << min(bits, 2)) - 1 + (1 << max(bits - 2, 0)) - 1


def bit_of(number, bit):
    return (number // (1 << bit)) % 2


def flip(number, bit):
    return number + (1 << bit) * (1 - 2 * bit_of(number, bit))


def dot(left, right):
    return jnp.dot(left, right, preferred_element_type=F32)


def dot_rows(left, right):
    return lax.dot_general(left, right, (((1,), (1,)), ((), ())), preferred_element_type=F32)


def dot_cols(left, right):
    return lax.dot_general(left, right, (((0,), (0,)), ((), ())), preferred_element_type=F32)


def at_chunk(index, size=CHUNK):
    return pl.ds(index * size, size)


def loop(first, last, body, **options):
    def step(at, carry):
        body(at)
        return carry

    lax.fori_loop(first, last, step, 0, **options)


def layer_kernel(sizes, in_names, out_names, scratch_names, *refs):
    micro, block, width, hidden_width, devices, groups = sizes
    r = dict(zip(in_names + out_names + scratch_names, refs))
    lower = devices // groups
    bits = groups.bit_length() - 2
    count = 1 << bits
    half = count // 2
    step_places, _ = step_layout(bits)
    orders = {name: [bit for bit in part[3] if bit <= bits] for name, part in PARTS.items()}
    rows_all = micro * block
    chunks = width // CHUNK
    full = hidden_width // CHUNK
    tail = hidden_width % CHUNK
    depth = r["ring_gate"].shape[0]
    kept = full - depth
    scale = 1.0 / math.sqrt(HEAD)

    schedule = SCHEDULE
    if bits != 4:
        schedule = {"last": [
            (INDEX[name], level, first)
            for level in range(bits) for name in PARTS
            for first in range(0, length(name), step_span(name, min(level + 1, bits - 1)))
        ]}

    position = lax.axis_index("seq")
    me, rest = position // lower, position % lower
    core = me % 2
    my_unit = me // 2
    after = ((position + 1) % devices,)
    behind = ((position + devices - 1) % devices,)

    def partner(*some):
        other = me
        for bit in some:
            other = flip(other, bit)
        return (other * lower + rest,)

    stages = [[0], list(range(1, bits + 1))[:2], list(range(1, bits + 1))[2:]]
    stages = [stage for stage in stages if stage]
    peers = [
        [partner(*[bit for place, bit in enumerate(stage) if mask >> place & 1]) for mask in range(1, 1 << len(stage))]
        for stage in stages
    ]


    def local_copy(source, target, index):
        return pltpu.make_async_copy(source, target, r["local_sem"].at[index])

    def remote_copy(source, target, sems, index, device):
        send, recv = r[sems + "_send"], r[sems + "_recv"]
        return pltpu.make_async_remote_copy(
            src_ref=source, dst_ref=target, send_sem=send.at[index], recv_sem=recv.at[index],
            device_id=device, device_id_type=MESH,
        )

    load_tokens = local_copy(r["tokens"], r["x"], 0)
    load_cot = local_copy(r["cotangent"], r["col_cot"].at[0], 1)
    load_out = local_copy(r["w_out"], r["wo"], 2)
    rings = ("ring_gate", "ring_up", "ring_down")
    past = pl.ds(full * CHUNK, tail)
    load_tails = [
        local_copy(r[name].at[past, :], r["tail_" + name[2:]], 3 + index)
        for index, name in enumerate(("w_gate", "w_up", "w_down"))
    ]
    attention_weights = [
        pltpu.make_async_copy(r[name].at[at_chunk(slot), :], r[ring].at[slot], r["ring_sem"].at[index, slot])
        for index, (name, ring) in enumerate(zip(("w_query", "w_key", "w_value"), rings))
        for slot in range(depth)
    ]

    def hidden_weights(chunk, place):
        slot = place % depth
        return [
            pltpu.make_async_copy(r[name].at[at_chunk(chunk), :], r[ring].at[slot], r["ring_sem"].at[index, slot])
            for index, (name, ring) in enumerate(zip(("w_gate", "w_up", "w_down"), rings))
        ]

    def pair_copies():
        plan = {}
        for name in ROWS:
            plan[name] = (r["row_" + name].at[:, 1 - core], r["peer_" + name])
        plan["cot"] = (r["cotangent"], r["col_cot"].at[1])
        for name in ("branch", "dquery", "dkeyval", "dkvback"):
            plan[name] = (r["col_" + name].at[0], r["col_" + name].at[1])
        return {
            name: remote_copy(source, target, "pair", index, partner(0))
            for index, (name, (source, target)) in enumerate(plan.items())
        }

    pair = pair_copies()
    ready = set()

    def need(name):
        if name not in ready and name not in CHUNKED:
            ready.add(name)
            pair[name].wait_recv()

    def pair_chunk(first, last=None):
        ref = r["col_hidden"]
        some = pl.ds(first, 1 if last is None else last - first)
        return pltpu.make_async_remote_copy(
            src_ref=ref.at[0, some], dst_ref=ref.at[1, some],
            send_sem=r["chunk_send"].at[0], recv_sem=r["chunk_recv"].at[first],
            device_id=partner(0), device_id_type=MESH,
        )

    halo_out = remote_copy(r["x"], r["x_before"], "halo", 0, after)
    halo_back = remote_copy(r["back_out"], r["back_in"], "halo", 1, behind)

    load_tokens.start()
    r["x_before"][...] = jnp.zeros_like(r["x_before"])
    barrier = pltpu.get_barrier_semaphore()
    greeted = [after, behind] + [device for stage in peers for device in stage]
    for device in greeted:
        pl.semaphore_signal(barrier, inc=1, device_id=device, device_id_type=MESH)
    for copy in attention_weights:
        copy.start()
    for part in range(2):
        r["col_hidden"][0, full, part] = jnp.zeros((rows_all, CHUNK), BF16)


    def unit_at(order, slot):
        unit = my_unit
        for place, bit in enumerate(order):
            rel = (slot // (1 << (bits - 1 - place))) % 2
            unit = unit + (1 << (bit - 1)) * rel * (1 - 2 * bit_of(me, bit))
        return unit

    def factors(name, base):
        matrix = PARTS[name][0]
        units = [unit_at(orders[name], base + slot) for slot in range(half)]
        pairs = []
        for row, col in MATRICES[matrix]:
            need(row)
            need(col)
            for source in range(2):
                parts = [
                    r["row_" + row][unit, core] if source == 0 else r["peer_" + row][unit] for unit in units
                ]
                pairs.append((jnp.concatenate(parts, axis=0), col, source))
        return pairs

    def product(pairs, chunk):
        total = None
        for left, col, source in pairs:
            if col in CHUNKED:
                right = r["col_hidden"][source, chunk, CHUNKED.index(col)]
            else:
                right = r["col_" + col][source, :, at_chunk(chunk)]
            term = dot(left, right)
            total = term if total is None else total + term
        return total.reshape(half, total.shape[0] // half, CHUNK)

    def step_copy(name, level, first, last):
        size = half >> level
        some = pl.ds(first, last - first)
        if level == 0:
            source = r["send_" + name].at[some]
        else:
            source = r[f"land_{name}{level - 1}"].at[some, pl.ds(size, size)]
        place = step_places[name, level] + first // step_span(name, level)
        return pltpu.make_async_remote_copy(
            src_ref=source, dst_ref=r[f"land_{name}{level}"].at[some],
            send_sem=r["step_send"].at[INDEX[name], level], recv_sem=r["step_recv"].at[place],
            device_id=partner(orders[name][level]), device_id_type=MESH,
        )

    def send_products(name):
        pairs = factors(name, half)
        for at in range(length(name)):
            r["send_" + name][at] = product(pairs, PARTS[name][1] + at).astype(BF16)
            step_copy(name, 0, at, at + 1).start()

    def arrive(name, level, first):
        last = min(first + step_span(name, min(level + 1, bits - 1)), length(name))
        matrix, base = PARTS[name][:2]
        here = r[f"land_{name}{level}"]
        pairs = factors(name, 0) if level == 0 else None
        size = half >> level
        span = step_span(name, level)
        for at in range(first, last, span):
            step_copy(name, level, at, min(at + span, last)).wait_recv()
        for at in range(first, last):
            if level == 0:
                own = product(pairs, base + at)
            else:
                own = r[f"land_{name}{level - 1}"][at, :size].astype(F32)
            total = own + here[at].astype(F32)
            if level < bits - 1:
                here[at] = total.astype(BF16)
            elif matrix in ("gate", "up"):
                rows = total.shape[1]
                for part in range(CHUNK // 128):
                    place = ((base + at) * (CHUNK // 128) + part) * rows
                    r["turn_" + matrix][pl.ds(place, rows), :] = total[0, :, 128 * part : 128 * (part + 1)]
            else:
                r["total_" + name][at] = total[0]
        if level < bits - 1:
            step_copy(name, level + 1, first, last).start()
        else:
            unfinished[matrix] -= last - first
            if not unfinished[matrix]:
                finish(matrix)

    unfinished = {}
    for name, part in PARTS.items():
        unfinished[part[0]] = unfinished.get(part[0], 0) + length(name)

    def finish(matrix):
        if matrix in ("gate", "up"):
            flat, turn = r["flat_" + matrix], r["turn_" + matrix]
            whole = hidden_width // 128
            steps = hidden_width // 64
            rows = turn.shape[0] // (whole + 1)
            few = rows // 2
            even = [turn[pl.ds(rows * j, few, stride=2), :] for j in range(whole + 1)]
            odd = [pltpu.roll(turn[pl.ds(rows * j + 1, few, stride=2), :], 64, 1) for j in range(whole + 1)]
            low = lax.broadcasted_iota(jnp.int32, (few, 128), 1) < 64
            for j in range(whole):
                flat[pl.ds(j, few, stride=steps), :] = even[j]
                flat[pl.ds(whole + 1 + j, few, stride=steps), :] = jnp.where(low, odd[j], odd[j + 1])
            flat[pl.ds(whole, few, stride=steps), :] = jnp.where(low, even[whole], odd[0])
            return
        per_row = width // 128
        for name, part in PARTS.items():
            if part[0] != matrix:
                continue
            for at in range(length(name)):
                total = r["total_" + name][at]
                for piece in range(CHUNK // 128):
                    column = (part[1] + at) * (CHUNK // 128) + piece
                    target = "flat_value" if column >= per_row else "flat_" + matrix
                    rows = r[target].shape[0] // per_row
                    r[target][pl.ds(column % per_row, rows, stride=per_row), :] = total[:rows, 128 * piece : 128 * (piece + 1)]

    def gain_copy(stage, index):
        base = sum(len(group) + 1 for group in peers[:stage])
        return remote_copy(
            r["gain_buf"].at[base], r["gain_buf"].at[base + 1 + index], "gain", base - stage + index, peers[stage][index]
        )

    def gain_start(stage, value):
        r["gain_buf"][sum(len(group) + 1 for group in peers[:stage])] = value
        for index in range(len(peers[stage])):
            gain_copy(stage, index).start()

    def gain_step(stage):
        base = sum(len(group) + 1 for group in peers[:stage])
        total = r["gain_buf"][base]
        for index in range(len(peers[stage])):
            gain_copy(stage, index).wait_recv()
            total = total + r["gain_buf"][base + 1 + index]
        if stage + 1 < len(peers):
            gain_start(stage + 1, total)
            return
        for row, name in enumerate(("gain_attn_sum", "gain_mlp_sum")):
            for j in range(width // 128):
                r[name][j : j + 1, :] = total[row : row + 1, 128 * j : 128 * (j + 1)]

    def arrivals(point):
        for part, level, first in schedule.get(point, ()):
            arrive(tuple(PARTS)[part], level, first)


    def some_rows(at):
        return pl.ds(at * block, block)

    def row_scale(value):
        return lax.rsqrt(jnp.mean(value * value, axis=-1, keepdims=True) + EPSILON)

    def first_norm(source, target):
        def body(at):
            value = source[some_rows(at), :].astype(F32)
            target[some_rows(at), :] = (value * row_scale(value) * r["gain_attn"][...]).astype(BF16)

        loop(0, micro, body)

    def by_owner(name, source):
        ref = r["row_" + name]
        ref[...] = source[...].T.reshape(ref.shape)
        pair[name].start()

    def project(left, ring, target):
        target[...] = dot(left[...], r[ring][...].reshape(width, width)).astype(BF16)

    act, other = r["act"], r["other"]
    load_tokens.wait()
    pl.semaphore_wait(barrier, len(greeted))
    pl.when(position < devices - 1)(halo_out.start)
    first_norm(r["x"], act)
    load_out.start()
    load_cot.start()
    for copy in load_tails:
        copy.start()
    for index, (ring, target) in enumerate(zip(rings, ("queries", "keys", "values"))):
        for copy in attention_weights[index * depth : (index + 1) * depth]:
            copy.wait()
        project(act, ring, r[target])
    by_owner("first", act)
    pl.when(position > 0)(halo_out.wait_recv)
    first_norm(r["x_before"], other)
    project(other, "ring_up", r["keys_before"])
    project(other, "ring_down", r["values_before"])
    for slot in range(depth):
        for copy in hidden_weights(slot, slot):
            copy.start()

    quad = CHUNK // HEAD
    start = position * block
    lane_head = lax.broadcasted_iota(jnp.int32, (block, CHUNK), 1) // HEAD
    key_at = start - WIN + lax.broadcasted_iota(jnp.int32, (2 * block, CHUNK), 0)
    query_at = start + lax.broadcasted_iota(jnp.int32, (1, CHUNK), 1) % block

    def stacked(value):
        return jnp.concatenate([jnp.where(lane_head == h, value, jnp.zeros_like(value)) for h in range(quad)], axis=0)

    def unstacked(value):
        total = jnp.zeros((block, CHUNK), F32)
        for h in range(quad):
            total = jnp.where(lane_head == h, value[h * block : (h + 1) * block], total)
        return total

    def unit(index):
        return index // chunks, some_rows(index // chunks), at_chunk(index % chunks)

    def both(before, own, rows, lanes):
        return jnp.concatenate([r[before][rows, lanes], r[own][rows, lanes]], axis=0)

    def allowed(which):
        def body(at, carry):
            end, low = carry
            end = end + r["lengths"][which, at]
            return end, jnp.where(query_at >= end, end, low)

        _, low = lax.fori_loop(
            0, r["lengths"].shape[1], body, (jnp.int32(0), jnp.zeros((1, CHUNK), jnp.int32))
        )
        low = jnp.maximum(low, query_at - (WIN - 1))
        return (key_at >= low) & (key_at <= query_at)

    def scores(which, keys, queries):
        return jnp.where(allowed(which), dot_rows(keys, queries) * scale, -1e30)

    def attend(index):
        which, rows, lanes = unit(index)
        logits = scores(which, both("keys_before", "keys", rows, lanes), stacked(r["queries"][rows, lanes]))
        peak = jnp.max(logits, axis=0, keepdims=True)
        powers = jnp.exp(logits - peak)
        total = jnp.sum(powers, axis=0, keepdims=True)
        r["log_sums"][index] = jnp.broadcast_to(peak + jnp.log(total), (8, CHUNK))
        probability = (powers / total).astype(BF16)
        mixed = dot_cols(probability, both("values_before", "values", rows, lanes))
        act[rows, lanes] = unstacked(mixed).astype(BF16)

    pair["cot"].start()
    loop(0, micro * chunks, attend, unroll=2)
    load_out.wait()
    middle = r["input_grad"]

    middle[...] = r["x"][...].astype(F32) + dot(act[...], r["wo"][...])

    def second_norm(at):
        value = middle[some_rows(at), :]
        other[some_rows(at), :] = (value * row_scale(value) * r["gain_mlp"][...]).astype(BF16)

    loop(0, micro, second_norm)
    by_owner("second", other)


    def hidden_part(gate, up, grad_hidden):
        sigmoid = jax.nn.sigmoid(gate)
        silu = gate * sigmoid
        hidden = (silu * up).astype(BF16)
        dgate = (grad_hidden * up * sigmoid * (1.0 + gate * (1.0 - sigmoid))).astype(BF16)
        return hidden, dgate, (grad_hidden * silu).astype(BF16)

    columns = r["columns"]

    def hidden_chunk(at, prefetch):
        slot = at % depth
        for copy in hidden_weights(at, at):
            copy.wait()
        wait_chunk(at - LAG)
        hidden, dgate, dup = hidden_part(
            dot_rows(other[...], r["ring_gate"][slot]),
            dot_rows(other[...], r["ring_up"][slot]),
            dot_rows(r["col_cot"][0], r["ring_down"][slot]),
        )
        lanes = at_chunk(at)
        form_chunk(at - LAG)
        r["hidden"][:, lanes] = hidden
        r["col_hidden"][0, at, 0] = dgate
        r["col_hidden"][0, at, 1] = dup
        columns[lanes, :] = hidden.astype(F32).T
        pair_chunk(at).start()
        send_chunk(at - LAG)
        if prefetch:
            for copy in hidden_weights(at + depth, at + depth):
                copy.start()

    early_factors = {}

    def early(at):
        return [
            (name, at - part[1]) for name, part in PARTS.items() if part[0] in ("gate", "up") and part[1] <= at < part[2]
        ]

    def wait_chunk(at):
        if at >= 0:
            pair_chunk(at).wait_recv()

    def form_chunk(at):
        for name, place in early(at):
            if name not in early_factors:
                early_factors[name] = factors(name, half)
            r["send_" + name][place] = product(early_factors[name], at).astype(BF16)

    def send_chunk(at):
        for name, place in early(at):
            step_copy(name, 0, place, place + 1).start()

    load_cot.wait()
    for copy in load_tails:
        copy.wait()
    for at in range(full):
        hidden_chunk(at, at < kept)
    hidden, dgate, dup = hidden_part(
        dot_rows(other[...], r["tail_gate"][...]),
        dot_rows(other[...], r["tail_up"][...]),
        dot_rows(r["col_cot"][0], r["tail_down"][...]),
    )
    r["hidden"][:, past] = hidden
    r["col_hidden"][0, full, 0, :, :tail] = dgate
    r["col_hidden"][0, full, 1, :, :tail] = dup
    pair_chunk(full).start()
    r["square"][...] = jnp.zeros_like(r["square"])
    r["square"][:, :tail] = hidden.astype(F32)
    columns[pl.ds(full * CHUNK, CHUNK), :] = r["square"][...].T
    own_rows = hidden_width // groups
    held_rows = r["row_hidden"].shape[2]
    for owner in range(groups):
        r["row_hidden"][owner // 2, owner % 2] = columns[pl.ds(owner * own_rows, held_rows), :].astype(BF16)
    pair["hidden"].start()
    for at in range(full - LAG, full + 1):
        wait_chunk(at)
        form_chunk(at)
        send_chunk(at)
    for name, part in PARTS.items():
        if part[0] == "down":
            send_products(name)


    sums = [pl.ds(n * CHUNK, CHUNK) for n in range(2 * chunks)]

    def fold(*pieces):
        back = None
        for dgate, dup, gate_ref, up_ref in pieces:
            one = dot(dgate, gate_ref[...]) + dot(dup, up_ref[...])
            back = one if back is None else back + one
        for n in range(chunks):
            columns[sums[n], :] += back[:, n * CHUNK : (n + 1) * CHUNK]

    def fold_chunks(places):
        pieces = []
        for at in places:
            chunk = at - depth if at < full + depth else at - depth - full
            if at >= full + depth:
                for copy in hidden_weights(chunk, at)[:2]:
                    copy.wait()
            pieces.append((
                r["col_hidden"][0, chunk, 0], r["col_hidden"][0, chunk, 1],
                *(r[ring].at[at % depth] for ring in rings[:2]),
            ))
        fold(*pieces)
        for at in places:
            if at < full + kept:
                for copy in hidden_weights(at - full, at + depth)[:2]:
                    copy.start()

    for some in sums[:chunks]:
        columns[some, :] = jnp.zeros((CHUNK, CHUNK), F32)
    fold((
        r["col_hidden"][0, full, 0, :, :tail], r["col_hidden"][0, full, 1, :, :tail], r["tail_gate"], r["tail_up"],
    ))
    for at in range(full, 2 * full, 2):
        fold_chunks(range(at, min(at + 2, 2 * full)))
    for copy in attention_weights:
        copy.start()

    def output_load(chunk):
        return hidden_weights(chunk, chunk)[2]

    def output_chunks(first, last):
        for chunk in range(first, last):
            output_load(chunk).wait()
        total = None
        for chunk in range(first, last):
            term = dot(r["hidden"][:, at_chunk(chunk)], r["ring_down"][chunk % depth])
            total = term if total is None else total + term
        for n in range(chunks):
            columns[sums[chunks + n], :] += total[:, n * CHUNK : (n + 1) * CHUNK]
        for chunk in range(first + depth, min(last + depth, full)):
            output_load(chunk).start()

    def form_output():
        rest = dot(r["hidden"][:, past], r["tail_down"][...])
        for n in range(chunks):
            columns[sums[chunks + n], :] += rest[:, n * CHUNK : (n + 1) * CHUNK]
        for first in range(0, full, 2):
            output_chunks(first, min(first + 2, full))
        for n in range(chunks):
            r["output"][:, at_chunk(n)] = columns[sums[chunks + n], :].astype(BF16)

    def summed(at, base):
        return jnp.concatenate(
            [columns[pl.ds((base + n) * CHUNK + at * block, block), :] for n in range(chunks)],
            axis=1,
        )

    def norm_backward(grad, value, gain):
        inverse = row_scale(value)
        normed = value * inverse
        scaled = grad * gain
        mean = jnp.mean(scaled * normed, axis=-1, keepdims=True)
        return inverse * (scaled - normed * mean), jnp.sum(grad * normed, axis=0, keepdims=True)

    def middle_backward(at, gain_sum):
        rows = some_rows(at)
        value = middle[rows, :]
        for n in range(chunks):
            place = pl.ds((chunks + n) * CHUNK + at * block, block)
            columns[place, :] = value[:, n * CHUNK : (n + 1) * CHUNK]
        grad, part = norm_backward(summed(at, 0), value, r["gain_mlp"][...])
        grad = grad + r["col_cot"][0, rows, :].astype(F32)
        middle[rows, :] = grad
        r["col_branch"][0, rows, :] = grad.astype(BF16)
        return gain_sum + part

    gain_mlp_sum = lax.fori_loop(0, micro, middle_backward, jnp.zeros((1, width), F32))
    pair["branch"].start()
    by_owner("attended", act)
    first_norm(r["x_before"], r["back_out"])
    by_owner("before", r["back_out"])

    r["grad_attended"][...] = dot_rows(r["col_branch"][0], r["wo"][...]).astype(BF16)


    def attend_backward(index):
        which, rows, lanes = unit(index)
        keys = both("keys_before", "keys", rows, lanes)
        values = both("values_before", "values", rows, lanes)
        queries = stacked(r["queries"][rows, lanes])
        grads = stacked(r["grad_attended"][rows, lanes])
        probability = jnp.exp(scores(which, keys, queries) - r["log_sums"][index][:1])
        grad_prob = dot_rows(values, grads)
        delta = jnp.sum(probability * grad_prob, axis=0, keepdims=True)
        grad_scores = (scale * probability * (grad_prob - delta)).astype(BF16)
        r["col_dquery"][0, rows, lanes] = unstacked(dot_cols(grad_scores, keys)).astype(BF16)
        dkey = dot(grad_scores, queries).astype(BF16)
        dvalue = dot(probability.astype(BF16), grads).astype(BF16)
        lanes_value = at_chunk(chunks + index % chunks)
        r["col_dkvback"][0, rows, lanes] = dkey[:block]
        r["col_dkvback"][0, rows, lanes_value] = dvalue[:block]
        r["col_dkeyval"][0, rows, lanes] = dkey[block:]
        r["col_dkeyval"][0, rows, lanes_value] = dvalue[block:]

    arrivals("middle")
    for at in range(micro):
        loop(at * chunks, (at + 1) * chunks, attend_backward, unroll=2)
        arrivals("attend" + str(at))
    for name in ("dquery", "dkeyval", "dkvback"):
        pair[name].start()
    def through_keys(ref, at):
        return dot_rows(ref[0, :, :width], r["ring_up"][at]) + dot_rows(ref[0, :, width:], r["ring_down"][at])

    def back_chunk(at):
        r["back_out"][:, at_chunk(at)] = through_keys(r["col_dkvback"], at).astype(BF16)

    def first_chunk(at):
        columns[at_chunk(at), :] = through_keys(r["col_dkeyval"], at) + dot_rows(
            r["col_dquery"][0], r["ring_gate"][at]
        )

    for copy in attention_weights:
        copy.wait()
    loop(0, chunks, back_chunk)
    pl.when(position > 0)(halo_back.start)
    arrivals("back")
    send_products("out")
    arrivals("out")

    def gain_parts(at, gain_sum):
        rows = some_rows(at)
        for grad, name in ((summed(at, 0), "x"), (r["back_out"][rows, :].astype(F32), "x_before")):
            value = r[name][rows, :].astype(F32)
            gain_sum = gain_sum + jnp.sum(grad * (value * row_scale(value)), axis=0, keepdims=True)
        return gain_sum

    for name in ("query", "key", "keyb"):
        send_products(name)
        arrivals(name)
    loop(0, chunks, first_chunk)
    gain_attn_sum = lax.fori_loop(0, micro, gain_parts, jnp.zeros((1, width), F32))
    gain_start(0, jnp.concatenate([gain_attn_sum, gain_mlp_sum, jnp.zeros((6, width), F32)], axis=0))
    arrivals("first")
    for chunk in range(depth):
        output_load(chunk).start()

    def input_backward(at):
        rows = some_rows(at)
        back = jnp.where(position < devices - 1, r["back_in"][rows, :].astype(F32), 0.0)
        grad, _ = norm_backward(summed(at, 0) + back, r["x"][rows, :].astype(F32), r["gain_attn"][...])
        middle[rows, :] = middle[rows, :] + grad

    for stage in range(len(peers)):
        if stage == 1:
            form_output()
        gain_step(stage)
        arrivals("gain" + str(stage))
    pl.when(position < devices - 1)(halo_back.wait_recv)
    loop(0, micro, input_backward)
    arrivals("last")

    pl.when(position < devices - 1)(halo_out.wait_send)
    pl.when(position > 0)(halo_back.wait_send)
    for copy in pair.values():
        copy.wait_send()
    for stage, group in enumerate(peers):
        for index in range(len(group)):
            gain_copy(stage, index).wait_send()
    pair_chunk(0, full + 1).wait_send()
    for name in PARTS:
        for level in range(bits):
            step_copy(name, level, 0, length(name)).wait_send()


def layer(tokens, gain_attn, gain_mlp, weights, cotangent, lengths, micro, devices, groups):
    rows_all, width = tokens.shape
    hidden_width = weights["w_gate"].shape[0]
    block = rows_all // micro
    bits = groups.bit_length() - 2
    count = 1 << bits
    half = count // 2
    chunks = width // CHUNK
    padded = round_up(hidden_width, CHUNK)
    tail = hidden_width % CHUNK
    depth = chunks
    unit_rows = {name: width // groups for name in ROWS}
    unit_rows["hidden"] = round_up(hidden_width // groups, 16)
    widths = {name: width for name in COLS}
    widths.update(dkeyval=2 * width, dkvback=2 * width)

    inputs = {"tokens": tokens, "cotangent": cotangent, **weights}
    any_spec = pl.BlockSpec(memory_space=pl.ANY)
    vmem_spec = pl.BlockSpec(memory_space=pltpu.VMEM)
    in_specs = [any_spec] * len(inputs) + [vmem_spec] * 2 + [pl.BlockSpec(memory_space=pltpu.SMEM)]
    inputs.update(gain_attn=gain_attn[None], gain_mlp=gain_mlp[None], lengths=lengths)

    outs = {
        "output": ((rows_all, width), BF16),
        "input_grad": ((rows_all, width), F32),
        "gain_attn_sum": ((width // 128, 128), F32),
        "gain_mlp_sum": ((width // 128, 128), F32),
    }
    own = {"query": width * width, "keyval": width * width, "value": width * width, "out": width * width}
    own.update(gate=width * hidden_width, up=width * hidden_width, down=width * hidden_width)
    for name, size in own.items():
        outs["flat_" + name] = ((size // groups // 128, 128), F32)

    scratch = {
        "x": pltpu.VMEM((rows_all, width), BF16),
        "x_before": pltpu.VMEM((rows_all, width), BF16),
        "act": pltpu.VMEM((rows_all, width), BF16),
        "other": pltpu.VMEM((rows_all, width), BF16),
        "queries": pltpu.VMEM((rows_all, width), BF16),
        "keys": pltpu.VMEM((rows_all, width), BF16),
        "values": pltpu.VMEM((rows_all, width), BF16),
        "keys_before": pltpu.VMEM((rows_all, width), BF16),
        "values_before": pltpu.VMEM((rows_all, width), BF16),
        "grad_attended": pltpu.VMEM((rows_all, width), BF16),
        "back_out": pltpu.VMEM((rows_all, width), BF16),
        "back_in": pltpu.VMEM((rows_all, width), BF16),
        "log_sums": pltpu.VMEM((micro * chunks, 8, CHUNK), F32),
        "wo": pltpu.VMEM((width, width), BF16),
        "ring_gate": pltpu.VMEM((depth, CHUNK, width), BF16),
        "ring_up": pltpu.VMEM((depth, CHUNK, width), BF16),
        "ring_down": pltpu.VMEM((depth, CHUNK, width), BF16),
        "tail_gate": pltpu.VMEM((tail, width), BF16),
        "tail_up": pltpu.VMEM((tail, width), BF16),
        "tail_down": pltpu.VMEM((tail, width), BF16),
        "hidden": pltpu.VMEM((rows_all, padded), BF16),
        "columns": pltpu.VMEM((padded, rows_all), F32),
        "square": pltpu.VMEM((rows_all, CHUNK), F32),
        "gain_buf": pltpu.VMEM((stage_copies(bits) + 3, 8, width), F32),
    }
    for name in ROWS:
        scratch["row_" + name] = pltpu.VMEM((count, 2, unit_rows[name], rows_all), BF16)
        scratch["peer_" + name] = pltpu.VMEM((count, unit_rows[name], rows_all), BF16)
    for name in COLS:
        if name not in CHUNKED:
            scratch["col_" + name] = pltpu.VMEM((2, rows_all, widths[name]), BF16)
    scratch["col_hidden"] = pltpu.VMEM((2, padded // CHUNK, len(CHUNKED), rows_all, CHUNK), BF16)
    for name, (matrix, first, last, _, _) in PARTS.items():
        rows = unit_rows[MATRICES[matrix][0][0]]
        scratch["send_" + name] = pltpu.VMEM((last - first, half, rows, CHUNK), BF16)
        for level in range(bits):
            scratch[f"land_{name}{level}"] = pltpu.VMEM((last - first, half >> level, rows, CHUNK), BF16)
        if matrix in ("gate", "up"):
            scratch["turn_" + matrix] = pltpu.VMEM((padded // 128 * rows, 128), F32)
        else:
            scratch["total_" + name] = pltpu.VMEM((last - first, rows, CHUNK), F32)
    sems = {"local_sem": (6,), "ring_sem": (3, depth)}
    sems.update(chunk_send=(1,), chunk_recv=(padded // CHUNK,))
    sems.update(step_send=(len(PARTS), bits), step_recv=(step_layout(bits)[1],))
    for name, number in (("pair", len(ROWS) + len(COLS) - len(CHUNKED)), ("halo", 2), ("gain", stage_copies(bits))):
        sems[name + "_send"] = sems[name + "_recv"] = (number,)
    for name, shape in sems.items():
        scratch[name] = pltpu.SemaphoreType.DMA(shape)

    sizes = (micro, block, width, hidden_width, devices, groups)
    results = pl.pallas_call(
        functools.partial(layer_kernel, sizes, tuple(inputs), tuple(outs), tuple(scratch)),
        out_shape=[jax.ShapeDtypeStruct(*spec) for spec in outs.values()],
        in_specs=in_specs,
        out_specs=[vmem_spec] * len(outs),
        scratch_shapes=list(scratch.values()),
        compiler_params=pltpu.CompilerParams(
            collective_id=0, has_side_effects=True, vmem_limit_bytes=63 * 2**20
        ),
        name="layer",
    )(*inputs.values())
    return dict(zip(outs, handed_on(results)))


PIECES = 4


def hand_on_kernel(count, *refs):
    sources, targets, passing = (refs[part * count : (part + 1) * count] for part in range(3))
    sems = refs[-1]
    steps = []
    for index in range(count):
        rows = sources[index].shape[0]
        pieces = PIECES if index < 2 else 1
        for piece in range(pieces):
            some = pl.ds(piece * (rows // pieces), rows // pieces)
            place = len(steps)
            steps.append((
                pltpu.make_async_copy(sources[index].at[some], passing[index].at[some], sems.at[0, place]),
                pltpu.make_async_copy(passing[index].at[some], targets[index].at[some], sems.at[1, place]),
            ))
    for arriving, _ in steps:
        arriving.start()
    for arriving, leaving in steps:
        arriving.wait()
        leaving.start()
    for _, leaving in steps:
        leaving.wait()


def handed_on(arrays):
    any_spec = pl.BlockSpec(memory_space=pl.ANY)
    count = len(arrays)
    return pl.pallas_call(
        functools.partial(hand_on_kernel, count),
        out_shape=[jax.ShapeDtypeStruct(array.shape, array.dtype) for array in arrays],
        in_specs=[any_spec] * count,
        out_specs=[any_spec] * count,
        scratch_shapes=[pltpu.VMEM(array.shape, array.dtype) for array in arrays]
        + [pltpu.SemaphoreType.DMA((2, count + 2 * (PIECES - 1)))],
        name="hand_on",
    )(*arrays)


def per_device(
    tokens, gain_attn, gain_mlp, w_query, w_key, w_value, w_out, w_gate, w_up, w_down, cotangent, lengths
):
    devices = lax.axis_size("seq")
    groups = min(devices, MOST_GROUPS)
    lower = devices // groups
    micro, block, width = tokens.shape
    weights = dict(
        w_query=w_query, w_key=w_key, w_value=w_value, w_out=w_out, w_gate=w_gate.T, w_up=w_up.T, w_down=w_down
    )
    result = layer(
        tokens.reshape(micro * block, width), gain_attn, gain_mlp, weights,
        cotangent.reshape(micro * block, width), lengths, micro, devices, groups,
    )
    near = [[high * lower + low for low in range(lower)] for high in range(groups)]

    def slice_of(name):
        flat = result["flat_" + name].reshape(-1)
        if lower == 1:
            return flat
        return lax.psum_scatter(flat, "seq", axis_index_groups=near, tiled=True)

    gain_sums = [result["gain_attn_sum"].reshape(-1), result["gain_mlp_sum"].reshape(-1)]
    if lower > 1:
        gain_sums = lax.psum(gain_sums, "seq", axis_index_groups=near)
    return (
        result["output"].reshape(tokens.shape),
        result["input_grad"].reshape(tokens.shape),
        gain_sums[0],
        gain_sums[1],
        slice_of("query"),
        slice_of("keyval"),
        slice_of("value"),
        slice_of("out"),
        slice_of("gate"),
        slice_of("up"),
        slice_of("down"),
    )


def solution(mesh):
    tokens_spec = P(None, "seq", None)
    return jax.shard_map(
        per_device,
        mesh=mesh,
        in_specs=(tokens_spec,) + (P(),) * 9 + (tokens_spec, P()),
        out_specs=(tokens_spec, tokens_spec, P(), P()) + (P("seq"),) * 7,
        check_vma=False,
    )
```
